32 devices in a mesh: tok: 16 (over z, y, x), mem: 2 (over core).
Axes of the slice: x: 2, y: 2, z: 4, core: 2. Of those that a mesh axis runs over, the one named last changes fastest.
Arguments:
- inputs: bfloat16 [16384, 1472], P('tok'), may hold values from -6 to 6
- memory: bfloat16 [16, 1024, 1472], P('tok', 'mem'), may hold values from -6 to 6
- kept_mask: int32 [16, 1024], P('tok', 'mem'), may hold values from 0 to 1, as said below
- segment_ids: int32 [16384], P('tok'), may hold values from 0 to 63, never falling along the last dimension, each value on 1 to 512 neighbouring positions
- bucket_ids: int32 [1024], replicated, may hold values from 0 to 31
- out_grad: bfloat16 [16384, 1472], P('tok'), may hold values from -6 to 6
- self_weights: float32 [4, 384, 1472], P(None, 'mem', 'tok')
- self_first: float32 [4, 384, 1472], P(None, 'mem', 'tok'), may hold values from -0.00015258789 to 0.00015258789
- self_second: float32 [4, 384, 1472], P(None, 'mem', 'tok'), may hold values from 2.5843174e-09 to 1.0317618e-08
- cross_weights: float32 [4, 384, 1472], P(None, ('tok', 'mem'))
- cross_first: float32 [4, 384, 1472], P(None, ('tok', 'mem')), may hold values from -0.00015258789 to 0.00015258789
- cross_second: float32 [4, 384, 1472], P(None, ('tok', 'mem')), may hold values from 2.5843174e-09 to 1.0317618e-08
- ffn_weights: float32 [3, 3584, 1472], P(None, 'mem', 'tok')
- ffn_first: float32 [3, 3584, 1472], P(None, 'mem', 'tok'), may hold values from -3.8146973e-05 to 3.8146973e-05
- ffn_second: float32 [3, 3584, 1472], P(None, 'mem', 'tok'), may hold values from 6.3870964e-11 to 2.60397e-10
- norm_gains: float32 [3, 1472], P(None, 'tok'), may hold values from 0.5 to 1.5
- gains_first: float32 [3, 1472], P(None, 'tok'), may hold values from -0.00015258789 to 0.00015258789
- gains_second: float32 [3, 1472], P(None, 'tok'), may hold values from 1.4739454e-09 to 5.8957816e-09
- rel_bias: float32 [6, 32], P('mem'), may hold values from -3 to 3
- rel_first: float32 [6, 32], P('mem'), may hold values from -0.00015258789 to 0.00015258789
- rel_second: float32 [6, 32], P('mem'), may hold values from 1.4739454e-09 to 5.8957816e-09
Outputs:
- layer_out: bfloat16 [16384, 1472], P('tok')
- input_grad: float32 [16384, 1472], P('tok')
- memory_grad: float32 [16, 1024, 1472], P('tok', 'mem')
- grad_norm: float32 [], replicated
- self_new: float32 [4, 384, 1472], P(None, 'mem', 'tok')
- self_first_new: float32 [4, 384, 1472], P(None, 'mem', 'tok')
- self_second_new: float32 [4, 384, 1472], P(None, 'mem', 'tok')
- cross_new: float32 [4, 384, 1472], P(None, ('tok', 'mem'))
- cross_first_new: float32 [4, 384, 1472], P(None, ('tok', 'mem'))
- cross_second_new: float32 [4, 384, 1472], P(None, ('tok', 'mem'))
- ffn_new: float32 [3, 3584, 1472], P(None, 'mem', 'tok')
- ffn_first_new: float32 [3, 3584, 1472], P(None, 'mem', 'tok')
- ffn_second_new: float32 [3, 3584, 1472], P(None, 'mem', 'tok')
- gains_new: float32 [3, 1472], P(None, 'tok')
- gains_first_new: float32 [3, 1472], P(None, 'tok')
- gains_second_new: float32 [3, 1472], P(None, 'tok')
- rel_new: float32 [6, 32], P('mem')
- rel_first_new: float32 [6, 32], P('mem')
- rel_second_new: float32 [6, 32], P('mem')
The draws below stay inside these ranges and needn't reach their ends.
Inputs may be any that keep to these rules, and one draw needn't show every extreme that they name: `kept_mask`: 1 where the deletion gate kept the row's encoder position; position 0 of every row is kept. `segment_ids`: segment numbers never fall along the tokens; a segment holds half of 1024 tokens or fewer. `bucket_ids`: entry d is the bucket of a key d positions before its query.
All inputs are finite; a program needn't handle non-finite values.
Results may differ from the reference program's by a relative error of at most 0.03.
The reference program's roundings to bfloat16 on the way count: a program that leaves them out, or rounds other values in their place, can miss the bound.
Values may be sent and summed in bfloat16 or wider, within the bound.
No kernel may reach another device: no remote copies, remote signals or barrier semaphores. Data moves between devices by JAX's collectives and lax.ppermute only.
A program may use at most 384 MiB of HBM per device.

```python
import math
import jax
import jax.numpy as jnp
import numpy as np
from jax import lax

D = 1472
H = 6
DK = 64
FF = 3584
NB = 32
LEN = 1024
ENC = 1024
STEP = 10
INNER = 384
ROWS = 16
TOKENS = 16384
PARAMS = 20353536


def stacked_draw(key, salt, factors, height, width):
    own_key = jax.random.fold_in(key, salt)
    unit_draw = jnp.clip(jax.random.normal(own_key, (len(factors), height, width), jnp.float32), -6.0, 6.0)
    return unit_draw * jnp.asarray(factors, jnp.float32)[:, None, None]


def draw_self_weights(key, part):
    return stacked_draw(key, 11, [0.25 * D ** (-0.5), D ** (-0.5), D ** (-0.5), 3.0 * INNER ** (-0.5)], INNER, D)


def draw_cross_weights(key, part):
    return stacked_draw(key, 23, [0.25 * D ** (-0.5), D ** (-0.5), D ** (-0.5), 3.0 * INNER ** (-0.5)], INNER, D)


def draw_ffn_weights(key, part):
    return stacked_draw(key, 37, [D ** (-0.5), D ** (-0.5), 1.5 * FF ** (-0.5)], FF, D)


def draw_kept_mask(key, part):
    first_key, second_key = jax.random.split(key)
    limits = jax.random.randint(first_key, (ROWS, 2, 1), 20, 90)
    rolls = jax.random.randint(second_key, (ROWS, 2, ENC // 2), 0, 100)
    kept_vals = (rolls < limits).astype(jnp.int32).reshape(ROWS, ENC)
    return kept_vals.at[:, 0].set(1)


def place_ends(values, key, low, top_value):
    extent = values.shape
    spot = [jax.random.randint(jax.random.fold_in(key, axis), (), 0, extent[axis]) for axis in range(len(extent))]
    values = values.at[tuple(spot)].set(low)
    longest = extent.index(max(extent))
    spot[longest] = (spot[longest] + 1) % extent[longest]
    return values.at[tuple(spot)].set(top_value)


def block_levels(rng, extent, cuts, least, high):
    gain, own = 1.0, jax.random.fold_in(rng, 6)
    for dim, parts in cuts:
        steps = jnp.exp(jax.random.uniform(jax.random.fold_in(own, dim), (parts,), jnp.float32, least / len(cuts), high / len(cuts)))
        gain = gain * jnp.repeat(steps, extent[dim] // parts).reshape([-1 if axis == dim else 1 for axis in range(len(extent))])
    return gain


def length_profile(count, total, limit, lean):
    loads = [(1 << 20) // math.isqrt(grade ** lean) + 1 for grade in range(2, count + 1)]
    rest, given = total - limit - (count - 1), [1] * (count - 1)
    while rest > 0:
        free = [i for i in range(count - 1) if given[i] < limit]
        whole, remaining = sum([loads[i] for i in free]), rest
        for i in free:
            addition = min(limit - given[i], max(1, remaining * loads[i] // whole), rest)
            given[i] = given[i] + addition
            rest = rest - addition
    return np.array([limit] + given)


def uneven_parts(key, count, total, reach, slope):
    if count == 2:
        one = jax.random.randint(key, (), max(1, total - reach), min(reach, total - 1) + 1)
        return jnp.stack([one, total - one])
    tallies = jnp.asarray(length_profile(count, total, reach, slope), jnp.int32)
    twos = (count - 1) // 2
    giver, sink = tallies[1:1 + 2 * twos:2], tallies[2:2 + 2 * twos:2]
    slack = jnp.minimum(giver - 1, reach - sink)
    moved = jax.random.randint(jax.random.fold_in(key, 1), (twos,), 0, 1 << 20) % (slack + 1)
    tallies = tallies.at[1:1 + 2 * twos:2].set(giver - moved).at[2:2 + 2 * twos:2].set(sink + moved)
    return tallies[jax.random.permutation(jax.random.fold_in(key, 2), count)]


def scatter_about(stream_key, dims, deviation, reach, shards=(), kind=jnp.bfloat16):
    values = jax.random.normal(stream_key, dims, jnp.float32) * deviation
    if len(shards) > 0:
        values = block_levels(stream_key, dims, shards, -0.22, 0.18) * values
    return jnp.clip(values, min=-reach, max=reach).astype(kind)


def setup_inputs(seed: int = 0) -> dict:
    seeds = jax.random.split(jax.random.key(seed), 22)
    return {
        "inputs": scatter_about(seeds[0], (TOKENS, D), 1.0, 6.0, ((0, 16),)),
        "memory": scatter_about(seeds[1], (ROWS, ENC, D), 1.0, 6.0, ((0, 16), (1, 2))),
        "kept_mask": draw_kept_mask(jax.random.fold_in(seeds[21], 71), 0),
        "segment_ids": jnp.searchsorted(jnp.cumsum(uneven_parts(seeds[3], ROWS * 4, TOKENS, LEN // 2, 1)), jnp.arange(TOKENS), side="right").astype(jnp.int32),
        "bucket_ids": place_ends(jax.random.randint(seeds[4], (LEN,), 0, NB), jax.random.fold_in(seeds[4], 1), 0, NB - 1).astype(jnp.int32),
        "out_grad": scatter_about(seeds[5], (TOKENS, D), 1.0, 6.0, ((0, 16),)),
        "self_weights": draw_self_weights(jax.random.fold_in(seeds[21], 71), 0),
        "self_first": scatter_about(seeds[7], (4, INNER, D), (0.111 / PARAMS ** 0.5), 0.00015258789, ((1, 2), (2, 16)), jnp.float32),
        "self_second": jnp.clip(jnp.exp(math.log(1.0317617871180573e-08) - 1.3843914854378192 * jax.random.uniform(seeds[8], (4, INNER, D), jnp.float32) ** block_levels(seeds[8], (4, INNER, D), ((1, 2), (2, 16)), -0.2, 0.2)), 2.5843174267237146e-09, 1.0317617871180573e-08),
        "cross_weights": draw_cross_weights(jax.random.fold_in(seeds[21], 71), 0),
        "cross_first": scatter_about(seeds[10], (4, INNER, D), (0.111 / PARAMS ** 0.5), 0.00015258789, ((1, 32),), jnp.float32),
        "cross_second": jnp.clip(jnp.exp(math.log(1.0317617871180573e-08) - 1.3843914854378192 * jax.random.uniform(seeds[11], (4, INNER, D), jnp.float32) ** block_levels(seeds[11], (4, INNER, D), ((1, 32),), -0.2, 0.2)), 2.5843174267237146e-09, 1.0317617871180573e-08),
        "ffn_weights": draw_ffn_weights(jax.random.fold_in(seeds[21], 71), 0),
        "ffn_first": scatter_about(seeds[13], (3, FF, D), (0.03 / PARAMS ** 0.5), 3.814697265625e-05, ((1, 2), (2, 16)), jnp.float32),
        "ffn_second": jnp.clip(jnp.exp(math.log(2.603970095105268e-10) - 1.4053426 * jax.random.uniform(seeds[14], (3, FF, D), jnp.float32) ** block_levels(seeds[14], (3, FF, D), ((1, 2), (2, 16)), -0.2, 0.2)), 6.387096407323156e-11, 2.603970095105268e-10),
        "norm_gains": jnp.clip(1.0 + 0.1 * jax.random.normal(seeds[15], (3, D), jnp.float32), 0.5, 1.5),
        "gains_first": scatter_about(seeds[16], (3, D), (0.111 / PARAMS ** 0.5), 0.00015258789, ((1, 16),), jnp.float32),
        "gains_second": jnp.clip(jnp.exp(math.log(5.895781640674613e-09) - 1.3862944 * jax.random.uniform(seeds[17], (3, D), jnp.float32) ** block_levels(seeds[17], (3, D), ((1, 16),), -0.2, 0.2)), 1.4739454101686533e-09, 5.895781640674613e-09),
        "rel_bias": scatter_about(seeds[18], (H, NB), 0.5, 3.0, ((0, 2),), jnp.float32),
        "rel_first": scatter_about(seeds[19], (H, NB), (0.111 / PARAMS ** 0.5), 0.00015258789, ((0, 2),), jnp.float32),
        "rel_second": jnp.clip(jnp.exp(math.log(5.895781640674613e-09) - 1.3862944 * jax.random.uniform(seeds[20], (H, NB), jnp.float32) ** block_levels(seeds[20], (H, NB), ((0, 2),), -0.2, 0.2)), 1.4739454101686533e-09, 5.895781640674613e-09),
    }


EPS_NORM = 1e-06
NEG_FILL = -1e+30
BETA_FIRST = 0.9
BETA_SECOND = 0.95
ADAM_EPS = 1e-08
RATE_MATRIX = 0.05
RATE_SMALL = 1.0
DECAY_MATRIX = 0.1
CLIP_NORM = 1.0

@jax.custom_vjp
def low(v):
    return lax.optimization_barrier(v.astype(jnp.bfloat16)).astype(jnp.float32)

@jax.custom_vjp
def low_back(v):
    return v

def low_keep(v):
    return (low(v), None)

def low_pass(kept, grad):
    return (grad,)

def back_keep(v):
    return (v, None)

def back_low(kept, grad):
    return (low(grad),)
low.defvjp(low_keep, low_pass)
low_back.defvjp(back_keep, back_low)

def norm_low(values, gain_vec):
    inv_root = lax.rsqrt(lax.optimization_barrier(jnp.mean(values * values, axis=-1, keepdims=True)) + EPS_NORM)
    return low(values * inv_root * gain_vec)

def adam_step(weight, first_mom, second_mom, gradient, clip_scale, step_rate, decay_rate):
    clipped = gradient * clip_scale
    first_new = BETA_FIRST * first_mom + (1.0 - BETA_FIRST) * clipped
    second_new = BETA_SECOND * second_mom + (1.0 - BETA_SECOND) * clipped * clipped
    first_hat = first_new / (1.0 - BETA_FIRST ** STEP)
    second_hat = second_new / (1.0 - BETA_SECOND ** STEP)
    weight_new = weight - step_rate * (first_hat / (jnp.sqrt(second_hat) + ADAM_EPS) + decay_rate * weight)
    return (weight_new, first_new, second_new)

def reference(inputs, memory, kept_mask, segment_ids, bucket_ids, out_grad, self_weights, self_first, self_second, cross_weights, cross_first, cross_second, ffn_weights, ffn_first, ffn_second, norm_gains, gains_first, gains_second, rel_bias, rel_first, rel_second):
    highest = lax.Precision.HIGHEST
    positions = jnp.arange(LEN, dtype=jnp.int32)
    distance = jnp.clip(positions[:, None] - positions[None, :], 0, LEN - 1).astype(jnp.int32)
    causal = positions[:, None] >= positions[None, :]
    seg_rows = segment_ids.reshape(ROWS, LEN)
    kept_rows = kept_mask > 0

    def forward(resid_zero, memory_vals, self_w, cross_w, ffn_w, gain_w, rel_w):
        self_low = low(self_w)
        cross_low = low(cross_w)
        ffn_low = low(ffn_w)
        gain_low = low(gain_w)
        normed_one = norm_low(resid_zero, gain_low[0])
        qkv_self = low(low_back(jnp.einsum('rld,cid->crli', normed_one, self_low[:3], precision=highest)))
        bias_grid = rel_w[:, bucket_ids[distance]]

        def self_row(pieces):
            query_r, key_r, value_r, seg_r = pieces
            query_h = query_r.reshape(LEN, H, DK)
            key_h = key_r.reshape(LEN, H, DK)
            value_h = value_r.reshape(LEN, H, DK)
            raw_scores = low_back(jnp.einsum('qhd,khd->hqk', query_h, key_h, precision=highest) + bias_grid)
            allowed = causal & (seg_r[:, None] == seg_r[None, :])
            self_probs = jax.nn.softmax(jnp.where(allowed[None], raw_scores, NEG_FILL), axis=-1)
            mixed = jnp.einsum('hqk,khd->qhd', low(self_probs), value_h, precision=highest).reshape(LEN, INNER)
            return low(low_back(mixed))
        self_attn = lax.map(jax.checkpoint(self_row), (qkv_self[0], qkv_self[1], qkv_self[2], seg_rows))
        resid_one = resid_zero + low_back(jnp.einsum('rli,id->rld', self_attn, self_low[3], precision=highest))
        normed_two = norm_low(resid_one, gain_low[1])
        query_c = low(low_back(jnp.einsum('rld,id->rli', normed_two, cross_low[0], precision=highest)))
        kv_cross = low(low_back(jnp.einsum('rkd,cid->crki', memory_vals, cross_low[1:3], precision=highest)))

        def cross_row(pieces):
            query_r, key_r, value_r, kept_r = pieces
            query_h = query_r.reshape(LEN, H, DK)
            key_h = key_r.reshape(ENC, H, DK)
            value_h = value_r.reshape(ENC, H, DK)
            raw_scores = low_back(jnp.einsum('qhd,khd->hqk', query_h, key_h, precision=highest))
            cross_probs = jax.nn.softmax(jnp.where(kept_r[None, None, :], raw_scores, NEG_FILL), axis=-1)
            mixed = jnp.einsum('hqk,khd->qhd', low(cross_probs), value_h, precision=highest).reshape(LEN, INNER)
            return low(low_back(mixed))
        cross_attn = lax.map(jax.checkpoint(cross_row), (query_c, kv_cross[0], kv_cross[1], kept_rows))
        resid_two = resid_one + low_back(jnp.einsum('rli,id->rld', cross_attn, cross_low[3], precision=highest))
        normed_three = norm_low(resid_two, gain_low[2])
        gate_up = low_back(jnp.einsum('rld,cfd->crlf', normed_three, ffn_low[:2], precision=highest))
        hidden = low(jax.nn.gelu(gate_up[0], approximate=True) * gate_up[1])
        return resid_two + low_back(jnp.einsum('rlf,fd->rld', hidden, ffn_low[2], precision=highest))
    resid_zero = inputs.astype(jnp.float32).reshape(ROWS, LEN, D)
    out_full, pull_back = jax.vjp(forward, resid_zero, memory.astype(jnp.float32), self_weights, cross_weights, ffn_weights, norm_gains, rel_bias)
    grad_in, grad_mem, grad_self, grad_cross, grad_ffn, grad_gains, grad_rel = pull_back(out_grad.astype(jnp.float32).reshape(ROWS, LEN, D))
    total_squares = jnp.sum(grad_self * grad_self) + jnp.sum(grad_cross * grad_cross) + jnp.sum(grad_ffn * grad_ffn) + jnp.sum(grad_gains * grad_gains) + jnp.sum(grad_rel * grad_rel)
    grad_norm = jnp.sqrt(total_squares)
    clip_scale = CLIP_NORM / jnp.maximum(grad_norm, CLIP_NORM)
    self_new = adam_step(self_weights, self_first, self_second, grad_self, clip_scale, RATE_MATRIX, DECAY_MATRIX)
    cross_new = adam_step(cross_weights, cross_first, cross_second, grad_cross, clip_scale, RATE_MATRIX, DECAY_MATRIX)
    ffn_new = adam_step(ffn_weights, ffn_first, ffn_second, grad_ffn, clip_scale, RATE_MATRIX, DECAY_MATRIX)
    gains_new = adam_step(norm_gains, gains_first, gains_second, grad_gains, clip_scale, RATE_SMALL, 0.0)
    rel_new = adam_step(rel_bias, rel_first, rel_second, grad_rel, clip_scale, RATE_SMALL, 0.0)
    layer_out = out_full.reshape(TOKENS, D).astype(jnp.bfloat16)
    return (layer_out, grad_in.reshape(TOKENS, D), grad_mem, grad_norm, self_new[0], self_new[1], self_new[2], cross_new[0], cross_new[1], cross_new[2], ffn_new[0], ffn_new[1], ffn_new[2], gains_new[0], gains_new[1], gains_new[2], rel_new[0], rel_new[1], rel_new[2])
```

```python
import functools

import jax
import jax.numpy as jnp
from jax import lax
from jax.experimental import pallas as pl
from jax.experimental.pallas import tpu as pltpu
from jax.sharding import PartitionSpec as P

H = 6
DK = 64
NB = 32
LEN = 1024
STEP = 10
INNER = 384
D = 1472

EPS_NORM = 1e-06
NEG_FILL = -1e30
BETA_FIRST = 0.9
BETA_SECOND = 0.95
ADAM_EPS = 1e-08
RATE_MATRIX = 0.05
RATE_SMALL = 1.0
DECAY_MATRIX = 0.1
CLIP_NORM = 1.0

QB = 256
FC = 256
VMEM = 60 * 1024 * 1024
BF = jnp.bfloat16
F32 = jnp.float32


def dot_nn(a, b):
    return lax.dot_general(a, b, (((1,), (0,)), ((), ())), preferred_element_type=F32)


def dot_tn(a, b):
    return lax.dot_general(a, b, (((0,), (0,)), ((), ())), preferred_element_type=F32)


def dot_nt(a, b):
    return lax.dot_general(a, b, (((1,), (1,)), ((), ())), preferred_element_type=F32)


def bias_tile(vec, delta):
    row = vec[:, delta * QB : delta * QB + 2 * QB]
    wide = pltpu.roll(jnp.broadcast_to(row, (QB, 2 * QB)), 0, 1, stride=1, stride_axis=0)
    return wide[:, QB:]


def band(block):
    return max(0, block - LEN // 2 // QB)


def self_scores(q_ref, k_ref, segr_ref, segc_ref, tiles, block):
    low, high = band(block) * QB, (block + 1) * QB
    cols = slice(block * QB, high)
    scores = dot_tn(k_ref[:, low:high], q_ref[:, cols])
    scores = scores + jnp.concatenate([tiles[block - b] for b in range(band(block), block + 1)], axis=0)
    keys = lax.broadcasted_iota(jnp.int32, scores.shape, 0) + low
    queries = lax.broadcasted_iota(jnp.int32, scores.shape, 1) + block * QB
    allowed = (segc_ref[low:high, :] == segr_ref[:, cols]) & (keys <= queries)
    return jnp.where(allowed, scores, NEG_FILL)


def softmax_store(scores, v_block, o_ref, lse_ref, cols):
    top = jnp.max(scores, axis=0, keepdims=True)
    exps = jnp.exp(scores - top)
    total = jnp.sum(exps, axis=0, keepdims=True)
    probs = (exps * (1.0 / total)).astype(BF)
    o_ref[:, cols] = dot_nn(v_block, probs).astype(BF)
    lse_ref[0, :, cols] = top + jnp.log(total)


def self_fwd_kernel(q_ref, k_ref, v_ref, segr_ref, segc_ref, vec_ref, o_ref, lse_ref):
    tiles = [bias_tile(vec_ref[0], d) for d in range(LEN // 2 // QB + 1)]
    for block in range(LEN // QB):
        scores = self_scores(q_ref, k_ref, segr_ref, segc_ref, tiles, block)
        low, high = band(block) * QB, (block + 1) * QB
        softmax_store(scores, v_ref[:, low:high], o_ref, lse_ref, slice(block * QB, high))


def cross_fwd_kernel(q_ref, k_ref, v_ref, keep_ref, o_ref, lse_ref):
    for block in range(LEN // QB):
        cols = slice(block * QB, (block + 1) * QB)
        scores = dot_tn(k_ref[...], q_ref[:, cols]) + keep_ref[...]
        softmax_store(scores, v_ref[...], o_ref, lse_ref, cols)


def score_grads(scores, lse, k_block, v_block, q_block, do_block):
    probs = jnp.exp(scores - lse)
    grad_probs = dot_tn(v_block, do_block)
    delta = jnp.sum(probs * grad_probs, axis=0, keepdims=True)
    grads = (probs * (grad_probs - delta)).astype(BF)
    grad_q = dot_nn(k_block, grads)
    grad_k = dot_nt(q_block, grads)
    grad_v = dot_nt(do_block, probs.astype(BF))
    return grads, grad_q, grad_k, grad_v


def self_bwd_kernel(
    q_ref, k_ref, v_ref, do_ref, lse_ref, segr_ref, segc_ref, vec_ref,
    grad_ref, diag_ref, dk_acc, dv_acc, tile_acc,
):
    count = LEN // 2 // QB + 1
    tiles = [bias_tile(vec_ref[0], d) for d in range(count)]
    dk_acc[...] = jnp.zeros_like(dk_acc)
    dv_acc[...] = jnp.zeros_like(dv_acc)
    tile_acc[...] = jnp.zeros_like(tile_acc)
    for block in range(LEN // QB):
        low, high = band(block) * QB, (block + 1) * QB
        cols = slice(block * QB, high)
        scores = self_scores(q_ref, k_ref, segr_ref, segc_ref, tiles, block)
        grads, grad_q, grad_k, grad_v = score_grads(
            scores, lse_ref[0, :, cols], k_ref[:, low:high], v_ref[:, low:high], q_ref[:, cols], do_ref[:, cols]
        )
        grad_ref[0, :, cols] = grad_q.astype(BF)
        dk_acc[:, low:high] += grad_k
        dv_acc[:, low:high] += grad_v
        for b in range(band(block), block + 1):
            start = b * QB - low
            tile_acc[block - b] += grads[start : start + QB].astype(F32)
    grad_ref[1] = dk_acc[...].astype(BF)
    grad_ref[2] = dv_acc[...].astype(BF)
    spots = lax.broadcasted_iota(jnp.int32, (QB, QB), 0) + lax.broadcasted_iota(jnp.int32, (QB, QB), 1)
    mirror = (spots == QB - 1).astype(F32)
    for d in range(count):
        mirrored = lax.dot_general(
            tile_acc[d], mirror, (((1,), (0,)), ((), ())),
            precision=lax.Precision.HIGHEST, preferred_element_type=F32,
        )
        padded = jnp.concatenate([mirrored, jnp.zeros((QB, QB), F32)], axis=1)
        skewed = pltpu.roll(padded, 0, 1, stride=1, stride_axis=0)
        diag_ref[0, d : d + 1, :] = jnp.sum(skewed, axis=0, keepdims=True)


def cross_bwd_kernel(q_ref, k_ref, v_ref, do_ref, lse_ref, keep_ref, grad_ref, dk_acc, dv_acc):
    dk_acc[...] = jnp.zeros_like(dk_acc)
    dv_acc[...] = jnp.zeros_like(dv_acc)
    for block in range(LEN // QB):
        cols = slice(block * QB, (block + 1) * QB)
        scores = dot_tn(k_ref[...], q_ref[:, cols]) + keep_ref[...]
        grads, grad_q, grad_k, grad_v = score_grads(
            scores, lse_ref[0, :, cols], k_ref[...], v_ref[...], q_ref[:, cols], do_ref[:, cols]
        )
        grad_ref[0, :, cols] = grad_q.astype(BF)
        dk_acc[...] += grad_k
        dv_acc[...] += grad_v
    grad_ref[1] = dk_acc[...].astype(BF)
    grad_ref[2] = dv_acc[...].astype(BF)


def head_spec(first):
    return pl.BlockSpec((DK, LEN), lambda h: (first + h, 0))


def whole_spec(shape):
    return pl.BlockSpec(shape, lambda h: (0,) * len(shape))


def attn_call(kernel, heads, in_specs, out_specs, out_shape, operands, scratch, flops):
    return pl.pallas_call(
        kernel,
        grid=(heads,),
        in_specs=in_specs,
        out_specs=out_specs,
        out_shape=out_shape,
        scratch_shapes=scratch,
        compiler_params=pltpu.CompilerParams(vmem_limit_bytes=VMEM),
        cost_estimate=pl.CostEstimate(flops=flops, bytes_accessed=4 << 20, transcendentals=heads << 20),
    )(*operands)


def shape_of(*dims, dtype=BF):
    return jax.ShapeDtypeStruct(dims, dtype)


GRAD_SPEC = pl.BlockSpec((3, DK, LEN), lambda h: (0, h, 0))
LSE_SPEC = pl.BlockSpec((1, 1, LEN), lambda h: (h, 0, 0))


def self_forward(qkv, seg_row, seg_col, vec, heads):
    vec_spec = pl.BlockSpec((1, 1, vec.shape[2]), lambda h: (h, 0, 0))
    return attn_call(
        self_fwd_kernel, heads,
        [head_spec(0), head_spec(heads), head_spec(2 * heads), whole_spec((1, LEN)), whole_spec((LEN, 1)), vec_spec],
        [head_spec(0), LSE_SPEC],
        [shape_of(heads * DK, LEN), shape_of(heads, 1, LEN, dtype=F32)],
        (qkv, qkv, qkv, seg_row, seg_col, vec), [], heads * 2 * 2 * DK * LEN * LEN,
    )


def cross_forward(query, keyval, keep, heads):
    return attn_call(
        cross_fwd_kernel, heads,
        [head_spec(0), head_spec(0), head_spec(heads), whole_spec((LEN, 1))],
        [head_spec(0), LSE_SPEC],
        [shape_of(heads * DK, LEN), shape_of(heads, 1, LEN, dtype=F32)],
        (query, keyval, keyval, keep), [], heads * 2 * 2 * DK * LEN * LEN,
    )


def self_backward(qkv, grad_attn, lse, seg_row, seg_col, vec, heads):
    count = LEN // 2 // QB + 1
    vec_spec = pl.BlockSpec((1, 1, vec.shape[2]), lambda h: (h, 0, 0))
    out = shape_of(3, heads * DK, LEN)
    return attn_call(
        self_bwd_kernel, heads,
        [
            head_spec(0), head_spec(heads), head_spec(2 * heads), head_spec(0), LSE_SPEC,
            whole_spec((1, LEN)), whole_spec((LEN, 1)), vec_spec,
        ],
        [GRAD_SPEC, pl.BlockSpec((1, count, 2 * QB), lambda h: (h, 0, 0))],
        [out, shape_of(heads, count, 2 * QB, dtype=F32)],
        (qkv, qkv, qkv, grad_attn, lse, seg_row, seg_col, vec),
        [pltpu.VMEM((DK, LEN), F32), pltpu.VMEM((DK, LEN), F32), pltpu.VMEM((count, QB, QB), F32)],
        heads * 2 * 5 * DK * LEN * LEN,
    )


def cross_backward(query, keyval, grad_attn, lse, keep, heads):
    out = shape_of(3, heads * DK, LEN)
    return attn_call(
        cross_bwd_kernel, heads,
        [head_spec(0), head_spec(0), head_spec(heads), head_spec(0), LSE_SPEC, whole_spec((LEN, 1))],
        [GRAD_SPEC],
        [out],
        (query, keyval, keyval, grad_attn, lse, keep),
        [pltpu.VMEM((DK, LEN), F32), pltpu.VMEM((DK, LEN), F32)],
        heads * 2 * 5 * DK * LEN * LEN,
    )


def owner_copies(refs, owners_ref, target, sems, inward):
    copies = []
    slot = 0
    for ref in refs:
        for j in range(ref.shape[0]):
            owner = owners_ref[slot]
            here = target.at[:, owner]
            pair = (ref.at[j], here) if inward else (here, ref.at[j])
            copies.append(pltpu.make_async_copy(*pair, sems.at[slot]))
            slot += 1
    return copies


def ffn_kernel(by_owner, first, last, *refs):
    owners_ref, x_hbm, og_hbm, weight_hbm = refs[:4]
    refs = refs[4:]
    acc_refs, refs = ((), refs) if first else (refs[:2], refs[2:])
    out_refs, refs = refs[:2], refs[2:]
    grad_refs, refs = refs[:by_owner], refs[by_owner:]
    x_ref, og_ref, out_acc, back_acc, weights, grads, x_sems, in_sems, out_sems, acc_sems = refs[:10]
    unused, count, block, width = weights.shape
    rows = count * block
    inputs = [
        pltpu.make_async_copy(src, dst, x_sems.at[i])
        for i, (src, dst) in enumerate(((x_hbm, x_ref), (og_hbm, og_ref)))
    ]
    loads = [pltpu.make_async_copy(weight_hbm.at[:, c], weights.at[c], in_sems.at[c]) for c in range(3)]
    accs = [
        pltpu.make_async_copy(src, dst, acc_sems.at[i])
        for i, (src, dst) in enumerate(zip(acc_refs, (out_acc, back_acc)))
    ]
    for copy in (inputs[0], *loads, inputs[1], *accs):
        copy.start()
    inputs[0].wait()
    loads[0].wait()
    normed = x_ref[...]
    slope = 0.7978845608028654
    stores = []
    for step in range(width // FC):
        cols = slice(step * FC, (step + 1) * FC)
        w_gate = weights[0, :, :, cols].reshape(rows, FC)
        gate = dot_tn(w_gate, normed)
        square = gate * gate
        tanh = jnp.tanh(slope * gate * (1.0 + 0.044715 * square))
        half = 0.5 * (1.0 + tanh)
        act = gate * half
        act_grad = half + 0.5 * gate * (1.0 - tanh * tanh) * (slope * (1.0 + 0.134145 * square))
        if step == 0:
            loads[1].wait()
        w_up = weights[1, :, :, cols].reshape(rows, FC)
        upward = dot_tn(w_up, normed)
        hidden = (act * upward).astype(BF)
        if step == 0:
            loads[2].wait()
            inputs[1].wait()
        w_down = weights[2, :, :, cols].reshape(rows, FC)
        out_grad = og_ref[...]
        grad_hidden = dot_tn(w_down, out_grad)
        grad_gate = (grad_hidden * upward * act_grad).astype(BF)
        grad_up = (grad_hidden * act).astype(BF)
        if step == 0:
            for copy in accs:
                copy.wait()
        back = dot_nn(w_gate, grad_gate) + dot_nn(w_up, grad_up)
        out = dot_nn(w_down, hidden)
        if step > 0 or not first:
            back = back_acc[...] + back
            out = out_acc[...] + out
        final = step == width // FC - 1
        if final and last:
            out_low, back_low = refs[10:]
            back_low[...] = back.astype(BF)
            out_low[...] = out.astype(BF)
            sources = (out_low, back_low)
        else:
            back_acc[...] = back
            out_acc[...] = out
            sources = (out_acc, back_acc)
        if final:
            stores = [pltpu.make_async_copy(src, dst, acc_sems.at[i]) for i, (src, dst) in enumerate(zip(sources, out_refs))]
            for copy in stores:
                copy.start()
        shape = (count, block, FC)
        grads[0, :, :, cols] = dot_nt(normed, grad_gate).astype(BF).reshape(shape)
        grads[1, :, :, cols] = dot_nt(normed, grad_up).astype(BF).reshape(shape)
        grads[2, :, :, cols] = dot_nt(out_grad, hidden).astype(BF).reshape(shape)
    if by_owner == 1:
        sends = [pltpu.make_async_copy(grads.at[c], grad_refs[0].at[:, c], out_sems.at[c]) for c in range(3)]
    else:
        sends = owner_copies(grad_refs, owners_ref, grads, out_sems, False)
    for copy in sends:
        copy.start()
    for copy in stores + sends:
        copy.wait()


SMEM_SPEC = pl.BlockSpec(memory_space=pltpu.SMEM)
VMEM_SPEC = pl.BlockSpec(memory_space=pltpu.VMEM)
ANY_SPEC = pl.BlockSpec(memory_space=pl.ANY)


def feed_forward(owners, normed, out_grad, weights, sums, by_owner, last):
    count, unused, block, width = weights.shape
    rows, tokens = normed.shape
    first = sums is None
    kind = BF if last else F32
    total = shape_of(rows, tokens, dtype=kind)
    sizes = block_sizes(count) if by_owner else [count]
    results = pl.pallas_call(
        functools.partial(ffn_kernel, len(sizes), first, last),
        in_specs=[SMEM_SPEC] + [ANY_SPEC] * (3 if first else 5),
        out_specs=[ANY_SPEC] * (2 + len(sizes)),
        out_shape=[total, total] + [shape_of(size, 3, block, width) for size in sizes],
        input_output_aliases={} if first or last else {4: 0, 5: 1},
        scratch_shapes=[
            pltpu.VMEM((rows, tokens), BF),
            pltpu.VMEM((rows, tokens), BF),
            pltpu.VMEM((rows, tokens), F32),
            pltpu.VMEM((rows, tokens), F32),
            pltpu.VMEM((3, count, block, width), BF),
            pltpu.VMEM((3, count, block, width), BF),
            pltpu.SemaphoreType.DMA((2,)),
            pltpu.SemaphoreType.DMA((3,)),
            pltpu.SemaphoreType.DMA((count,)),
            pltpu.SemaphoreType.DMA((2,)),
        ]
        + [pltpu.VMEM((rows, tokens), BF)] * (2 if last else 0),
        compiler_params=pltpu.CompilerParams(vmem_limit_bytes=VMEM),
        cost_estimate=pl.CostEstimate(
            flops=9 * 2 * rows * width * tokens, bytes_accessed=32 << 20, transcendentals=width * tokens
        ),
    )(owners, normed, out_grad, weights, *(() if first else sums))
    return results[:2], list(results[2:])


def block_sizes(count):
    return [2] * 8 if count == 16 else [count]


def place_kernel(parts, inward, owners_ref, *refs):
    sems = refs[-1]
    if inward:
        copies = owner_copies(refs[:parts], owners_ref, refs[parts], sems, True)
    else:
        copies = owner_copies(refs[1 : 1 + parts], owners_ref, refs[0], sems, False)
    for copy in copies:
        copy.start()
    for copy in copies:
        copy.wait()


def place_blocks(owners, blocks):
    count = owners.shape[0]
    return pl.pallas_call(
        functools.partial(place_kernel, len(blocks), True),
        in_specs=[SMEM_SPEC] + [ANY_SPEC] * len(blocks),
        out_specs=VMEM_SPEC,
        out_shape=shape_of(1, count, *blocks[0].shape[2:]),
        scratch_shapes=[pltpu.SemaphoreType.DMA((count,))],
        compiler_params=pltpu.CompilerParams(vmem_limit_bytes=VMEM),
    )(owners, *blocks)[0]


def split_blocks(owners, value):
    count = owners.shape[0]
    sizes = block_sizes(count)
    return list(
        pl.pallas_call(
            functools.partial(place_kernel, len(sizes), False),
            in_specs=[SMEM_SPEC, VMEM_SPEC],
            out_specs=[ANY_SPEC] * len(sizes),
            out_shape=[shape_of(size, 1, *value.shape[1:]) for size in sizes],
            scratch_shapes=[pltpu.SemaphoreType.DMA((count,))],
            compiler_params=pltpu.CompilerParams(vmem_limit_bytes=VMEM),
        )(owners, value[None])
    )


def merge_kernel(own_map, other_map, own_ref, other_ref, out_ref):
    rows = own_ref.shape[-1]
    here = dot_nn(own_map[...], own_ref[...].reshape(-1, rows))
    there = dot_nn(other_map[...], other_ref[...].reshape(-1, rows))
    out_ref[0] = (here + there).astype(BF)


def merge_cores(own_map, other_map, own, other):
    count, maps, share, rows = own.shape
    height = own_map.shape[0]
    whole = pl.BlockSpec(own_map.shape, lambda c: (0, 0))
    part = pl.BlockSpec((count, 1, share, rows), lambda c: (0, c, 0, 0))
    return pl.pallas_call(
        merge_kernel,
        grid=(maps,),
        in_specs=[whole, whole, part, part],
        out_specs=pl.BlockSpec((1, height, rows), lambda c: (c, 0, 0)),
        out_shape=shape_of(maps, height, rows),
        compiler_params=pltpu.CompilerParams(vmem_limit_bytes=VMEM),
        cost_estimate=pl.CostEstimate(flops=4 * maps * height * count * share * rows, bytes_accessed=12 << 20, transcendentals=0),
    )(own_map, other_map, own, other)


def cross_grad_kernel(parts, owners_ref, own_map, other_map, own_ref, other_ref, attn_own, attn_other, x_ref, mem_ref, g_ref, *refs):
    grads, sems = refs[parts:]
    unused, count, maps, share, rows = grads.shape
    pairs = [(own_ref[c], other_ref[c]) for c in range(3)] + [(attn_own[...], attn_other[...])]
    for c, (own, other) in enumerate(pairs):
        picked = (dot_tn(own_map[...], own) + dot_tn(other_map[...], other)).astype(BF)
        wide = (x_ref, mem_ref, mem_ref, g_ref)[c][...]
        grads[0, :, c] = dot_nt(picked, wide).astype(BF).reshape(count, share, rows)
    copies = owner_copies(refs[:parts], owners_ref, grads, sems, False)
    for copy in copies:
        copy.start()
    for copy in copies:
        copy.wait()


def cross_weight_grads(owners, own_map, other_map, own, other, attn_own, attn_other, normed, memory, grad, share):
    count = owners.shape[0]
    sizes = block_sizes(count)
    rows, tokens = normed.shape
    return list(
        pl.pallas_call(
            functools.partial(cross_grad_kernel, len(sizes)),
            in_specs=[SMEM_SPEC] + [VMEM_SPEC] * 9,
            out_specs=[ANY_SPEC] * len(sizes),
            out_shape=[shape_of(size, 1, 4, share, rows) for size in sizes],
            scratch_shapes=[pltpu.VMEM((1, count, 4, share, rows), BF), pltpu.SemaphoreType.DMA((count,))],
            compiler_params=pltpu.CompilerParams(vmem_limit_bytes=VMEM),
            cost_estimate=pl.CostEstimate(flops=8 * count * share * rows * tokens, bytes_accessed=16 << 20, transcendentals=0),
        )(owners, own_map, other_map, own, other, attn_own, attn_other, normed, memory, grad)
    )


def self_grad_kernel(parts, owners_ref, x_ref, qkv_ref, g_ref, attn_ref, *refs):
    grads, sems = refs[parts:]
    unused, count, block, width = grads.shape
    first = dot_nt(x_ref[...], qkv_ref[...].reshape(-1, x_ref.shape[1]))
    second = dot_nt(g_ref[...], attn_ref[...])
    grads[0] = jnp.concatenate([first, second], axis=1).astype(BF).reshape(count, block, width)
    copies = owner_copies(refs[:parts], owners_ref, grads, sems, False)
    for copy in copies:
        copy.start()
    for copy in copies:
        copy.wait()


def self_weight_grads(owners, normed, grad_qkv, grad, attn):
    count = owners.shape[0]
    sizes = block_sizes(count)
    rows, tokens = normed.shape
    width = 4 * attn.shape[0]
    return list(
        pl.pallas_call(
            functools.partial(self_grad_kernel, len(sizes)),
            in_specs=[SMEM_SPEC] + [VMEM_SPEC] * 4,
            out_specs=[ANY_SPEC] * len(sizes),
            out_shape=[shape_of(size, 1, rows // count, width) for size in sizes],
            scratch_shapes=[pltpu.VMEM((1, count, rows // count, width), BF), pltpu.SemaphoreType.DMA((count,))],
            compiler_params=pltpu.CompilerParams(vmem_limit_bytes=VMEM),
            cost_estimate=pl.CostEstimate(flops=2 * rows * width * tokens, bytes_accessed=12 << 20, transcendentals=0),
        )(owners, normed, grad_qkv, grad, attn)
    )


def squeeze_rows(value, block, pad):
    return jnp.concatenate([value[i : i + block] for i in range(0, value.shape[0], pad)], axis=0)


def spread_kernel(block, pad, in_ref, out_ref):
    value = in_ref[...].astype(F32)
    gap = jnp.zeros((pad - block, value.shape[1]), F32)
    parts = []
    for i in range(0, value.shape[0], block):
        parts += [value[i : i + block], gap]
    out_ref[...] = jnp.concatenate(parts, axis=0).astype(BF)


def spread_rows(value, block, pad):
    height, tokens = value.shape
    rows = height // block * pad
    return pl.pallas_call(
        functools.partial(spread_kernel, block, pad),
        grid=(tokens // QB,),
        in_specs=[pl.BlockSpec((height, QB), lambda j: (0, j))],
        out_specs=pl.BlockSpec((rows, QB), lambda j: (0, j)),
        out_shape=shape_of(rows, tokens),
        compiler_params=pltpu.CompilerParams(vmem_limit_bytes=VMEM),
        cost_estimate=pl.CostEstimate(flops=rows * tokens, bytes_accessed=4 * rows * tokens, transcendentals=0),
    )(value)


def out_kernel(block, pad, resid_ref, own_ref, other_ref, out_ref):
    total = resid_ref[...] + (own_ref[...].astype(F32) + other_ref[...].astype(F32))
    out_ref[...] = squeeze_rows(total, block, pad).astype(BF)


def layer_output(resid, own, other, block, pad):
    rows, tokens = resid.shape
    part = pl.BlockSpec((rows, QB), lambda j: (0, j))
    return pl.pallas_call(
        functools.partial(out_kernel, block, pad),
        grid=(tokens // QB,),
        in_specs=[part, part, part],
        out_specs=pl.BlockSpec((rows // pad * block, QB), lambda j: (0, j)),
        out_shape=shape_of(rows // pad * block, tokens),
        compiler_params=pltpu.CompilerParams(vmem_limit_bytes=VMEM),
        cost_estimate=pl.CostEstimate(flops=4 * rows * tokens, bytes_accessed=10 * rows * tokens, transcendentals=0),
    )(resid, own, other)


def norm_back_kernel(upstream, squeeze, n_ups, *refs):
    values_ref, inv_ref, gain_ref, base_ref = refs[:4]
    outs = refs[4 + n_ups :]
    up = upstream(*refs[4 : 4 + n_ups])
    values = values_ref[...].astype(F32)
    inv_root = inv_ref[...]
    scaled = up * gain_ref[...]
    along = jnp.sum(values * scaled, axis=0, keepdims=True) * (inv_root * inv_root * (1.0 / D))
    total = base_ref[...].astype(F32) + inv_root * (scaled - values * along)
    if squeeze:
        outs[0][...] = squeeze_rows(total, *squeeze)
    else:
        outs[0][...] = total
        outs[2][...] = total.astype(BF)
    gain_part = jnp.sum(up * (values * inv_root), axis=1, keepdims=True)

    @pl.when(pl.program_id(0) == 0)
    def start():
        outs[1][...] = gain_part

    @pl.when(pl.program_id(0) > 0)
    def add():
        outs[1][...] += gain_part


def norm_back(values, inv_root, gain, base, upstream, ups, fixed, squeeze=None, flops=0):
    rows, tokens = values.shape
    part = pl.BlockSpec((rows, QB), lambda j: (0, j))

    def spec(array, whole):
        if whole:
            return pl.BlockSpec(array.shape, lambda j: (0,) * array.ndim)
        return pl.BlockSpec(array.shape[:-1] + (QB,), lambda j: (0,) * (array.ndim - 1) + (j,))

    column = pl.BlockSpec((rows, 1), lambda j: (0, 0))
    height = rows // squeeze[1] * squeeze[0] if squeeze else rows
    return pl.pallas_call(
        functools.partial(norm_back_kernel, upstream, squeeze, len(ups)),
        grid=(tokens // QB,),
        in_specs=[part, pl.BlockSpec((1, QB), lambda j: (0, j)), column, part]
        + [spec(a, w) for a, w in zip(ups, fixed)],
        out_specs=[pl.BlockSpec((height, QB), lambda j: (0, j)), column] + ([] if squeeze else [part]),
        out_shape=[shape_of(height, tokens, dtype=F32), shape_of(rows, 1, dtype=F32)]
        + ([] if squeeze else [shape_of(rows, tokens)]),
        compiler_params=pltpu.CompilerParams(vmem_limit_bytes=VMEM),
        cost_estimate=pl.CostEstimate(flops=flops + 12 * rows * tokens, bytes_accessed=20 * rows * tokens, transcendentals=0),
    )(values, inv_root, gain, base, *ups)


def rotated(value, step):
    return lax.ppermute(value, "tok", [(t, (t // 4 + step) % 4 * 4 + t % 4) for t in range(16)])


def flipped(value, bits):
    return lax.ppermute(value, "tok", [(t, t ^ bits) for t in range(16)])


def block_owners():
    count = lax.axis_size("tok")
    index = lax.axis_index("tok")
    if count != 16:
        return jnp.arange(count, dtype=jnp.int32)
    owners = [(index // 4 + 4 - k) % 4 * 4 + (index % 4 ^ bits) for bits in range(4) for k in range(4)]
    return jnp.stack(owners).astype(jnp.int32)


class Transfer:
    def __init__(self, steps):
        self.steps = steps
        self.value = None
        self.flying = None

    @property
    def done(self):
        return self.value is not None

    def resume(self, arrived):
        try:
            return next(self.steps) if self.flying is None else self.steps.send(arrived)
        except StopIteration as stop:
            self.value = stop.value
            return []

    def launch(self, sends):
        self.flying = [move(operand, *way) for operand, move, way in sends]

    def finish(self):
        while not self.done:
            self.launch(self.resume(self.flying))
        return self.value


def tick(state, *transfers):
    moving = [t for t in transfers if not t.done]
    state, arrived = lax.optimization_barrier((state, [t.flying or [] for t in moving]))
    sends = [t.resume(a) for t, a in zip(moving, arrived)]
    operands = [[send[0] for send in group] for group in sends]
    state, operands = lax.optimization_barrier((state, operands))
    for t, group, ready in zip(moving, sends, operands):
        t.launch([(value, *send[1:]) for value, send in zip(ready, group)])
    return state


def gather_steps(value):
    if lax.axis_size("tok") != 16:
        return [lax.all_gather(value, "tok", axis=0, tiled=False)]
    far = yield [(value, rotated, (k,)) for k in (1, 2, 3)]
    low, high = jnp.stack([value, far[0]]), jnp.stack(far[1:])
    x_low, x_high, y_low, y_high = yield [
        (low, flipped, (1,)), (high, flipped, (1,)), (low, flipped, (2,)), (high, flipped, (2,))
    ]
    d_low, d_high = yield [(y_low, flipped, (1,)), (x_high, flipped, (2,))]
    return [low, high, x_low, x_high, y_low, y_high, d_low, d_high]


def low_sum(*terms):
    return sum(term.astype(F32) for term in terms).astype(BF)


def scatter_steps(blocks):
    if len(blocks) == 1:
        return lax.psum_scatter(blocks[0], "tok", scatter_dimension=0, tiled=False).astype(F32)
    m_low, m_high, x_low, x_high, y_low, y_high, d_low, d_high = blocks
    to_y, to_x, x_first, y_second = yield [
        (d_low, flipped, (1,)), (d_high, flipped, (2,)), (x_low, flipped, (1,)), (y_high, flipped, (2,))
    ]
    x_second, y_first = yield [
        (low_sum(x_high, to_x), flipped, (1,)), (low_sum(y_low, to_y), flipped, (2,))
    ]
    held = [
        low_sum(mine[k], gx[k], gy[k])
        for mine, gx, gy in ((m_low, x_first, y_first), (m_high, x_second, y_second))
        for k in range(2)
    ]
    far = yield [(held[k], rotated, (4 - k,)) for k in (1, 2, 3)]
    return sum(term.astype(F32) for term in (held[0], *far))


def sum_all(value):
    if lax.axis_size("tok") != 16:
        return lax.psum(value, ("tok", "mem"))
    value = value + other_core(value)
    value = (value + flipped(value, 1)) + (flipped(value, 2) + flipped(value, 3))
    return (value + rotated(value, 2)) + (rotated(value, 1) + rotated(value, 3))


def norm_stats(values):
    return lax.rsqrt(jnp.sum(values * values, axis=0, keepdims=True) * (1.0 / D) + EPS_NORM)


def adam_step(weight, first_mom, second_mom, gradient, clip_scale, step_rate, decay_rate):
    clipped = gradient * clip_scale
    first_new = BETA_FIRST * first_mom + (1.0 - BETA_FIRST) * clipped
    second_new = BETA_SECOND * second_mom + (1.0 - BETA_SECOND) * clipped * clipped
    first_hat = first_new / (1.0 - BETA_FIRST**STEP)
    second_hat = second_new / (1.0 - BETA_SECOND**STEP)
    weight_new = weight - step_rate * (
        first_hat / (jnp.sqrt(second_hat) + ADAM_EPS) + decay_rate * weight
    )
    return (weight_new, first_new, second_new)


def other_core(value):
    return lax.ppermute(value, "mem", [(0, 1), (1, 0)])


def core_pair(value, mem_index):
    other = other_core(value)
    return jnp.where(mem_index == 0, value, other), jnp.where(mem_index == 0, other, value)


def chunk_sizes(width):
    if lax.axis_size("tok") != 16:
        return [FC] * (width // FC)
    return [4 * FC, width - 4 * FC]


def shards(
    inputs,
    memory,
    kept_mask,
    segment_ids,
    bucket_ids,
    out_grad,
    self_weights,
    self_first,
    self_second,
    cross_weights,
    cross_first,
    cross_second,
    ffn_weights,
    ffn_first,
    ffn_second,
    norm_gains,
    gains_first,
    gains_second,
    rel_bias,
    rel_first,
    rel_second,
):
    count = lax.axis_size("tok")
    mem_index = lax.axis_index("mem")
    heads = rel_bias.shape[0]
    own = heads * DK
    block = norm_gains.shape[1]
    pad = -(-block // 16) * 16
    rows = count * pad
    share = cross_weights.shape[1]
    enc = memory.shape[1]

    def widen(value, axis):
        shape = value.shape
        split = value.reshape(shape[:axis] + (shape[axis] // block, block) + shape[axis + 1 :])
        pads = [(0, 0)] * split.ndim
        pads[axis + 1] = (0, pad - block)
        return jnp.pad(split, pads).reshape(shape[:axis] + (-1,) + shape[axis + 1 :])

    def narrow(value, axis):
        shape = value.shape
        split = value.reshape(shape[:axis] + (shape[axis] // pad, pad) + shape[axis + 1 :])
        kept = lax.slice_in_dim(split, 0, block, axis=axis + 1)
        return kept.reshape(shape[:axis] + (-1,) + shape[axis + 1 :])

    owners = block_owners()
    self_wire = widen(jnp.transpose(self_weights, (2, 0, 1)).astype(BF).reshape(block, 4 * own), 0)
    share_pad = -(-share // 16) * 16
    self_wire = self_wire.at[block : block + 3, :block].set(norm_gains.astype(BF))
    self_w = Transfer(gather_steps(self_wire[None]))
    tick((), self_w)
    ffn_wire = widen(jnp.transpose(ffn_weights, (0, 2, 1)).astype(BF), 1)
    ffn_w = []
    start = 0
    for size in chunk_sizes(ffn_wire.shape[2]):
        ffn_w.append(lax.all_gather(ffn_wire[:, :, start : start + size], "tok", axis=0, tiled=False))
        start += size
    cross_wire = jnp.pad(widen(cross_weights.astype(BF), 2), ((0, 0), (0, share_pad - share), (0, 0)))[None]
    cross_w = Transfer(gather_steps(cross_wire))
    ffn_wire = tick(ffn_wire, cross_w)

    x_low = spread_rows(inputs.T, block, pad)
    resid_zero = x_low.astype(F32)
    inv_one = norm_stats(resid_zero)
    x_low, inv_one = tick((x_low, inv_one), self_w)
    resid_zero = x_low.astype(F32)
    og_low = spread_rows(out_grad.T, block, pad)
    og_low, inv_one = tick((og_low, inv_one), self_w, cross_w)
    mem_own = spread_rows(memory.reshape(enc, D).T, block, pad)
    mem_parts = core_pair(mem_own, mem_index)
    mem_full = jnp.concatenate(mem_parts, axis=1)
    kept_parts = core_pair(kept_mask.reshape(enc), mem_index)
    keep = jnp.where(jnp.concatenate(kept_parts) > 0, 0.0, NEG_FILL).astype(F32).reshape(LEN, 1)
    seg_row = segment_ids.reshape(1, LEN)
    seg_col = segment_ids.reshape(LEN, 1)
    bucket_hot = (bucket_ids[None, :] == jnp.arange(NB, dtype=jnp.int32)[:, None]).astype(F32)
    bias_vec = jnp.dot(rel_bias, bucket_hot, precision=lax.Precision.HIGHEST)
    vec = jnp.pad(bias_vec, ((0, 0), (QB, 0))).reshape(heads, 1, QB + LEN)
    mem_full, inv_one, vec, keep = tick((mem_full, inv_one, vec, keep), self_w)

    self_blocks = place_blocks(owners, self_w.finish())
    gain_blocks = self_blocks[:, block : block + 3, :block]
    gains = widen(jnp.transpose(gain_blocks, (1, 0, 2)).reshape(3, -1), 1).reshape(3, rows, 1).astype(F32)
    self_own = self_blocks.reshape(rows, 4 * own)
    self_low, self_high = core_pair(self_own, mem_index)
    normed_one = (resid_zero * inv_one * gains[0]).astype(BF)
    qkv = dot_tn(self_own[:, : 3 * own], normed_one).astype(BF)
    qkv = tick(qkv, cross_w)
    attn_self, lse_self = self_forward(qkv, seg_row, seg_col, vec, heads)
    attn_self = tick(attn_self, cross_w)
    attn_low, attn_high = core_pair(attn_self, mem_index)
    resid_one = resid_zero + (
        dot_nn(self_low[:, 3 * own :], attn_low) + dot_nn(self_high[:, 3 * own :], attn_high)
    )

    inv_two = norm_stats(resid_one)
    normed_two = (resid_one * inv_two * gains[1]).astype(BF)
    cross_blocks = place_blocks(owners, cross_w.finish())
    place = jnp.arange(INNER, dtype=jnp.int32)[:, None]
    spot = jnp.arange(count * share_pad, dtype=jnp.int32)[None, :]
    match = (place // (2 * share) == spot // share_pad) & (place % share == spot % share_pad)
    core_of = place // share % 2
    own_map = (match & (core_of == mem_index)).astype(BF)
    other_map = (match & (core_of != mem_index)).astype(BF)
    cross_full = merge_cores(own_map, other_map, cross_blocks, other_core(cross_blocks))
    cross_own = lax.dynamic_slice_in_dim(cross_full, mem_index * own, own, 1)
    keyval = dot_nn(cross_own[1:3].reshape(2 * own, rows), mem_full).astype(BF)
    query = dot_nn(cross_own[0], normed_two).astype(BF)
    attn_cross, lse_cross = cross_forward(query, keyval, keep, heads)
    attn_cross_other = other_core(attn_cross)
    attn_cross_full = jnp.concatenate(
        [jnp.where(mem_index == 0, attn_cross, attn_cross_other), jnp.where(mem_index == 0, attn_cross_other, attn_cross)]
    )
    resid_two = resid_one + dot_tn(cross_full[3], attn_cross_full)

    inv_three = norm_stats(resid_two)
    normed_three = (resid_two * inv_three * gains[2]).astype(BF)
    sums = None
    ffn_g = []
    for i, weights in enumerate(ffn_w):
        last = i == len(ffn_w) - 1
        sums, grads = feed_forward(owners, normed_three, og_low, weights, sums, not last, last)
        ffn_g.append(Transfer(scatter_steps(grads)))
        if not last:
            sums = tick(sums, ffn_g[i])
    out_low, back_low = sums
    back_other = other_core(back_low)
    back_low, back_other = tick((back_low, back_other), *ffn_g[1:])
    grad_two, gain_three, grad_two_low = norm_back(
        resid_two, inv_three, gains[2], og_low,
        lambda own, other: own[...].astype(F32) + other[...].astype(F32), (back_low, back_other), (False, False),
    )

    grad_cattn = dot_nn(cross_own[3], grad_two_low).astype(BF)
    (cross_d,) = cross_backward(query, keyval, grad_cattn, lse_cross, keep, heads)
    cross_d = tick(cross_d, ffn_g[0])
    cross_d_other = other_core(cross_d)
    grad_q_full = jnp.concatenate(
        [jnp.where(mem_index == 0, cross_d[0], cross_d_other[0]), jnp.where(mem_index == 0, cross_d_other[0], cross_d[0])]
    )
    grad_one, gain_two, grad_one_low = norm_back(
        resid_one, inv_two, gains[1], grad_two,
        lambda w, g: dot_tn(w[...], g[...]), (cross_full[0], grad_q_full), (True, False), flops=2 * INNER * rows * LEN,
    )

    grad_sattn = dot_tn(self_own[:, 3 * own :], grad_one_low).astype(BF)
    grad_qkv, diag = self_backward(qkv, grad_sattn, lse_self, seg_row, seg_col, vec, heads)
    self_g = Transfer(scatter_steps(self_weight_grads(owners, normed_one, grad_qkv, grad_one_low, attn_self)))
    grad_qkv = tick(grad_qkv, self_g, ffn_g[0])
    other_half = lax.dynamic_slice_in_dim(own_map, (1 - mem_index) * own, own, 0)
    own_half = lax.dynamic_slice_in_dim(own_map, mem_index * own, own, 0)
    cross_g = Transfer(
        scatter_steps(
            cross_weight_grads(
                owners, own_half, other_half, cross_d, cross_d_other, attn_cross, attn_cross_other,
                normed_two, mem_full, grad_two_low, share_pad,
            )
        )
    )
    grad_qkv = tick(grad_qkv, cross_g)

    grad_other = other_core(grad_qkv)
    qkv_low = jnp.where(mem_index == 0, grad_qkv, grad_other).reshape(3 * own, LEN)
    qkv_high = jnp.where(mem_index == 0, grad_other, grad_qkv).reshape(3 * own, LEN)
    input_grad, gain_one = norm_back(
        x_low, inv_one, gains[0], grad_one,
        lambda a, b, c, d: dot_nn(a[:, : 3 * own], c[...]) + dot_nn(b[:, : 3 * own], d[...]),
        (self_low, self_high, qkv_low, qkv_high), (True, True, False, False), (block, pad), 12 * own * rows * LEN,
    )
    input_grad, gain_one = tick((input_grad.T, gain_one), self_g)
    kv_own = lax.dynamic_slice_in_dim(cross_d[1:], mem_index * enc, enc, 2)
    kv_other = lax.dynamic_slice_in_dim(cross_d_other[1:], mem_index * enc, enc, 2)
    kv_all = jnp.concatenate(
        [jnp.where(mem_index == 0, kv_own, kv_other), jnp.where(mem_index == 0, kv_other, kv_own)], axis=1
    ).reshape(2 * INNER, enc)
    memory_grad = narrow(dot_tn(cross_full[1:3].reshape(2 * INNER, rows), kv_all), 0).T.reshape(1, enc, D)
    memory_grad = tick(memory_grad, cross_g, self_g, ffn_g[0])
    layer_out = layer_output(resid_two, out_low, other_core(out_low), block, pad).T
    spread = jnp.zeros((heads, QB + LEN), F32)
    diag = diag[:, :, ::-1]
    for d in range(diag.shape[1]):
        spread = spread.at[:, d * QB : d * QB + 2 * QB].add(diag[:, d])
    rel_grad = jnp.dot(spread[:, QB:], bucket_hot.T, precision=lax.Precision.HIGHEST)
    layer_out = tick(layer_out, cross_g)
    ffn_sum = jnp.concatenate([t.finish() for t in ffn_g], axis=2)
    cross_sum = cross_g.finish()[0, :, :share]
    self_sum = self_g.finish()[0, :block]

    self_grads = self_sum.reshape(block, 4, own).transpose(1, 2, 0)
    ffn_grads = ffn_sum[:, :block].transpose(0, 2, 1)
    cross_grads = narrow(cross_sum, 2)
    local_squares = (
        jnp.sum(jnp.square(self_sum)) + jnp.sum(jnp.square(ffn_sum)) + jnp.sum(jnp.square(cross_sum))
    )
    gain_rows = 3 * rows // 128
    gain_grad = jnp.where(mem_index == 0, jnp.concatenate([gain_one, gain_two, gain_three], axis=1).T, 0.0)
    rel_padded = lax.dynamic_update_slice_in_dim(
        jnp.zeros((8, 128), F32), jnp.pad(rel_grad, ((0, 0), (0, 128 - NB))), mem_index * heads, 0
    )
    totals = sum_all(
        jnp.concatenate([gain_grad.reshape(gain_rows, 128), rel_padded.at[H, 0].set(local_squares)])
    )
    gains_total, rel_total = totals[:gain_rows].reshape(3, rows), totals[gain_rows : gain_rows + H, :NB]
    gains_sum = lax.dynamic_slice_in_dim(gains_total, lax.axis_index("tok") * pad, pad, 1)[:, :block]
    total_squares = totals[gain_rows + H, 0] + jnp.sum(gains_total * gains_total)
    grad_norm = jnp.sqrt(total_squares + jnp.sum(rel_total * rel_total))
    rel_g = lax.dynamic_slice_in_dim(rel_total, mem_index * heads, heads, 0)
    clip_scale = CLIP_NORM / jnp.maximum(grad_norm, CLIP_NORM)
    self_new = adam_step(self_weights, self_first, self_second, self_grads, clip_scale, RATE_MATRIX, DECAY_MATRIX)
    cross_new = adam_step(cross_weights, cross_first, cross_second, cross_grads, clip_scale, RATE_MATRIX, DECAY_MATRIX)
    ffn_new = adam_step(ffn_weights, ffn_first, ffn_second, ffn_grads, clip_scale, RATE_MATRIX, DECAY_MATRIX)
    gains_new = adam_step(norm_gains, gains_first, gains_second, gains_sum, clip_scale, RATE_SMALL, 0.0)
    rel_new = adam_step(rel_bias, rel_first, rel_second, rel_g, clip_scale, RATE_SMALL, 0.0)
    return (
        layer_out,
        input_grad,
        memory_grad,
        grad_norm,
        *self_new,
        *cross_new,
        *ffn_new,
        *gains_new,
        *rel_new,
    )


def solution(mesh):
    placed = (
        P("tok", None),
        P("tok", "mem", None),
        P("tok", "mem"),
        P("tok"),
        P(),
        P("tok", None),
        P(None, "mem", "tok"),
        P(None, "mem", "tok"),
        P(None, "mem", "tok"),
        P(None, ("tok", "mem"), None),
        P(None, ("tok", "mem"), None),
        P(None, ("tok", "mem"), None),
        P(None, "mem", "tok"),
        P(None, "mem", "tok"),
        P(None, "mem", "tok"),
        P(None, "tok"),
        P(None, "tok"),
        P(None, "tok"),
        P("mem", None),
        P("mem", None),
        P("mem", None),
    )
    return jax.shard_map(
        shards,
        mesh=mesh,
        in_specs=placed,
        out_specs=(
            P("tok", None),
            P("tok", None),
            P("tok", "mem", None),
            P(),
            P(None, "mem", "tok"),
            P(None, "mem", "tok"),
            P(None, "mem", "tok"),
            P(None, ("tok", "mem"), None),
            P(None, ("tok", "mem"), None),
            P(None, ("tok", "mem"), None),
            P(None, "mem", "tok"),
            P(None, "mem", "tok"),
            P(None, "mem", "tok"),
            P(None, "tok"),
            P(None, "tok"),
            P(None, "tok"),
            P("mem", None),
            P("mem", None),
            P("mem", None),
        ),
        check_vma=False,
    )
```

```python
import functools

import jax
import jax.numpy as jnp
from jax import lax
from jax.experimental import pallas as pl
from jax.experimental.pallas import tpu as pltpu
from jax.sharding import PartitionSpec as P

H = 6
DK = 64
NB = 32
LEN = 1024
STEP = 10
INNER = 384
D = 1472

EPS_NORM = 1e-06
NEG_FILL = -1e30
BETA_FIRST = 0.9
BETA_SECOND = 0.95
ADAM_EPS = 1e-08
RATE_MATRIX = 0.05
RATE_SMALL = 1.0
DECAY_MATRIX = 0.1
CLIP_NORM = 1.0

QB = 256
FC = 256
VMEM = 60 * 1024 * 1024
BF = jnp.bfloat16
F32 = jnp.float32


def dot_nn(a, b):
    return lax.dot_general(a, b, (((1,), (0,)), ((), ())), preferred_element_type=F32)


def dot_tn(a, b):
    return lax.dot_general(a, b, (((0,), (0,)), ((), ())), preferred_element_type=F32)


def dot_nt(a, b):
    return lax.dot_general(a, b, (((1,), (1,)), ((), ())), preferred_element_type=F32)


def bias_tile(vec, delta):
    row = vec[:, delta * QB : delta * QB + 2 * QB]
    wide = pltpu.roll(jnp.broadcast_to(row, (QB, 2 * QB)), 0, 1, stride=1, stride_axis=0)
    return wide[:, QB:]


def band(block):
    return max(0, block - LEN // 2 // QB)


def self_scores(q_ref, k_ref, segr_ref, segc_ref, tiles, block):
    low, high = band(block) * QB, (block + 1) * QB
    cols = slice(block * QB, high)
    scores = dot_tn(k_ref[:, low:high], q_ref[:, cols])
    scores = scores + jnp.concatenate([tiles[block - b] for b in range(band(block), block + 1)], axis=0)
    keys = lax.broadcasted_iota(jnp.int32, scores.shape, 0) + low
    queries = lax.broadcasted_iota(jnp.int32, scores.shape, 1) + block * QB
    allowed = (segc_ref[low:high, :] == segr_ref[:, cols]) & (keys <= queries)
    return jnp.where(allowed, scores, NEG_FILL)


def softmax_store(scores, v_block, o_ref, lse_ref, cols):
    top = jnp.max(scores, axis=0, keepdims=True)
    exps = jnp.exp(scores - top)
    total = jnp.sum(exps, axis=0, keepdims=True)
    probs = (exps * (1.0 / total)).astype(BF)
    o_ref[:, cols] = dot_nn(v_block, probs).astype(BF)
    lse_ref[0, :, cols] = top + jnp.log(total)


def self_fwd_kernel(q_ref, k_ref, v_ref, segr_ref, segc_ref, vec_ref, o_ref, lse_ref):
    tiles = [bias_tile(vec_ref[0], d) for d in range(LEN // 2 // QB + 1)]
    for block in range(LEN // QB):
        scores = self_scores(q_ref, k_ref, segr_ref, segc_ref, tiles, block)
        low, high = band(block) * QB, (block + 1) * QB
        softmax_store(scores, v_ref[:, low:high], o_ref, lse_ref, slice(block * QB, high))


def cross_fwd_kernel(q_ref, k_ref, v_ref, keep_ref, o_ref, lse_ref):
    for block in range(LEN // QB):
        cols = slice(block * QB, (block + 1) * QB)
        scores = dot_tn(k_ref[...], q_ref[:, cols]) + keep_ref[...]
        softmax_store(scores, v_ref[...], o_ref, lse_ref, cols)


def score_grads(scores, lse, k_block, v_block, q_block, do_block):
    probs = jnp.exp(scores - lse)
    grad_probs = dot_tn(v_block, do_block)
    delta = jnp.sum(probs * grad_probs, axis=0, keepdims=True)
    grads = (probs * (grad_probs - delta)).astype(BF)
    grad_q = dot_nn(k_block, grads)
    grad_k = dot_nt(q_block, grads)
    grad_v = dot_nt(do_block, probs.astype(BF))
    return grads, grad_q, grad_k, grad_v


def self_bwd_kernel(
    q_ref, k_ref, v_ref, do_ref, lse_ref, segr_ref, segc_ref, vec_ref,
    grad_ref, diag_ref, dk_acc, dv_acc, tile_acc,
):
    count = LEN // 2 // QB + 1
    tiles = [bias_tile(vec_ref[0], d) for d in range(count)]
    dk_acc[...] = jnp.zeros_like(dk_acc)
    dv_acc[...] = jnp.zeros_like(dv_acc)
    tile_acc[...] = jnp.zeros_like(tile_acc)
    for block in range(LEN // QB):
        low, high = band(block) * QB, (block + 1) * QB
        cols = slice(block * QB, high)
        scores = self_scores(q_ref, k_ref, segr_ref, segc_ref, tiles, block)
        grads, grad_q, grad_k, grad_v = score_grads(
            scores, lse_ref[0, :, cols], k_ref[:, low:high], v_ref[:, low:high], q_ref[:, cols], do_ref[:, cols]
        )
        grad_ref[0, :, cols] = grad_q.astype(BF)
        dk_acc[:, low:high] += grad_k
        dv_acc[:, low:high] += grad_v
        for b in range(band(block), block + 1):
            start = b * QB - low
            tile_acc[block - b] += grads[start : start + QB].astype(F32)
    grad_ref[1] = dk_acc[...].astype(BF)
    grad_ref[2] = dv_acc[...].astype(BF)
    spots = lax.broadcasted_iota(jnp.int32, (QB, QB), 0) + lax.broadcasted_iota(jnp.int32, (QB, QB), 1)
    mirror = (spots == QB - 1).astype(F32)
    for d in range(count):
        mirrored = lax.dot_general(
            tile_acc[d], mirror, (((1,), (0,)), ((), ())),
            precision=lax.Precision.HIGHEST, preferred_element_type=F32,
        )
        padded = jnp.concatenate([mirrored, jnp.zeros((QB, QB), F32)], axis=1)
        skewed = pltpu.roll(padded, 0, 1, stride=1, stride_axis=0)
        diag_ref[0, d : d + 1, :] = jnp.sum(skewed, axis=0, keepdims=True)


def cross_bwd_kernel(q_ref, k_ref, v_ref, do_ref, lse_ref, keep_ref, grad_ref, dk_acc, dv_acc):
    dk_acc[...] = jnp.zeros_like(dk_acc)
    dv_acc[...] = jnp.zeros_like(dv_acc)
    for block in range(LEN // QB):
        cols = slice(block * QB, (block + 1) * QB)
        scores = dot_tn(k_ref[...], q_ref[:, cols]) + keep_ref[...]
        grads, grad_q, grad_k, grad_v = score_grads(
            scores, lse_ref[0, :, cols], k_ref[...], v_ref[...], q_ref[:, cols], do_ref[:, cols]
        )
        grad_ref[0, :, cols] = grad_q.astype(BF)
        dk_acc[...] += grad_k
        dv_acc[...] += grad_v
    grad_ref[1] = dk_acc[...].astype(BF)
    grad_ref[2] = dv_acc[...].astype(BF)


def head_spec(first):
    return pl.BlockSpec((DK, LEN), lambda h: (first + h, 0))


def whole_spec(shape):
    return pl.BlockSpec(shape, lambda h: (0,) * len(shape))


def attn_call(kernel, heads, in_specs, out_specs, out_shape, operands, scratch, flops):
    return pl.pallas_call(
        kernel,
        grid=(heads,),
        in_specs=in_specs,
        out_specs=out_specs,
        out_shape=out_shape,
        scratch_shapes=scratch,
        compiler_params=pltpu.CompilerParams(vmem_limit_bytes=VMEM),
        cost_estimate=pl.CostEstimate(flops=flops, bytes_accessed=4 << 20, transcendentals=heads << 20),
    )(*operands)


def shape_of(*dims, dtype=BF):
    return jax.ShapeDtypeStruct(dims, dtype)


GRAD_SPEC = pl.BlockSpec((3, DK, LEN), lambda h: (0, h, 0))
LSE_SPEC = pl.BlockSpec((1, 1, LEN), lambda h: (h, 0, 0))


def self_forward(qkv, seg_row, seg_col, vec, heads):
    vec_spec = pl.BlockSpec((1, 1, vec.shape[2]), lambda h: (h, 0, 0))
    return attn_call(
        self_fwd_kernel, heads,
        [head_spec(0), head_spec(heads), head_spec(2 * heads), whole_spec((1, LEN)), whole_spec((LEN, 1)), vec_spec],
        [head_spec(0), LSE_SPEC],
        [shape_of(heads * DK, LEN), shape_of(heads, 1, LEN, dtype=F32)],
        (qkv, qkv, qkv, seg_row, seg_col, vec), [], heads * 2 * 2 * DK * LEN * LEN,
    )


def cross_forward(query, keyval, keep, heads):
    return attn_call(
        cross_fwd_kernel, heads,
        [head_spec(0), head_spec(0), head_spec(heads), whole_spec((LEN, 1))],
        [head_spec(0), LSE_SPEC],
        [shape_of(heads * DK, LEN), shape_of(heads, 1, LEN, dtype=F32)],
        (query, keyval, keyval, keep), [], heads * 2 * 2 * DK * LEN * LEN,
    )


def self_backward(qkv, grad_attn, lse, seg_row, seg_col, vec, heads):
    count = LEN // 2 // QB + 1
    vec_spec = pl.BlockSpec((1, 1, vec.shape[2]), lambda h: (h, 0, 0))
    out = shape_of(3, heads * DK, LEN)
    return attn_call(
        self_bwd_kernel, heads,
        [
            head_spec(0), head_spec(heads), head_spec(2 * heads), head_spec(0), LSE_SPEC,
            whole_spec((1, LEN)), whole_spec((LEN, 1)), vec_spec,
        ],
        [GRAD_SPEC, pl.BlockSpec((1, count, 2 * QB), lambda h: (h, 0, 0))],
        [out, shape_of(heads, count, 2 * QB, dtype=F32)],
        (qkv, qkv, qkv, grad_attn, lse, seg_row, seg_col, vec),
        [pltpu.VMEM((DK, LEN), F32), pltpu.VMEM((DK, LEN), F32), pltpu.VMEM((count, QB, QB), F32)],
        heads * 2 * 5 * DK * LEN * LEN,
    )


def cross_backward(query, keyval, grad_attn, lse, keep, heads):
    out = shape_of(3, heads * DK, LEN)
    return attn_call(
        cross_bwd_kernel, heads,
        [head_spec(0), head_spec(0), head_spec(heads), head_spec(0), LSE_SPEC, whole_spec((LEN, 1))],
        [GRAD_SPEC],
        [out],
        (query, keyval, keyval, grad_attn, lse, keep),
        [pltpu.VMEM((DK, LEN), F32), pltpu.VMEM((DK, LEN), F32)],
        heads * 2 * 5 * DK * LEN * LEN,
    )


def owner_copies(refs, owners_ref, target, sems, inward):
    copies = []
    slot = 0
    for ref in refs:
        for j in range(ref.shape[0]):
            owner = owners_ref[slot]
            here = target.at[:, owner]
            pair = (ref.at[j], here) if inward else (here, ref.at[j])
            copies.append(pltpu.make_async_copy(*pair, sems.at[slot]))
            slot += 1
    return copies


def ffn_kernel(by_owner, first, last, *refs):
    owners_ref, x_hbm, og_hbm, weight_hbm = refs[:4]
    refs = refs[4:]
    acc_refs, refs = ((), refs) if first else (refs[:2], refs[2:])
    out_refs, refs = refs[:2], refs[2:]
    grad_refs, refs = refs[:by_owner], refs[by_owner:]
    x_ref, og_ref, out_acc, back_acc, weights, grads, x_sems, in_sems, out_sems, acc_sems = refs[:10]
    unused, count, block, width = weights.shape
    rows = count * block
    inputs = [
        pltpu.make_async_copy(src, dst, x_sems.at[i])
        for i, (src, dst) in enumerate(((x_hbm, x_ref), (og_hbm, og_ref)))
    ]
    loads = [pltpu.make_async_copy(weight_hbm.at[:, c], weights.at[c], in_sems.at[c]) for c in range(3)]
    accs = [
        pltpu.make_async_copy(src, dst, acc_sems.at[i])
        for i, (src, dst) in enumerate(zip(acc_refs, (out_acc, back_acc)))
    ]
    for copy in (inputs[0], *loads, inputs[1], *accs):
        copy.start()
    inputs[0].wait()
    loads[0].wait()
    normed = x_ref[...]
    slope = 0.7978845608028654
    stores = []
    for step in range(width // FC):
        cols = slice(step * FC, (step + 1) * FC)
        w_gate = weights[0, :, :, cols].reshape(rows, FC)
        gate = dot_tn(w_gate, normed)
        square = gate * gate
        tanh = jnp.tanh(slope * gate * (1.0 + 0.044715 * square))
        half = 0.5 * (1.0 + tanh)
        act = gate * half
        act_grad = half + 0.5 * gate * (1.0 - tanh * tanh) * (slope * (1.0 + 0.134145 * square))
        if step == 0:
            loads[1].wait()
        w_up = weights[1, :, :, cols].reshape(rows, FC)
        upward = dot_tn(w_up, normed)
        hidden = (act * upward).astype(BF)
        if step == 0:
            loads[2].wait()
            inputs[1].wait()
        w_down = weights[2, :, :, cols].reshape(rows, FC)
        out_grad = og_ref[...]
        grad_hidden = dot_tn(w_down, out_grad)
        grad_gate = (grad_hidden * upward * act_grad).astype(BF)
        grad_up = (grad_hidden * act).astype(BF)
        if step == 0:
            for copy in accs:
                copy.wait()
        back = dot_nn(w_gate, grad_gate) + dot_nn(w_up, grad_up)
        out = dot_nn(w_down, hidden)
        if step > 0 or not first:
            back = back_acc[...] + back
            out = out_acc[...] + out
        final = step == width // FC - 1
        if final and last:
            out_low, back_low = refs[10:]
            back_low[...] = back.astype(BF)
            out_low[...] = out.astype(BF)
            sources = (out_low, back_low)
        else:
            back_acc[...] = back
            out_acc[...] = out
            sources = (out_acc, back_acc)
        if final:
            stores = [pltpu.make_async_copy(src, dst, acc_sems.at[i]) for i, (src, dst) in enumerate(zip(sources, out_refs))]
            for copy in stores:
                copy.start()
        shape = (count, block, FC)
        grads[0, :, :, cols] = dot_nt(normed, grad_gate).astype(BF).reshape(shape)
        grads[1, :, :, cols] = dot_nt(normed, grad_up).astype(BF).reshape(shape)
        grads[2, :, :, cols] = dot_nt(out_grad, hidden).astype(BF).reshape(shape)
    if by_owner == 1:
        sends = [pltpu.make_async_copy(grads.at[c], grad_refs[0].at[:, c], out_sems.at[c]) for c in range(3)]
    else:
        sends = owner_copies(grad_refs, owners_ref, grads, out_sems, False)
    for copy in sends:
        copy.start()
    for copy in stores + sends:
        copy.wait()


SMEM_SPEC = pl.BlockSpec(memory_space=pltpu.SMEM)
VMEM_SPEC = pl.BlockSpec(memory_space=pltpu.VMEM)
ANY_SPEC = pl.BlockSpec(memory_space=pl.ANY)


def feed_forward(owners, normed, out_grad, weights, sums, by_owner, last):
    count, unused, block, width = weights.shape
    rows, tokens = normed.shape
    first = sums is None
    kind = BF if last else F32
    total = shape_of(rows, tokens, dtype=kind)
    sizes = block_sizes(count) if by_owner else [count]
    results = pl.pallas_call(
        functools.partial(ffn_kernel, len(sizes), first, last),
        in_specs=[SMEM_SPEC] + [ANY_SPEC] * (3 if first else 5),
        out_specs=[ANY_SPEC] * (2 + len(sizes)),
        out_shape=[total, total] + [shape_of(size, 3, block, width) for size in sizes],
        input_output_aliases={} if first or last else {4: 0, 5: 1},
        scratch_shapes=[
            pltpu.VMEM((rows, tokens), BF),
            pltpu.VMEM((rows, tokens), BF),
            pltpu.VMEM((rows, tokens), F32),
            pltpu.VMEM((rows, tokens), F32),
            pltpu.VMEM((3, count, block, width), BF),
            pltpu.VMEM((3, count, block, width), BF),
            pltpu.SemaphoreType.DMA((2,)),
            pltpu.SemaphoreType.DMA((3,)),
            pltpu.SemaphoreType.DMA((count,)),
            pltpu.SemaphoreType.DMA((2,)),
        ]
        + [pltpu.VMEM((rows, tokens), BF)] * (2 if last else 0),
        compiler_params=pltpu.CompilerParams(vmem_limit_bytes=VMEM),
        cost_estimate=pl.CostEstimate(
            flops=9 * 2 * rows * width * tokens, bytes_accessed=32 << 20, transcendentals=width * tokens
        ),
    )(owners, normed, out_grad, weights, *(() if first else sums))
    return results[:2], list(results[2:])


def block_sizes(count):
    return [2] * 8 if count == 16 else [count]


def place_kernel(parts, inward, owners_ref, *refs):
    sems = refs[-1]
    if inward:
        copies = owner_copies(refs[:parts], owners_ref, refs[parts], sems, True)
    else:
        copies = owner_copies(refs[1 : 1 + parts], owners_ref, refs[0], sems, False)
    for copy in copies:
        copy.start()
    for copy in copies:
        copy.wait()


def place_blocks(owners, blocks):
    count = owners.shape[0]
    return pl.pallas_call(
        functools.partial(place_kernel, len(blocks), True),
        in_specs=[SMEM_SPEC] + [ANY_SPEC] * len(blocks),
        out_specs=VMEM_SPEC,
        out_shape=shape_of(1, count, *blocks[0].shape[2:]),
        scratch_shapes=[pltpu.SemaphoreType.DMA((count,))],
        compiler_params=pltpu.CompilerParams(vmem_limit_bytes=VMEM),
    )(owners, *blocks)[0]


def split_blocks(owners, value):
    count = owners.shape[0]
    sizes = block_sizes(count)
    return list(
        pl.pallas_call(
            functools.partial(place_kernel, len(sizes), False),
            in_specs=[SMEM_SPEC, VMEM_SPEC],
            out_specs=[ANY_SPEC] * len(sizes),
            out_shape=[shape_of(size, 1, *value.shape[1:]) for size in sizes],
            scratch_shapes=[pltpu.SemaphoreType.DMA((count,))],
            compiler_params=pltpu.CompilerParams(vmem_limit_bytes=VMEM),
        )(owners, value[None])
    )


def merge_kernel(own_map, other_map, own_ref, other_ref, out_ref):
    rows = own_ref.shape[-1]
    here = dot_nn(own_map[...], own_ref[...].reshape(-1, rows))
    there = dot_nn(other_map[...], other_ref[...].reshape(-1, rows))
    out_ref[0] = (here + there).astype(BF)


def merge_cores(own_map, other_map, own, other):
    count, maps, share, rows = own.shape
    height = own_map.shape[0]
    whole = pl.BlockSpec(own_map.shape, lambda c: (0, 0))
    part = pl.BlockSpec((count, 1, share, rows), lambda c: (0, c, 0, 0))
    return pl.pallas_call(
        merge_kernel,
        grid=(maps,),
        in_specs=[whole, whole, part, part],
        out_specs=pl.BlockSpec((1, height, rows), lambda c: (c, 0, 0)),
        out_shape=shape_of(maps, height, rows),
        compiler_params=pltpu.CompilerParams(vmem_limit_bytes=VMEM),
        cost_estimate=pl.CostEstimate(flops=4 * maps * height * count * share * rows, bytes_accessed=12 << 20, transcendentals=0),
    )(own_map, other_map, own, other)


def cross_grad_kernel(parts, owners_ref, own_map, other_map, own_ref, other_ref, attn_own, attn_other, x_ref, mem_ref, g_ref, *refs):
    grads, sems = refs[parts:]
    unused, count, maps, share, rows = grads.shape
    pairs = [(own_ref[c], other_ref[c]) for c in range(3)] + [(attn_own[...], attn_other[...])]
    for c, (own, other) in enumerate(pairs):
        picked = (dot_tn(own_map[...], own) + dot_tn(other_map[...], other)).astype(BF)
        wide = (x_ref, mem_ref, mem_ref, g_ref)[c][...]
        grads[0, :, c] = dot_nt(picked, wide).astype(BF).reshape(count, share, rows)
    copies = owner_copies(refs[:parts], owners_ref, grads, sems, False)
    for copy in copies:
        copy.start()
    for copy in copies:
        copy.wait()


def cross_weight_grads(owners, own_map, other_map, own, other, attn_own, attn_other, normed, memory, grad, share):
    count = owners.shape[0]
    sizes = block_sizes(count)
    rows, tokens = normed.shape
    return list(
        pl.pallas_call(
            functools.partial(cross_grad_kernel, len(sizes)),
            in_specs=[SMEM_SPEC] + [VMEM_SPEC] * 9,
            out_specs=[ANY_SPEC] * len(sizes),
            out_shape=[shape_of(size, 1, 4, share, rows) for size in sizes],
            scratch_shapes=[pltpu.VMEM((1, count, 4, share, rows), BF), pltpu.SemaphoreType.DMA((count,))],
            compiler_params=pltpu.CompilerParams(vmem_limit_bytes=VMEM),
            cost_estimate=pl.CostEstimate(flops=8 * count * share * rows * tokens, bytes_accessed=16 << 20, transcendentals=0),
        )(owners, own_map, other_map, own, other, attn_own, attn_other, normed, memory, grad)
    )


def self_grad_kernel(parts, owners_ref, x_ref, qkv_ref, g_ref, attn_ref, *refs):
    grads, sems = refs[parts:]
    unused, count, block, width = grads.shape
    first = dot_nt(x_ref[...], qkv_ref[...].reshape(-1, x_ref.shape[1]))
    second = dot_nt(g_ref[...], attn_ref[...])
    grads[0] = jnp.concatenate([first, second], axis=1).astype(BF).reshape(count, block, width)
    copies = owner_copies(refs[:parts], owners_ref, grads, sems, False)
    for copy in copies:
        copy.start()
    for copy in copies:
        copy.wait()


def self_weight_grads(owners, normed, grad_qkv, grad, attn):
    count = owners.shape[0]
    sizes = block_sizes(count)
    rows, tokens = normed.shape
    width = 4 * attn.shape[0]
    return list(
        pl.pallas_call(
            functools.partial(self_grad_kernel, len(sizes)),
            in_specs=[SMEM_SPEC] + [VMEM_SPEC] * 4,
            out_specs=[ANY_SPEC] * len(sizes),
            out_shape=[shape_of(size, 1, rows // count, width) for size in sizes],
            scratch_shapes=[pltpu.VMEM((1, count, rows // count, width), BF), pltpu.SemaphoreType.DMA((count,))],
            compiler_params=pltpu.CompilerParams(vmem_limit_bytes=VMEM),
            cost_estimate=pl.CostEstimate(flops=2 * rows * width * tokens, bytes_accessed=12 << 20, transcendentals=0),
        )(owners, normed, grad_qkv, grad, attn)
    )


def squeeze_rows(value, block, pad):
    return jnp.concatenate([value[i : i + block] for i in range(0, value.shape[0], pad)], axis=0)


def spread_kernel(block, pad, in_ref, out_ref):
    value = in_ref[...].astype(F32)
    gap = jnp.zeros((pad - block, value.shape[1]), F32)
    parts = []
    for i in range(0, value.shape[0], block):
        parts += [value[i : i + block], gap]
    out_ref[...] = jnp.concatenate(parts, axis=0).astype(BF)


def spread_rows(value, block, pad):
    height, tokens = value.shape
    rows = height // block * pad
    return pl.pallas_call(
        functools.partial(spread_kernel, block, pad),
        grid=(tokens // QB,),
        in_specs=[pl.BlockSpec((height, QB), lambda j: (0, j))],
        out_specs=pl.BlockSpec((rows, QB), lambda j: (0, j)),
        out_shape=shape_of(rows, tokens),
        compiler_params=pltpu.CompilerParams(vmem_limit_bytes=VMEM),
        cost_estimate=pl.CostEstimate(flops=rows * tokens, bytes_accessed=4 * rows * tokens, transcendentals=0),
    )(value)


def out_kernel(block, pad, resid_ref, own_ref, other_ref, out_ref):
    total = resid_ref[...] + (own_ref[...].astype(F32) + other_ref[...].astype(F32))
    out_ref[...] = squeeze_rows(total, block, pad).astype(BF)


def layer_output(resid, own, other, block, pad):
    rows, tokens = resid.shape
    part = pl.BlockSpec((rows, QB), lambda j: (0, j))
    return pl.pallas_call(
        functools.partial(out_kernel, block, pad),
        grid=(tokens // QB,),
        in_specs=[part, part, part],
        out_specs=pl.BlockSpec((rows // pad * block, QB), lambda j: (0, j)),
        out_shape=shape_of(rows // pad * block, tokens),
        compiler_params=pltpu.CompilerParams(vmem_limit_bytes=VMEM),
        cost_estimate=pl.CostEstimate(flops=4 * rows * tokens, bytes_accessed=10 * rows * tokens, transcendentals=0),
    )(resid, own, other)


def norm_back_kernel(upstream, squeeze, n_ups, *refs):
    values_ref, inv_ref, gain_ref, base_ref = refs[:4]
    outs = refs[4 + n_ups :]
    up = upstream(*refs[4 : 4 + n_ups])
    values = values_ref[...].astype(F32)
    inv_root = inv_ref[...]
    scaled = up * gain_ref[...]
    along = jnp.sum(values * scaled, axis=0, keepdims=True) * (inv_root * inv_root * (1.0 / D))
    total = base_ref[...].astype(F32) + inv_root * (scaled - values * along)
    outs[0][...] = squeeze_rows(total, *squeeze) if squeeze else total.astype(BF)
    gain_part = jnp.sum(up * (values * inv_root), axis=1, keepdims=True)

    @pl.when(pl.program_id(0) == 0)
    def start():
        outs[1][...] = gain_part

    @pl.when(pl.program_id(0) > 0)
    def add():
        outs[1][...] += gain_part


def norm_back(values, inv_root, gain, base, upstream, ups, fixed, squeeze=None, flops=0):
    rows, tokens = values.shape
    part = pl.BlockSpec((rows, QB), lambda j: (0, j))

    def spec(array, whole):
        if whole:
            return pl.BlockSpec(array.shape, lambda j: (0,) * array.ndim)
        return pl.BlockSpec(array.shape[:-1] + (QB,), lambda j: (0,) * (array.ndim - 1) + (j,))

    column = pl.BlockSpec((rows, 1), lambda j: (0, 0))
    height = rows // squeeze[1] * squeeze[0] if squeeze else rows
    return pl.pallas_call(
        functools.partial(norm_back_kernel, upstream, squeeze, len(ups)),
        grid=(tokens // QB,),
        in_specs=[part, pl.BlockSpec((1, QB), lambda j: (0, j)), column, part]
        + [spec(a, w) for a, w in zip(ups, fixed)],
        out_specs=[pl.BlockSpec((height, QB), lambda j: (0, j)), column],
        out_shape=[shape_of(height, tokens, dtype=F32 if squeeze else BF), shape_of(rows, 1, dtype=F32)],
        compiler_params=pltpu.CompilerParams(vmem_limit_bytes=VMEM),
        cost_estimate=pl.CostEstimate(flops=flops + 12 * rows * tokens, bytes_accessed=20 * rows * tokens, transcendentals=0),
    )(values, inv_root, gain, base, *ups)


def rotated(value, step):
    return lax.ppermute(value, "tok", [(t, (t // 4 + step) % 4 * 4 + t % 4) for t in range(16)])


def flipped(value, bits):
    return lax.ppermute(value, "tok", [(t, t ^ bits) for t in range(16)])


def block_owners():
    count = lax.axis_size("tok")
    index = lax.axis_index("tok")
    if count != 16:
        return jnp.arange(count, dtype=jnp.int32)
    owners = [(index // 4 + 4 - k) % 4 * 4 + (index % 4 ^ bits) for bits in range(4) for k in range(4)]
    return jnp.stack(owners).astype(jnp.int32)


class Transfer:
    def __init__(self, steps):
        self.steps = steps
        self.value = None
        self.flying = None

    @property
    def done(self):
        return self.value is not None

    def resume(self, arrived):
        try:
            return next(self.steps) if self.flying is None else self.steps.send(arrived)
        except StopIteration as stop:
            self.value = stop.value
            return []

    def launch(self, sends):
        self.flying = [move(operand, *way) for operand, move, way in sends]

    def finish(self):
        while not self.done:
            self.launch(self.resume(self.flying))
        return self.value


def tick(state, *transfers):
    moving = [t for t in transfers if not t.done]
    state, arrived = lax.optimization_barrier((state, [t.flying or [] for t in moving]))
    sends = [t.resume(a) for t, a in zip(moving, arrived)]
    operands = [[send[0] for send in group] for group in sends]
    state, operands = lax.optimization_barrier((state, operands))
    for t, group, ready in zip(moving, sends, operands):
        t.launch([(value, *send[1:]) for value, send in zip(ready, group)])
    return state


def gather_steps(value):
    if lax.axis_size("tok") != 16:
        return [lax.all_gather(value, "tok", axis=0, tiled=False)]
    far = yield [(value, rotated, (k,)) for k in (1, 2, 3)]
    low, high = jnp.stack([value, far[0]]), jnp.stack(far[1:])
    x_low, x_high, y_low, y_high = yield [
        (low, flipped, (1,)), (high, flipped, (1,)), (low, flipped, (2,)), (high, flipped, (2,))
    ]
    d_low, d_high = yield [(y_low, flipped, (1,)), (x_high, flipped, (2,))]
    return [low, high, x_low, x_high, y_low, y_high, d_low, d_high]


def low_sum(*terms):
    return sum(term.astype(F32) for term in terms).astype(BF)


def scatter_steps(blocks, wide=False):
    if len(blocks) == 1:
        return lax.psum_scatter(blocks[0], "tok", scatter_dimension=0, tiled=False).astype(F32)
    m_low, m_high, x_low, x_high, y_low, y_high, d_low, d_high = blocks
    if wide:
        to_y, to_x = yield [(d_low, flipped, (1,)), (d_high, flipped, (2,))]
        x_first, y_second = yield [(x_low, flipped, (1,)), (y_high, flipped, (2,))]
    else:
        to_y, to_x, x_first, y_second = yield [
            (d_low, flipped, (1,)), (d_high, flipped, (2,)), (x_low, flipped, (1,)), (y_high, flipped, (2,))
        ]
    x_second, y_first = yield [
        (low_sum(x_high, to_x), flipped, (1,)), (low_sum(y_low, to_y), flipped, (2,))
    ]
    held = [
        low_sum(mine[k], gx[k], gy[k])
        for mine, gx, gy in ((m_low, x_first, y_first), (m_high, x_second, y_second))
        for k in range(2)
    ]
    far = yield [(held[k], rotated, (4 - k,)) for k in (1, 2, 3)]
    return sum(term.astype(F32) for term in (held[0], *far))


def sum_all(value):
    if lax.axis_size("tok") != 16:
        return lax.psum(value, ("tok", "mem"))
    value = value + other_core(value)
    value = (value + flipped(value, 1)) + (flipped(value, 2) + flipped(value, 3))
    return (value + rotated(value, 2)) + (rotated(value, 1) + rotated(value, 3))


def norm_stats(values):
    return lax.rsqrt(jnp.sum(values * values, axis=0, keepdims=True) * (1.0 / D) + EPS_NORM)


def adam_step(weight, first_mom, second_mom, gradient, clip_scale, step_rate, decay_rate):
    clipped = gradient * clip_scale
    first_new = BETA_FIRST * first_mom + (1.0 - BETA_FIRST) * clipped
    second_new = BETA_SECOND * second_mom + (1.0 - BETA_SECOND) * clipped * clipped
    first_hat = first_new / (1.0 - BETA_FIRST**STEP)
    second_hat = second_new / (1.0 - BETA_SECOND**STEP)
    weight_new = weight - step_rate * (
        first_hat / (jnp.sqrt(second_hat) + ADAM_EPS) + decay_rate * weight
    )
    return (weight_new, first_new, second_new)


def other_core(value):
    return lax.ppermute(value, "mem", [(0, 1), (1, 0)])


def core_pair(value, mem_index):
    other = other_core(value)
    return jnp.where(mem_index == 0, value, other), jnp.where(mem_index == 0, other, value)


def chunk_sizes(width):
    if lax.axis_size("tok") != 16:
        return [FC] * (width // FC)
    return [5 * FC, width - 5 * FC]


def shards(
    inputs,
    memory,
    kept_mask,
    segment_ids,
    bucket_ids,
    out_grad,
    self_weights,
    self_first,
    self_second,
    cross_weights,
    cross_first,
    cross_second,
    ffn_weights,
    ffn_first,
    ffn_second,
    norm_gains,
    gains_first,
    gains_second,
    rel_bias,
    rel_first,
    rel_second,
):
    count = lax.axis_size("tok")
    mem_index = lax.axis_index("mem")
    heads = rel_bias.shape[0]
    own = heads * DK
    block = norm_gains.shape[1]
    pad = -(-block // 16) * 16
    rows = count * pad
    share = cross_weights.shape[1]
    enc = memory.shape[1]

    def widen(value, axis):
        shape = value.shape
        split = value.reshape(shape[:axis] + (shape[axis] // block, block) + shape[axis + 1 :])
        pads = [(0, 0)] * split.ndim
        pads[axis + 1] = (0, pad - block)
        return jnp.pad(split, pads).reshape(shape[:axis] + (-1,) + shape[axis + 1 :])

    def narrow(value, axis):
        shape = value.shape
        split = value.reshape(shape[:axis] + (shape[axis] // pad, pad) + shape[axis + 1 :])
        kept = lax.slice_in_dim(split, 0, block, axis=axis + 1)
        return kept.reshape(shape[:axis] + (-1,) + shape[axis + 1 :])

    owners = block_owners()
    self_wire = widen(jnp.transpose(self_weights, (2, 0, 1)).astype(BF).reshape(block, 4 * own), 0)
    share_pad = -(-share // 16) * 16
    self_wire = self_wire.at[block : block + 3, :block].set(norm_gains.astype(BF))
    self_w = Transfer(gather_steps(self_wire[None]))
    tick((), self_w)
    ffn_wire = widen(jnp.transpose(ffn_weights, (0, 2, 1)).astype(BF), 1)
    ffn_w = []
    start = 0
    for size in chunk_sizes(ffn_wire.shape[2]):
        ffn_w.append(lax.all_gather(ffn_wire[:, :, start : start + size], "tok", axis=0, tiled=False))
        start += size
    cross_wire = jnp.pad(widen(cross_weights.astype(BF), 2), ((0, 0), (0, share_pad - share), (0, 0)))[None]
    cross_w = Transfer(gather_steps(cross_wire))

    x_low = spread_rows(inputs.T, block, pad)
    x_low = tick(x_low, self_w, cross_w)
    resid_zero = x_low.astype(F32)
    inv_one = norm_stats(resid_zero)
    og_low = spread_rows(out_grad.T, block, pad)
    og_low, inv_one = tick((og_low, inv_one), self_w, cross_w)
    mem_own = spread_rows(memory.reshape(enc, D).T, block, pad)
    mem_parts = core_pair(mem_own, mem_index)
    mem_full = jnp.concatenate(mem_parts, axis=1)
    kept_parts = core_pair(kept_mask.reshape(enc), mem_index)
    keep = jnp.where(jnp.concatenate(kept_parts) > 0, 0.0, NEG_FILL).astype(F32).reshape(LEN, 1)
    seg_row = segment_ids.reshape(1, LEN)
    seg_col = segment_ids.reshape(LEN, 1)
    bucket_hot = (bucket_ids[None, :] == jnp.arange(NB, dtype=jnp.int32)[:, None]).astype(F32)
    bias_vec = jnp.dot(rel_bias, bucket_hot, precision=lax.Precision.HIGHEST)
    vec = jnp.pad(bias_vec, ((0, 0), (QB, 0))).reshape(heads, 1, QB + LEN)
    mem_full, inv_one, vec, keep = tick((mem_full, inv_one, vec, keep), self_w)

    self_blocks = place_blocks(owners, self_w.finish())
    gain_blocks = self_blocks[:, block : block + 3, :block]
    gain_rows = widen(jnp.transpose(gain_blocks, (1, 0, 2)).reshape(3, -1), 1).astype(F32)
    gains = lax.optimization_barrier([gain_rows[c].reshape(rows, 1) for c in range(3)])
    self_own = self_blocks.reshape(rows, 4 * own)
    self_low, self_high = core_pair(self_own, mem_index)
    normed_one = (resid_zero * inv_one * gains[0]).astype(BF)
    qkv = dot_tn(self_own[:, : 3 * own], normed_one).astype(BF)
    qkv = tick(qkv, cross_w)
    attn_self, lse_self = self_forward(qkv, seg_row, seg_col, vec, heads)
    attn_self = tick(attn_self, cross_w)
    attn_low, attn_high = core_pair(attn_self, mem_index)
    resid_one = resid_zero + (
        dot_nn(self_low[:, 3 * own :], attn_low) + dot_nn(self_high[:, 3 * own :], attn_high)
    )

    inv_two = norm_stats(resid_one)
    normed_two = (resid_one * inv_two * gains[1]).astype(BF)
    cross_blocks = place_blocks(owners, cross_w.finish())
    place = jnp.arange(INNER, dtype=jnp.int32)[:, None]
    spot = jnp.arange(count * share_pad, dtype=jnp.int32)[None, :]
    match = (place // (2 * share) == spot // share_pad) & (place % share == spot % share_pad)
    core_of = place // share % 2
    own_map = (match & (core_of == mem_index)).astype(BF)
    other_map = (match & (core_of != mem_index)).astype(BF)
    cross_full = merge_cores(own_map, other_map, cross_blocks, other_core(cross_blocks))
    cross_own = lax.dynamic_slice_in_dim(cross_full, mem_index * own, own, 1)
    keyval = dot_nn(cross_own[1:3].reshape(2 * own, rows), mem_full).astype(BF)
    query = dot_nn(cross_own[0], normed_two).astype(BF)
    attn_cross, lse_cross = cross_forward(query, keyval, keep, heads)
    attn_cross_other = other_core(attn_cross)
    attn_cross_full = jnp.concatenate(
        [jnp.where(mem_index == 0, attn_cross, attn_cross_other), jnp.where(mem_index == 0, attn_cross_other, attn_cross)]
    )
    resid_two = resid_one + dot_tn(cross_full[3], attn_cross_full)

    inv_three = norm_stats(resid_two)
    normed_three = (resid_two * inv_three * gains[2]).astype(BF)
    sums = None
    ffn_g = []
    for i, weights in enumerate(ffn_w):
        last = i == len(ffn_w) - 1
        sums, grads = feed_forward(owners, normed_three, og_low, weights, sums, last and count == 16, last)
        ffn_g.append(Transfer(scatter_steps(grads, True)))
        if not last:
            sums = tick(sums, ffn_g[i])
    out_low, back_low = sums
    back_other = other_core(back_low)
    back_low, back_other = tick((back_low, back_other), ffn_g[-1])
    grad_two_low, gain_three = norm_back(
        resid_two, inv_three, gains[2], og_low,
        lambda own, other: own[...].astype(F32) + other[...].astype(F32), (back_low, back_other), (False, False),
    )

    grad_two_low = tick(grad_two_low, ffn_g[-1])
    grad_cattn = dot_nn(cross_own[3], grad_two_low).astype(BF)
    (cross_d,) = cross_backward(query, keyval, grad_cattn, lse_cross, keep, heads)
    cross_d = tick(cross_d, ffn_g[-1])
    cross_d_other = other_core(cross_d)
    grad_q_full = jnp.concatenate(
        [jnp.where(mem_index == 0, cross_d[0], cross_d_other[0]), jnp.where(mem_index == 0, cross_d_other[0], cross_d[0])]
    )
    grad_one_low, gain_two = norm_back(
        resid_one, inv_two, gains[1], grad_two_low,
        lambda w, g: dot_tn(w[...], g[...]), (cross_full[0], grad_q_full), (True, False), flops=2 * INNER * rows * LEN,
    )

    grad_one_low, cross_d, cross_d_other = tick((grad_one_low, cross_d, cross_d_other), ffn_g[-1])
    other_half = lax.dynamic_slice_in_dim(own_map, (1 - mem_index) * own, own, 0)
    own_half = lax.dynamic_slice_in_dim(own_map, mem_index * own, own, 0)
    cross_g = Transfer(
        scatter_steps(
            cross_weight_grads(
                owners, own_half, other_half, cross_d, cross_d_other, attn_cross, attn_cross_other,
                normed_two, mem_full, grad_two_low, share_pad,
            )
        )
    )
    grad_sattn = dot_tn(self_own[:, 3 * own :], grad_one_low).astype(BF)
    grad_sattn = tick(grad_sattn, ffn_g[-1], cross_g)

    grad_qkv, diag = self_backward(qkv, grad_sattn, lse_self, seg_row, seg_col, vec, heads)
    grad_qkv = tick(grad_qkv, cross_g)
    self_g = Transfer(scatter_steps(self_weight_grads(owners, normed_one, grad_qkv, grad_one_low, attn_self)))
    grad_qkv, grad_other, out_low = tick((grad_qkv, other_core(grad_qkv), out_low), cross_g, self_g)

    qkv_low = jnp.where(mem_index == 0, grad_qkv, grad_other).reshape(3 * own, LEN)
    qkv_high = jnp.where(mem_index == 0, grad_other, grad_qkv).reshape(3 * own, LEN)
    input_grad, gain_one = norm_back(
        x_low, inv_one, gains[0], grad_one_low,
        lambda a, b, c, d: dot_nn(a[:, : 3 * own], c[...]) + dot_nn(b[:, : 3 * own], d[...]),
        (self_low, self_high, qkv_low, qkv_high), (True, True, False, False), (block, pad), 12 * own * rows * LEN,
    )
    input_grad, gain_one, out_low, cross_d, cross_d_other, diag = tick(
        (input_grad.T, gain_one, out_low, cross_d, cross_d_other, diag), self_g
    )
    out_other = other_core(out_low)
    kv_own = lax.dynamic_slice_in_dim(cross_d[1:], mem_index * enc, enc, 2)
    kv_other = lax.dynamic_slice_in_dim(cross_d_other[1:], mem_index * enc, enc, 2)
    kv_all = jnp.concatenate(
        [jnp.where(mem_index == 0, kv_own, kv_other), jnp.where(mem_index == 0, kv_other, kv_own)], axis=1
    ).reshape(2 * INNER, enc)
    memory_grad = narrow(dot_tn(cross_full[1:3].reshape(2 * INNER, rows), kv_all), 0).T.reshape(1, enc, D)
    memory_grad, out_low, out_other, diag = tick((memory_grad, out_low, out_other, diag), cross_g, self_g)
    layer_out = layer_output(resid_two, out_low, out_other, block, pad).T
    spread = jnp.zeros((heads, QB + LEN), F32)
    diag = diag[:, :, ::-1]
    for d in range(diag.shape[1]):
        spread = spread.at[:, d * QB : d * QB + 2 * QB].add(diag[:, d])
    rel_grad = jnp.dot(spread[:, QB:], bucket_hot.T, precision=lax.Precision.HIGHEST)
    layer_out, rel_grad = tick((layer_out, rel_grad), self_g, cross_g)
    ffn_sum = jnp.concatenate([t.finish() for t in ffn_g], axis=2)
    cross_sum = cross_g.finish()[0, :, :share]
    self_sum = self_g.finish()[0, :block]

    self_grads = self_sum.reshape(block, 4, own).transpose(1, 2, 0)
    ffn_grads = ffn_sum[:, :block].transpose(0, 2, 1)
    cross_grads = narrow(cross_sum, 2)
    local_squares = (
        jnp.sum(jnp.square(self_sum)) + jnp.sum(jnp.square(ffn_sum)) + jnp.sum(jnp.square(cross_sum))
    )
    self_grads, ffn_grads, cross_grads, local_squares = lax.optimization_barrier(
        (self_grads, ffn_grads, cross_grads, local_squares)
    )
    gain_lines = 3 * rows // 128
    gain_grad = jnp.where(mem_index == 0, jnp.concatenate([gain_one, gain_two, gain_three], axis=1).T, 0.0)
    rel_padded = lax.dynamic_update_slice_in_dim(
        jnp.zeros((8, 128), F32), jnp.pad(rel_grad, ((0, 0), (0, 128 - NB))), mem_index * heads, 0
    )
    totals = sum_all(
        jnp.concatenate([gain_grad.reshape(gain_lines, 128), rel_padded.at[H, 0].set(local_squares)])
    )
    gains_total, rel_total = totals[:gain_lines].reshape(3, rows), totals[gain_lines : gain_lines + H, :NB]
    gains_sum = lax.dynamic_slice_in_dim(gains_total, lax.axis_index("tok") * pad, pad, 1)[:, :block]
    total_squares = totals[gain_lines + H, 0] + jnp.sum(gains_total * gains_total)
    grad_norm = jnp.sqrt(total_squares + jnp.sum(rel_total * rel_total))
    rel_g = lax.dynamic_slice_in_dim(rel_total, mem_index * heads, heads, 0)
    clip_scale = CLIP_NORM / jnp.maximum(grad_norm, CLIP_NORM)
    self_new = adam_step(self_weights, self_first, self_second, self_grads, clip_scale, RATE_MATRIX, DECAY_MATRIX)
    cross_new = adam_step(cross_weights, cross_first, cross_second, cross_grads, clip_scale, RATE_MATRIX, DECAY_MATRIX)
    ffn_new = adam_step(ffn_weights, ffn_first, ffn_second, ffn_grads, clip_scale, RATE_MATRIX, DECAY_MATRIX)
    gains_new = adam_step(norm_gains, gains_first, gains_second, gains_sum, clip_scale, RATE_SMALL, 0.0)
    rel_new = adam_step(rel_bias, rel_first, rel_second, rel_g, clip_scale, RATE_SMALL, 0.0)
    return (
        layer_out,
        input_grad,
        memory_grad,
        grad_norm,
        *self_new,
        *cross_new,
        *ffn_new,
        *gains_new,
        *rel_new,
    )


def solution(mesh):
    placed = (
        P("tok", None),
        P("tok", "mem", None),
        P("tok", "mem"),
        P("tok"),
        P(),
        P("tok", None),
        P(None, "mem", "tok"),
        P(None, "mem", "tok"),
        P(None, "mem", "tok"),
        P(None, ("tok", "mem"), None),
        P(None, ("tok", "mem"), None),
        P(None, ("tok", "mem"), None),
        P(None, "mem", "tok"),
        P(None, "mem", "tok"),
        P(None, "mem", "tok"),
        P(None, "tok"),
        P(None, "tok"),
        P(None, "tok"),
        P("mem", None),
        P("mem", None),
        P("mem", None),
    )
    return jax.shard_map(
        shards,
        mesh=mesh,
        in_specs=placed,
        out_specs=(
            P("tok", None),
            P("tok", None),
            P("tok", "mem", None),
            P(),
            P(None, "mem", "tok"),
            P(None, "mem", "tok"),
            P(None, "mem", "tok"),
            P(None, ("tok", "mem"), None),
            P(None, ("tok", "mem"), None),
            P(None, ("tok", "mem"), None),
            P(None, "mem", "tok"),
            P(None, "mem", "tok"),
            P(None, "mem", "tok"),
            P(None, "tok"),
            P(None, "tok"),
            P(None, "tok"),
            P("mem", None),
            P("mem", None),
            P("mem", None),
        ),
        check_vma=False,
    )
```

```python
import functools

import jax
import jax.numpy as jnp
from jax import lax
from jax.experimental import pallas as pl
from jax.experimental.pallas import tpu as pltpu
from jax.sharding import PartitionSpec as P

H = 6
DK = 64
NB = 32
LEN = 1024
STEP = 10
INNER = 384
D = 1472

EPS_NORM = 1e-06
NEG_FILL = -1e30
BETA_FIRST = 0.9
BETA_SECOND = 0.95
ADAM_EPS = 1e-08
RATE_MATRIX = 0.05
RATE_SMALL = 1.0
DECAY_MATRIX = 0.1
CLIP_NORM = 1.0

QB = 256
FC = 256
VMEM = 60 * 1024 * 1024
BF = jnp.bfloat16
F32 = jnp.float32


def dot_nn(a, b):
    return lax.dot_general(a, b, (((1,), (0,)), ((), ())), preferred_element_type=F32)


def dot_tn(a, b):
    return lax.dot_general(a, b, (((0,), (0,)), ((), ())), preferred_element_type=F32)


def dot_nt(a, b):
    return lax.dot_general(a, b, (((1,), (1,)), ((), ())), preferred_element_type=F32)


def bias_tile(vec, delta):
    row = vec[:, delta * QB : delta * QB + 2 * QB]
    wide = pltpu.roll(jnp.broadcast_to(row, (QB, 2 * QB)), 0, 1, stride=1, stride_axis=0)
    return wide[:, QB:]


def band(block):
    return max(0, block - LEN // 2 // QB)


def self_scores(q_ref, k_ref, segr_ref, segc_ref, tiles, block):
    low, high = band(block) * QB, (block + 1) * QB
    cols = slice(block * QB, high)
    scores = dot_tn(k_ref[:, low:high], q_ref[:, cols])
    scores = scores + jnp.concatenate([tiles[block - b] for b in range(band(block), block + 1)], axis=0)
    keys = lax.broadcasted_iota(jnp.int32, scores.shape, 0) + low
    queries = lax.broadcasted_iota(jnp.int32, scores.shape, 1) + block * QB
    allowed = (segc_ref[low:high, :] == segr_ref[:, cols]) & (keys <= queries)
    return jnp.where(allowed, scores, NEG_FILL)


def softmax_store(scores, v_block, o_ref, lse_ref, cols):
    top = jnp.max(scores, axis=0, keepdims=True)
    exps = jnp.exp(scores - top)
    total = jnp.sum(exps, axis=0, keepdims=True)
    probs = (exps * (1.0 / total)).astype(BF)
    o_ref[:, cols] = dot_nn(v_block, probs).astype(BF)
    lse_ref[0, :, cols] = top + jnp.log(total)


def self_fwd_kernel(q_ref, k_ref, v_ref, segr_ref, segc_ref, vec_ref, o_ref, lse_ref):
    tiles = [bias_tile(vec_ref[0], d) for d in range(LEN // 2 // QB + 1)]
    for block in range(LEN // QB):
        scores = self_scores(q_ref, k_ref, segr_ref, segc_ref, tiles, block)
        low, high = band(block) * QB, (block + 1) * QB
        softmax_store(scores, v_ref[:, low:high], o_ref, lse_ref, slice(block * QB, high))


def cross_fwd_kernel(q_ref, k_ref, v_ref, keep_ref, o_ref, lse_ref):
    for block in range(LEN // QB):
        cols = slice(block * QB, (block + 1) * QB)
        scores = dot_tn(k_ref[...], q_ref[:, cols]) + keep_ref[...]
        softmax_store(scores, v_ref[...], o_ref, lse_ref, cols)


def score_grads(scores, lse, k_block, v_block, q_block, do_block):
    probs = jnp.exp(scores - lse)
    grad_probs = dot_tn(v_block, do_block)
    delta = jnp.sum(probs * grad_probs, axis=0, keepdims=True)
    grads = (probs * (grad_probs - delta)).astype(BF)
    grad_q = dot_nn(k_block, grads)
    grad_k = dot_nt(q_block, grads)
    grad_v = dot_nt(do_block, probs.astype(BF))
    return grads, grad_q, grad_k, grad_v


def self_bwd_kernel(
    q_ref, k_ref, v_ref, do_ref, lse_ref, segr_ref, segc_ref, vec_ref,
    grad_ref, diag_ref, dk_acc, dv_acc, tile_acc,
):
    count = LEN // 2 // QB + 1
    tiles = [bias_tile(vec_ref[0], d) for d in range(count)]
    dk_acc[...] = jnp.zeros_like(dk_acc)
    dv_acc[...] = jnp.zeros_like(dv_acc)
    tile_acc[...] = jnp.zeros_like(tile_acc)
    for block in range(LEN // QB):
        low, high = band(block) * QB, (block + 1) * QB
        cols = slice(block * QB, high)
        scores = self_scores(q_ref, k_ref, segr_ref, segc_ref, tiles, block)
        grads, grad_q, grad_k, grad_v = score_grads(
            scores, lse_ref[0, :, cols], k_ref[:, low:high], v_ref[:, low:high], q_ref[:, cols], do_ref[:, cols]
        )
        grad_ref[0, :, cols] = grad_q.astype(BF)
        dk_acc[:, low:high] += grad_k
        dv_acc[:, low:high] += grad_v
        for b in range(band(block), block + 1):
            start = b * QB - low
            tile_acc[block - b] += grads[start : start + QB].astype(F32)
    grad_ref[1] = dk_acc[...].astype(BF)
    grad_ref[2] = dv_acc[...].astype(BF)
    spots = lax.broadcasted_iota(jnp.int32, (QB, QB), 0) + lax.broadcasted_iota(jnp.int32, (QB, QB), 1)
    mirror = (spots == QB - 1).astype(F32)
    for d in range(count):
        mirrored = lax.dot_general(
            tile_acc[d], mirror, (((1,), (0,)), ((), ())),
            precision=lax.Precision.HIGHEST, preferred_element_type=F32,
        )
        padded = jnp.concatenate([mirrored, jnp.zeros((QB, QB), F32)], axis=1)
        skewed = pltpu.roll(padded, 0, 1, stride=1, stride_axis=0)
        diag_ref[0, d : d + 1, :] = jnp.sum(skewed, axis=0, keepdims=True)


def cross_bwd_kernel(q_ref, k_ref, v_ref, do_ref, lse_ref, keep_ref, grad_ref, dk_acc, dv_acc):
    dk_acc[...] = jnp.zeros_like(dk_acc)
    dv_acc[...] = jnp.zeros_like(dv_acc)
    for block in range(LEN // QB):
        cols = slice(block * QB, (block + 1) * QB)
        scores = dot_tn(k_ref[...], q_ref[:, cols]) + keep_ref[...]
        grads, grad_q, grad_k, grad_v = score_grads(
            scores, lse_ref[0, :, cols], k_ref[...], v_ref[...], q_ref[:, cols], do_ref[:, cols]
        )
        grad_ref[0, :, cols] = grad_q.astype(BF)
        dk_acc[...] += grad_k
        dv_acc[...] += grad_v
    grad_ref[1] = dk_acc[...].astype(BF)
    grad_ref[2] = dv_acc[...].astype(BF)


def head_spec(first):
    return pl.BlockSpec((DK, LEN), lambda h: (first + h, 0))


def whole_spec(shape):
    return pl.BlockSpec(shape, lambda h: (0,) * len(shape))


def attn_call(kernel, heads, in_specs, out_specs, out_shape, operands, scratch, flops):
    return pl.pallas_call(
        kernel,
        grid=(heads,),
        in_specs=in_specs,
        out_specs=out_specs,
        out_shape=out_shape,
        scratch_shapes=scratch,
        compiler_params=pltpu.CompilerParams(vmem_limit_bytes=VMEM),
        cost_estimate=pl.CostEstimate(flops=flops, bytes_accessed=4 << 20, transcendentals=heads << 20),
    )(*operands)


def shape_of(*dims, dtype=BF):
    return jax.ShapeDtypeStruct(dims, dtype)


GRAD_SPEC = pl.BlockSpec((3, DK, LEN), lambda h: (0, h, 0))
LSE_SPEC = pl.BlockSpec((1, 1, LEN), lambda h: (h, 0, 0))


def self_forward(qkv, seg_row, seg_col, vec, heads):
    vec_spec = pl.BlockSpec((1, 1, vec.shape[2]), lambda h: (h, 0, 0))
    return attn_call(
        self_fwd_kernel, heads,
        [head_spec(0), head_spec(heads), head_spec(2 * heads), whole_spec((1, LEN)), whole_spec((LEN, 1)), vec_spec],
        [head_spec(0), LSE_SPEC],
        [shape_of(heads * DK, LEN), shape_of(heads, 1, LEN, dtype=F32)],
        (qkv, qkv, qkv, seg_row, seg_col, vec), [], heads * 2 * 2 * DK * LEN * LEN,
    )


def cross_forward(query, keyval, keep, heads):
    return attn_call(
        cross_fwd_kernel, heads,
        [head_spec(0), head_spec(0), head_spec(heads), whole_spec((LEN, 1))],
        [head_spec(0), LSE_SPEC],
        [shape_of(heads * DK, LEN), shape_of(heads, 1, LEN, dtype=F32)],
        (query, keyval, keyval, keep), [], heads * 2 * 2 * DK * LEN * LEN,
    )


def self_backward(qkv, grad_attn, lse, seg_row, seg_col, vec, heads):
    count = LEN // 2 // QB + 1
    vec_spec = pl.BlockSpec((1, 1, vec.shape[2]), lambda h: (h, 0, 0))
    out = shape_of(3, heads * DK, LEN)
    return attn_call(
        self_bwd_kernel, heads,
        [
            head_spec(0), head_spec(heads), head_spec(2 * heads), head_spec(0), LSE_SPEC,
            whole_spec((1, LEN)), whole_spec((LEN, 1)), vec_spec,
        ],
        [GRAD_SPEC, pl.BlockSpec((1, count, 2 * QB), lambda h: (h, 0, 0))],
        [out, shape_of(heads, count, 2 * QB, dtype=F32)],
        (qkv, qkv, qkv, grad_attn, lse, seg_row, seg_col, vec),
        [pltpu.VMEM((DK, LEN), F32), pltpu.VMEM((DK, LEN), F32), pltpu.VMEM((count, QB, QB), F32)],
        heads * 2 * 5 * DK * LEN * LEN,
    )


def cross_backward(query, keyval, grad_attn, lse, keep, heads):
    out = shape_of(3, heads * DK, LEN)
    return attn_call(
        cross_bwd_kernel, heads,
        [head_spec(0), head_spec(0), head_spec(heads), head_spec(0), LSE_SPEC, whole_spec((LEN, 1))],
        [GRAD_SPEC],
        [out],
        (query, keyval, keyval, grad_attn, lse, keep),
        [pltpu.VMEM((DK, LEN), F32), pltpu.VMEM((DK, LEN), F32)],
        heads * 2 * 5 * DK * LEN * LEN,
    )


def owner_copies(refs, owners_ref, target, sems, inward):
    copies = []
    slot = 0
    for ref in refs:
        for j in range(ref.shape[0]):
            owner = owners_ref[slot]
            here = target.at[:, owner]
            pair = (ref.at[j], here) if inward else (here, ref.at[j])
            copies.append(pltpu.make_async_copy(*pair, sems.at[slot]))
            slot += 1
    return copies


def ffn_kernel(by_owner, first, last, *refs):
    owners_ref, x_hbm, og_hbm, weight_hbm = refs[:4]
    refs = refs[4:]
    acc_refs, refs = ((), refs) if first else (refs[:2], refs[2:])
    out_refs, refs = refs[:2], refs[2:]
    grad_refs, refs = refs[:by_owner], refs[by_owner:]
    x_ref, og_ref, out_acc, back_acc, weights, grads, x_sems, in_sems, out_sems, acc_sems = refs[:10]
    unused, count, block, width = weights.shape
    rows = count * block
    inputs = [
        pltpu.make_async_copy(src, dst, x_sems.at[i])
        for i, (src, dst) in enumerate(((x_hbm, x_ref), (og_hbm, og_ref)))
    ]
    loads = [pltpu.make_async_copy(weight_hbm.at[:, c], weights.at[c], in_sems.at[c]) for c in range(3)]
    accs = [
        pltpu.make_async_copy(src, dst, acc_sems.at[i])
        for i, (src, dst) in enumerate(zip(acc_refs, (out_acc, back_acc)))
    ]
    for copy in (inputs[0], *loads, inputs[1], *accs):
        copy.start()
    inputs[0].wait()
    loads[0].wait()
    normed = x_ref[...]
    slope = 0.7978845608028654
    stores = []
    for step in range(-(-width // FC)):
        cols = slice(step * FC, min((step + 1) * FC, width))
        units = cols.stop - cols.start
        w_gate = weights[0, :, :, cols].reshape(rows, units)
        gate = dot_tn(w_gate, normed)
        square = gate * gate
        tanh = jnp.tanh(slope * gate * (1.0 + 0.044715 * square))
        half = 0.5 * (1.0 + tanh)
        act = gate * half
        act_grad = half + 0.5 * gate * (1.0 - tanh * tanh) * (slope * (1.0 + 0.134145 * square))
        if step == 0:
            loads[1].wait()
        w_up = weights[1, :, :, cols].reshape(rows, units)
        upward = dot_tn(w_up, normed)
        hidden = (act * upward).astype(BF)
        if step == 0:
            loads[2].wait()
            inputs[1].wait()
        w_down = weights[2, :, :, cols].reshape(rows, units)
        out_grad = og_ref[...]
        grad_hidden = dot_tn(w_down, out_grad)
        grad_gate = (grad_hidden * upward * act_grad).astype(BF)
        grad_up = (grad_hidden * act).astype(BF)
        if step == 0:
            for copy in accs:
                copy.wait()
        back = dot_nn(w_gate, grad_gate) + dot_nn(w_up, grad_up)
        out = dot_nn(w_down, hidden)
        if step > 0 or not first:
            back = back_acc[...] + back
            out = out_acc[...] + out
        final = cols.stop == width
        if final and last:
            out_low, back_low = refs[10:]
            back_low[...] = back.astype(BF)
            out_low[...] = out.astype(BF)
            sources = (out_low, back_low)
        else:
            back_acc[...] = back
            out_acc[...] = out
            sources = (out_acc, back_acc)
        if final:
            stores = [pltpu.make_async_copy(src, dst, acc_sems.at[i]) for i, (src, dst) in enumerate(zip(sources, out_refs))]
            for copy in stores:
                copy.start()
        shape = (count, block, units)
        grads[0, :, :, cols] = dot_nt(normed, grad_gate).astype(BF).reshape(shape)
        grads[1, :, :, cols] = dot_nt(normed, grad_up).astype(BF).reshape(shape)
        grads[2, :, :, cols] = dot_nt(out_grad, hidden).astype(BF).reshape(shape)
    if by_owner == 1:
        sends = [pltpu.make_async_copy(grads.at[c], grad_refs[0].at[:, c], out_sems.at[c]) for c in range(3)]
    else:
        sends = owner_copies(grad_refs, owners_ref, grads, out_sems, False)
    for copy in sends:
        copy.start()
    for copy in stores + sends:
        copy.wait()


SMEM_SPEC = pl.BlockSpec(memory_space=pltpu.SMEM)
VMEM_SPEC = pl.BlockSpec(memory_space=pltpu.VMEM)
ANY_SPEC = pl.BlockSpec(memory_space=pl.ANY)


def feed_forward(owners, normed, out_grad, weights, sums, by_owner, last):
    count, unused, block, width = weights.shape
    rows, tokens = normed.shape
    first = sums is None
    kind = BF if last else F32
    total = shape_of(rows, tokens, dtype=kind)
    sizes = block_sizes(count) if by_owner else [count]
    results = pl.pallas_call(
        functools.partial(ffn_kernel, len(sizes), first, last),
        in_specs=[SMEM_SPEC] + [ANY_SPEC] * (3 if first else 5),
        out_specs=[ANY_SPEC] * (2 + len(sizes)),
        out_shape=[total, total] + [shape_of(size, 3, block, width) for size in sizes],
        input_output_aliases={} if first or last else {4: 0, 5: 1},
        scratch_shapes=[
            pltpu.VMEM((rows, tokens), BF),
            pltpu.VMEM((rows, tokens), BF),
            pltpu.VMEM((rows, tokens), F32),
            pltpu.VMEM((rows, tokens), F32),
            pltpu.VMEM((3, count, block, width), BF),
            pltpu.VMEM((3, count, block, width), BF),
            pltpu.SemaphoreType.DMA((2,)),
            pltpu.SemaphoreType.DMA((3,)),
            pltpu.SemaphoreType.DMA((count,)),
            pltpu.SemaphoreType.DMA((2,)),
        ]
        + [pltpu.VMEM((rows, tokens), BF)] * (2 if last else 0),
        compiler_params=pltpu.CompilerParams(vmem_limit_bytes=VMEM),
        cost_estimate=pl.CostEstimate(
            flops=9 * 2 * rows * width * tokens, bytes_accessed=32 << 20, transcendentals=width * tokens
        ),
    )(owners, normed, out_grad, weights, *(() if first else sums))
    return results[:2], list(results[2:])


def block_sizes(count):
    return [2] * 8 if count == 16 else [count]


def place_kernel(parts, inward, owners_ref, *refs):
    sems = refs[-1]
    if inward:
        copies = owner_copies(refs[:parts], owners_ref, refs[parts], sems, True)
    else:
        copies = owner_copies(refs[1 : 1 + parts], owners_ref, refs[0], sems, False)
    for copy in copies:
        copy.start()
    for copy in copies:
        copy.wait()


def place_blocks(owners, blocks):
    count = owners.shape[0]
    return pl.pallas_call(
        functools.partial(place_kernel, len(blocks), True),
        in_specs=[SMEM_SPEC] + [ANY_SPEC] * len(blocks),
        out_specs=VMEM_SPEC,
        out_shape=shape_of(1, count, *blocks[0].shape[2:]),
        scratch_shapes=[pltpu.SemaphoreType.DMA((count,))],
        compiler_params=pltpu.CompilerParams(vmem_limit_bytes=VMEM),
    )(owners, *blocks)[0]


def split_blocks(owners, value):
    count = owners.shape[0]
    sizes = block_sizes(count)
    return list(
        pl.pallas_call(
            functools.partial(place_kernel, len(sizes), False),
            in_specs=[SMEM_SPEC, VMEM_SPEC],
            out_specs=[ANY_SPEC] * len(sizes),
            out_shape=[shape_of(size, 1, *value.shape[1:]) for size in sizes],
            scratch_shapes=[pltpu.SemaphoreType.DMA((count,))],
            compiler_params=pltpu.CompilerParams(vmem_limit_bytes=VMEM),
        )(owners, value[None])
    )


def merge_kernel(own_map, other_map, own_ref, other_ref, out_ref):
    rows = own_ref.shape[-1]
    here = dot_nn(own_map[...], own_ref[...].reshape(-1, rows))
    there = dot_nn(other_map[...], other_ref[...].reshape(-1, rows))
    out_ref[0] = (here + there).astype(BF)


def merge_cores(own_map, other_map, own, other):
    count, maps, share, rows = own.shape
    height = own_map.shape[0]
    whole = pl.BlockSpec(own_map.shape, lambda c: (0, 0))
    part = pl.BlockSpec((count, 1, share, rows), lambda c: (0, c, 0, 0))
    return pl.pallas_call(
        merge_kernel,
        grid=(maps,),
        in_specs=[whole, whole, part, part],
        out_specs=pl.BlockSpec((1, height, rows), lambda c: (c, 0, 0)),
        out_shape=shape_of(maps, height, rows),
        compiler_params=pltpu.CompilerParams(vmem_limit_bytes=VMEM),
        cost_estimate=pl.CostEstimate(flops=4 * maps * height * count * share * rows, bytes_accessed=12 << 20, transcendentals=0),
    )(own_map, other_map, own, other)


def cross_grad_kernel(parts, owners_ref, own_map, other_map, own_ref, other_ref, attn_own, attn_other, x_ref, mem_ref, g_ref, *refs):
    grads, sems = refs[parts:]
    unused, count, maps, share, rows = grads.shape
    pairs = [(own_ref[c], other_ref[c]) for c in range(3)] + [(attn_own[...], attn_other[...])]
    for c, (own, other) in enumerate(pairs):
        picked = (dot_tn(own_map[...], own) + dot_tn(other_map[...], other)).astype(BF)
        wide = (x_ref, mem_ref, mem_ref, g_ref)[c][...]
        grads[0, :, c] = dot_nt(picked, wide).astype(BF).reshape(count, share, rows)
    copies = owner_copies(refs[:parts], owners_ref, grads, sems, False)
    for copy in copies:
        copy.start()
    for copy in copies:
        copy.wait()


def cross_weight_grads(owners, own_map, other_map, own, other, attn_own, attn_other, normed, memory, grad, share):
    count = owners.shape[0]
    sizes = block_sizes(count)
    rows, tokens = normed.shape
    return list(
        pl.pallas_call(
            functools.partial(cross_grad_kernel, len(sizes)),
            in_specs=[SMEM_SPEC] + [VMEM_SPEC] * 9,
            out_specs=[ANY_SPEC] * len(sizes),
            out_shape=[shape_of(size, 1, 4, share, rows) for size in sizes],
            scratch_shapes=[pltpu.VMEM((1, count, 4, share, rows), BF), pltpu.SemaphoreType.DMA((count,))],
            compiler_params=pltpu.CompilerParams(vmem_limit_bytes=VMEM),
            cost_estimate=pl.CostEstimate(flops=8 * count * share * rows * tokens, bytes_accessed=16 << 20, transcendentals=0),
        )(owners, own_map, other_map, own, other, attn_own, attn_other, normed, memory, grad)
    )


def self_grad_kernel(parts, owners_ref, x_ref, qkv_ref, g_ref, attn_ref, *refs):
    grads, sems = refs[parts:]
    unused, count, block, width = grads.shape
    first = dot_nt(x_ref[...], qkv_ref[...].reshape(-1, x_ref.shape[1]))
    second = dot_nt(g_ref[...], attn_ref[...])
    grads[0] = jnp.concatenate([first, second], axis=1).astype(BF).reshape(count, block, width)
    copies = owner_copies(refs[:parts], owners_ref, grads, sems, False)
    for copy in copies:
        copy.start()
    for copy in copies:
        copy.wait()


def self_weight_grads(owners, normed, grad_qkv, grad, attn):
    count = owners.shape[0]
    sizes = block_sizes(count)
    rows, tokens = normed.shape
    width = 4 * attn.shape[0]
    return list(
        pl.pallas_call(
            functools.partial(self_grad_kernel, len(sizes)),
            in_specs=[SMEM_SPEC] + [VMEM_SPEC] * 4,
            out_specs=[ANY_SPEC] * len(sizes),
            out_shape=[shape_of(size, 1, rows // count, width) for size in sizes],
            scratch_shapes=[pltpu.VMEM((1, count, rows // count, width), BF), pltpu.SemaphoreType.DMA((count,))],
            compiler_params=pltpu.CompilerParams(vmem_limit_bytes=VMEM),
            cost_estimate=pl.CostEstimate(flops=2 * rows * width * tokens, bytes_accessed=12 << 20, transcendentals=0),
        )(owners, normed, grad_qkv, grad, attn)
    )


def squeeze_rows(value, block, pad):
    return jnp.concatenate([value[i : i + block] for i in range(0, value.shape[0], pad)], axis=0)


def spread_kernel(block, pad, in_ref, out_ref):
    value = in_ref[...].astype(F32)
    gap = jnp.zeros((pad - block, value.shape[1]), F32)
    parts = []
    for i in range(0, value.shape[0], block):
        parts += [value[i : i + block], gap]
    out_ref[...] = jnp.concatenate(parts, axis=0).astype(BF)


def spread_rows(value, block, pad):
    height, tokens = value.shape
    rows = height // block * pad
    return pl.pallas_call(
        functools.partial(spread_kernel, block, pad),
        grid=(tokens // QB,),
        in_specs=[pl.BlockSpec((height, QB), lambda j: (0, j))],
        out_specs=pl.BlockSpec((rows, QB), lambda j: (0, j)),
        out_shape=shape_of(rows, tokens),
        compiler_params=pltpu.CompilerParams(vmem_limit_bytes=VMEM),
        cost_estimate=pl.CostEstimate(flops=rows * tokens, bytes_accessed=4 * rows * tokens, transcendentals=0),
    )(value)


def out_kernel(block, pad, resid_ref, own_ref, other_ref, out_ref):
    total = resid_ref[...] + (own_ref[...].astype(F32) + other_ref[...].astype(F32))
    out_ref[...] = squeeze_rows(total, block, pad).astype(BF)


def layer_output(resid, own, other, block, pad):
    rows, tokens = resid.shape
    part = pl.BlockSpec((rows, QB), lambda j: (0, j))
    return pl.pallas_call(
        functools.partial(out_kernel, block, pad),
        grid=(tokens // QB,),
        in_specs=[part, part, part],
        out_specs=pl.BlockSpec((rows // pad * block, QB), lambda j: (0, j)),
        out_shape=shape_of(rows // pad * block, tokens),
        compiler_params=pltpu.CompilerParams(vmem_limit_bytes=VMEM),
        cost_estimate=pl.CostEstimate(flops=4 * rows * tokens, bytes_accessed=10 * rows * tokens, transcendentals=0),
    )(resid, own, other)


def memory_kernel(block, pad, key_map, value_map, kv_ref, out_ref):
    total = dot_tn(key_map[0], kv_ref[0]) + dot_tn(value_map[0], kv_ref[1])
    out_ref[...] = squeeze_rows(total, block, pad)


def memory_gradient(maps, grad_kv, block, pad):
    unused, inner, rows = maps.shape
    enc = grad_kv.shape[2]
    return pl.pallas_call(
        functools.partial(memory_kernel, block, pad),
        grid=(enc // QB,),
        in_specs=[
            pl.BlockSpec((1, inner, rows), lambda j: (1, 0, 0)),
            pl.BlockSpec((1, inner, rows), lambda j: (2, 0, 0)),
            pl.BlockSpec((2, inner, QB), lambda j: (0, 0, j)),
        ],
        out_specs=pl.BlockSpec((rows // pad * block, QB), lambda j: (0, j)),
        out_shape=shape_of(rows // pad * block, enc, dtype=F32),
        compiler_params=pltpu.CompilerParams(vmem_limit_bytes=VMEM),
        cost_estimate=pl.CostEstimate(flops=4 * inner * rows * enc, bytes_accessed=8 << 20, transcendentals=0),
    )(maps, maps, grad_kv)


def norm_back_kernel(upstream, squeeze, n_ups, *refs):
    values_ref, inv_ref, gain_ref, base_ref = refs[:4]
    outs = refs[4 + n_ups :]
    up = upstream(*refs[4 : 4 + n_ups])
    values = values_ref[...].astype(F32)
    inv_root = inv_ref[...]
    scaled = up * gain_ref[...]
    along = jnp.sum(values * scaled, axis=0, keepdims=True) * (inv_root * inv_root * (1.0 / D))
    total = base_ref[...].astype(F32) + inv_root * (scaled - values * along)
    outs[0][...] = squeeze_rows(total, *squeeze) if squeeze else total.astype(BF)
    gain_part = jnp.sum(up * (values * inv_root), axis=1, keepdims=True)

    @pl.when(pl.program_id(0) == 0)
    def start():
        outs[1][...] = gain_part

    @pl.when(pl.program_id(0) > 0)
    def add():
        outs[1][...] += gain_part


def norm_back(values, inv_root, gain, base, upstream, ups, fixed, squeeze=None, flops=0):
    rows, tokens = values.shape
    part = pl.BlockSpec((rows, QB), lambda j: (0, j))

    def spec(array, whole):
        if whole is None:
            return pl.BlockSpec((1,) + array.shape[1:], lambda j: (0,) * array.ndim)
        if whole:
            return pl.BlockSpec(array.shape, lambda j: (0,) * array.ndim)
        return pl.BlockSpec(array.shape[:-1] + (QB,), lambda j: (0,) * (array.ndim - 1) + (j,))

    column = pl.BlockSpec((rows, 1), lambda j: (0, 0))
    height = rows // squeeze[1] * squeeze[0] if squeeze else rows
    return pl.pallas_call(
        functools.partial(norm_back_kernel, upstream, squeeze, len(ups)),
        grid=(tokens // QB,),
        in_specs=[part, pl.BlockSpec((1, QB), lambda j: (0, j)), column, part]
        + [spec(a, w) for a, w in zip(ups, fixed)],
        out_specs=[pl.BlockSpec((height, QB), lambda j: (0, j)), column],
        out_shape=[shape_of(height, tokens, dtype=F32 if squeeze else BF), shape_of(rows, 1, dtype=F32)],
        compiler_params=pltpu.CompilerParams(vmem_limit_bytes=VMEM),
        cost_estimate=pl.CostEstimate(flops=flops + 12 * rows * tokens, bytes_accessed=20 * rows * tokens, transcendentals=0),
    )(values, inv_root, gain, base, *ups)


def rotated(value, step):
    return lax.ppermute(value, "tok", [(t, (t // 4 + step) % 4 * 4 + t % 4) for t in range(16)])


def flipped(value, bits):
    return lax.ppermute(value, "tok", [(t, t ^ bits) for t in range(16)])


def block_owners():
    count = lax.axis_size("tok")
    index = lax.axis_index("tok")
    if count != 16:
        return jnp.arange(count, dtype=jnp.int32)
    owners = [(index // 4 + 4 - k) % 4 * 4 + (index % 4 ^ bits) for bits in range(4) for k in range(4)]
    return jnp.stack(owners).astype(jnp.int32)


class Transfer:
    def __init__(self, steps):
        self.steps = steps
        self.value = None
        self.flying = None

    @property
    def done(self):
        return self.value is not None

    def resume(self, arrived):
        try:
            return next(self.steps) if self.flying is None else self.steps.send(arrived)
        except StopIteration as stop:
            self.value = stop.value
            return []

    def launch(self, sends):
        self.flying = [move(operand, *way) for operand, move, way in sends]

    def finish(self):
        while not self.done:
            self.launch(self.resume(self.flying))
        return self.value


def tick(state, *transfers):
    moving = [t for t in transfers if not t.done]
    state, arrived = lax.optimization_barrier((state, [t.flying or [] for t in moving]))
    sends = [t.resume(a) for t, a in zip(moving, arrived)]
    operands = [[send[0] for send in group] for group in sends]
    state, operands = lax.optimization_barrier((state, operands))
    for t, group, ready in zip(moving, sends, operands):
        t.launch([(value, *send[1:]) for value, send in zip(ready, group)])
    return state


def gather_steps(value):
    if lax.axis_size("tok") != 16:
        return [lax.all_gather(value, "tok", axis=0, tiled=False)]
    far = yield [(value, rotated, (k,)) for k in (1, 2, 3)]
    low, high = jnp.stack([value, far[0]]), jnp.stack(far[1:])
    x_low, x_high, y_low, y_high = yield [
        (low, flipped, (1,)), (high, flipped, (1,)), (low, flipped, (2,)), (high, flipped, (2,))
    ]
    d_low, d_high = yield [(y_low, flipped, (1,)), (x_high, flipped, (2,))]
    return [low, high, x_low, x_high, y_low, y_high, d_low, d_high]


def low_sum(*terms):
    return sum(term.astype(F32) for term in terms).astype(BF)


def scatter_steps(blocks, wide=False):
    if len(blocks) == 1:
        return lax.psum_scatter(blocks[0], "tok", scatter_dimension=0, tiled=False).astype(F32)
    m_low, m_high, x_low, x_high, y_low, y_high, d_low, d_high = blocks
    if wide:
        to_y, to_x = yield [(d_low, flipped, (1,)), (d_high, flipped, (2,))]
        x_first, y_second = yield [(x_low, flipped, (1,)), (y_high, flipped, (2,))]
    else:
        to_y, to_x, x_first, y_second = yield [
            (d_low, flipped, (1,)), (d_high, flipped, (2,)), (x_low, flipped, (1,)), (y_high, flipped, (2,))
        ]
    x_second, y_first = yield [
        (low_sum(x_high, to_x), flipped, (1,)), (low_sum(y_low, to_y), flipped, (2,))
    ]
    held = [
        low_sum(mine[k], gx[k], gy[k])
        for mine, gx, gy in ((m_low, x_first, y_first), (m_high, x_second, y_second))
        for k in range(2)
    ]
    far = yield [(held[k], rotated, (4 - k,)) for k in (1, 2, 3)]
    return sum(term.astype(F32) for term in (held[0], *far))


def sum_all(value):
    if lax.axis_size("tok") != 16:
        return lax.psum(value, ("tok", "mem"))
    value = value + other_core(value)
    value = (value + flipped(value, 1)) + (flipped(value, 2) + flipped(value, 3))
    return (value + rotated(value, 2)) + (rotated(value, 1) + rotated(value, 3))


def norm_stats(values):
    return lax.rsqrt(jnp.sum(values * values, axis=0, keepdims=True) * (1.0 / D) + EPS_NORM)


def adam_step(weight, first_mom, second_mom, gradient, clip_scale, step_rate, decay_rate):
    clipped = gradient * clip_scale
    first_new = BETA_FIRST * first_mom + (1.0 - BETA_FIRST) * clipped
    second_new = BETA_SECOND * second_mom + (1.0 - BETA_SECOND) * clipped * clipped
    first_hat = first_new / (1.0 - BETA_FIRST**STEP)
    second_hat = second_new / (1.0 - BETA_SECOND**STEP)
    weight_new = weight - step_rate * (
        first_hat / (jnp.sqrt(second_hat) + ADAM_EPS) + decay_rate * weight
    )
    return (weight_new, first_new, second_new)


def other_core(value):
    return lax.ppermute(value, "mem", [(0, 1), (1, 0)])


def core_pair(value, mem_index):
    other = other_core(value)
    return jnp.where(mem_index == 0, value, other), jnp.where(mem_index == 0, other, value)


def chunk_sizes(width):
    if lax.axis_size("tok") != 16:
        return [FC] * (width // FC)
    return [5 * FC + FC // 2, width - 5 * FC - FC // 2]


def shards(
    inputs,
    memory,
    kept_mask,
    segment_ids,
    bucket_ids,
    out_grad,
    self_weights,
    self_first,
    self_second,
    cross_weights,
    cross_first,
    cross_second,
    ffn_weights,
    ffn_first,
    ffn_second,
    norm_gains,
    gains_first,
    gains_second,
    rel_bias,
    rel_first,
    rel_second,
):
    count = lax.axis_size("tok")
    mem_index = lax.axis_index("mem")
    heads = rel_bias.shape[0]
    own = heads * DK
    block = norm_gains.shape[1]
    pad = -(-block // 16) * 16
    rows = count * pad
    share = cross_weights.shape[1]
    enc = memory.shape[1]

    def widen(value, axis):
        shape = value.shape
        split = value.reshape(shape[:axis] + (shape[axis] // block, block) + shape[axis + 1 :])
        pads = [(0, 0)] * split.ndim
        pads[axis + 1] = (0, pad - block)
        return jnp.pad(split, pads).reshape(shape[:axis] + (-1,) + shape[axis + 1 :])

    def narrow(value, axis):
        shape = value.shape
        split = value.reshape(shape[:axis] + (shape[axis] // pad, pad) + shape[axis + 1 :])
        kept = lax.slice_in_dim(split, 0, block, axis=axis + 1)
        return kept.reshape(shape[:axis] + (-1,) + shape[axis + 1 :])

    owners = block_owners()
    self_wire = widen(jnp.transpose(self_weights, (2, 0, 1)).astype(BF).reshape(block, 4 * own), 0)
    share_pad = -(-share // 16) * 16
    self_wire = self_wire.at[block : block + 3, :block].set(norm_gains.astype(BF))
    self_w = Transfer(gather_steps(self_wire[None]))
    tick((), self_w)
    ffn_wire = widen(jnp.transpose(ffn_weights, (0, 2, 1)).astype(BF), 1)
    ffn_w = []
    start = 0
    for size in chunk_sizes(ffn_wire.shape[2]):
        ffn_w.append(lax.all_gather(ffn_wire[:, :, start : start + size], "tok", axis=0, tiled=False))
        start += size
    cross_wire = jnp.pad(widen(cross_weights.astype(BF), 2), ((0, 0), (0, share_pad - share), (0, 0)))[None]
    cross_w = Transfer(gather_steps(cross_wire))

    x_low = spread_rows(inputs.T, block, pad)
    x_low = tick(x_low, self_w, cross_w)
    resid_zero = x_low.astype(F32)
    inv_one = norm_stats(resid_zero)
    og_low = spread_rows(out_grad.T, block, pad)
    og_low, inv_one = tick((og_low, inv_one), self_w, cross_w)
    mem_own = spread_rows(memory.reshape(enc, D).T, block, pad)
    mem_parts = core_pair(mem_own, mem_index)
    mem_full = jnp.concatenate(mem_parts, axis=1)
    kept_parts = core_pair(kept_mask.reshape(enc), mem_index)
    keep = jnp.where(jnp.concatenate(kept_parts) > 0, 0.0, NEG_FILL).astype(F32).reshape(LEN, 1)
    seg_row = segment_ids.reshape(1, LEN)
    seg_col = segment_ids.reshape(LEN, 1)
    bucket_hot = (bucket_ids[None, :] == jnp.arange(NB, dtype=jnp.int32)[:, None]).astype(F32)
    bias_vec = jnp.dot(rel_bias, bucket_hot, precision=lax.Precision.HIGHEST)
    vec = jnp.pad(bias_vec, ((0, 0), (QB, 0))).reshape(heads, 1, QB + LEN)
    far_ids = jnp.pad(bucket_ids, (QB, 0), constant_values=-1)
    diag_ids = jnp.concatenate([far_ids[d * QB : (d + 2) * QB][::-1] for d in range(LEN // 2 // QB + 1)])
    diag_hot = (diag_ids[:, None] == jnp.arange(NB, dtype=jnp.int32)[None, :]).astype(F32)
    mem_full, inv_one, vec, keep, diag_hot = tick((mem_full, inv_one, vec, keep, diag_hot), self_w)

    self_blocks = place_blocks(owners, self_w.finish())
    gain_blocks = self_blocks[:, block : block + 3, :block]
    gain_rows = widen(jnp.transpose(gain_blocks, (1, 0, 2)).reshape(3, -1), 1).astype(F32)
    gains = lax.optimization_barrier([gain_rows[c].reshape(rows, 1) for c in range(3)])
    self_own = self_blocks.reshape(rows, 4 * own)
    self_low, self_high = core_pair(self_own, mem_index)
    normed_one = (resid_zero * inv_one * gains[0]).astype(BF)
    qkv = dot_tn(self_own[:, : 3 * own], normed_one).astype(BF)
    qkv = tick(qkv, cross_w)
    attn_self, lse_self = self_forward(qkv, seg_row, seg_col, vec, heads)
    attn_self = tick(attn_self, cross_w)
    attn_low, attn_high = core_pair(attn_self, mem_index)
    resid_one = resid_zero + (
        dot_nn(self_low[:, 3 * own :], attn_low) + dot_nn(self_high[:, 3 * own :], attn_high)
    )

    inv_two = norm_stats(resid_one)
    normed_two = (resid_one * inv_two * gains[1]).astype(BF)
    cross_blocks = place_blocks(owners, cross_w.finish())
    place = jnp.arange(INNER, dtype=jnp.int32)[:, None]
    spot = jnp.arange(count * share_pad, dtype=jnp.int32)[None, :]
    match = (place // (2 * share) == spot // share_pad) & (place % share == spot % share_pad)
    core_of = place // share % 2
    own_map = (match & (core_of == mem_index)).astype(BF)
    other_map = (match & (core_of != mem_index)).astype(BF)
    cross_full = merge_cores(own_map, other_map, cross_blocks, other_core(cross_blocks))
    cross_own = lax.dynamic_slice_in_dim(cross_full, mem_index * own, own, 1)
    keyval = dot_nn(cross_own[1:3].reshape(2 * own, rows), mem_full).astype(BF)
    query = dot_nn(cross_own[0], normed_two).astype(BF)
    attn_cross, lse_cross = cross_forward(query, keyval, keep, heads)
    attn_cross_other = other_core(attn_cross)
    attn_cross_full = jnp.concatenate(
        [jnp.where(mem_index == 0, attn_cross, attn_cross_other), jnp.where(mem_index == 0, attn_cross_other, attn_cross)]
    )
    resid_two = resid_one + dot_tn(cross_full[3], attn_cross_full)

    inv_three = norm_stats(resid_two)
    normed_three = (resid_two * inv_three * gains[2]).astype(BF)
    sums = None
    ffn_g = []
    for i, weights in enumerate(ffn_w):
        last = i == len(ffn_w) - 1
        sums, grads = feed_forward(owners, normed_three, og_low, weights, sums, last and count == 16, last)
        ffn_g.append(Transfer(scatter_steps(grads, True)))
        if not last:
            sums = tick(sums, ffn_g[i])
    out_low, back_low = sums
    back_other = other_core(back_low)
    back_low, back_other = tick((back_low, back_other), ffn_g[-1])
    grad_two_low, gain_three = norm_back(
        resid_two, inv_three, gains[2], og_low,
        lambda own, other: own[...].astype(F32) + other[...].astype(F32), (back_low, back_other), (False, False),
    )

    grad_two_low = tick(grad_two_low, ffn_g[-1])
    grad_cattn = dot_nn(cross_own[3], grad_two_low).astype(BF)
    (cross_d,) = cross_backward(query, keyval, grad_cattn, lse_cross, keep, heads)
    cross_d = tick(cross_d, ffn_g[-1])
    cross_d_other = other_core(cross_d)
    grad_q_full = jnp.concatenate(
        [jnp.where(mem_index == 0, cross_d[0], cross_d_other[0]), jnp.where(mem_index == 0, cross_d_other[0], cross_d[0])]
    )
    grad_one_low, gain_two = norm_back(
        resid_one, inv_two, gains[1], grad_two_low,
        lambda w, g: dot_tn(w[0], g[...]), (cross_full, grad_q_full), (None, False), flops=2 * INNER * rows * LEN,
    )

    grad_one_low, cross_d, cross_d_other = tick((grad_one_low, cross_d, cross_d_other), ffn_g[-1])
    other_half = lax.dynamic_slice_in_dim(own_map, (1 - mem_index) * own, own, 0)
    own_half = lax.dynamic_slice_in_dim(own_map, mem_index * own, own, 0)
    cross_g = Transfer(
        scatter_steps(
            cross_weight_grads(
                owners, own_half, other_half, cross_d, cross_d_other, attn_cross, attn_cross_other,
                normed_two, mem_full, grad_two_low, share_pad,
            )
        )
    )
    grad_sattn = dot_tn(self_own[:, 3 * own :], grad_one_low).astype(BF)
    grad_sattn = tick(grad_sattn, ffn_g[-1], cross_g)

    grad_qkv, diag = self_backward(qkv, grad_sattn, lse_self, seg_row, seg_col, vec, heads)
    grad_qkv = tick(grad_qkv, cross_g)
    self_g = Transfer(scatter_steps(self_weight_grads(owners, normed_one, grad_qkv, grad_one_low, attn_self)))
    grad_qkv, grad_other, out_low = tick((grad_qkv, other_core(grad_qkv), out_low), cross_g, self_g)

    qkv_low = jnp.where(mem_index == 0, grad_qkv, grad_other).reshape(3 * own, LEN)
    qkv_high = jnp.where(mem_index == 0, grad_other, grad_qkv).reshape(3 * own, LEN)
    input_grad, gain_one = norm_back(
        x_low, inv_one, gains[0], grad_one_low,
        lambda a, b, c, d: dot_nn(a[:, : 3 * own], c[...]) + dot_nn(b[:, : 3 * own], d[...]),
        (self_low, self_high, qkv_low, qkv_high), (True, True, False, False), (block, pad), 12 * own * rows * LEN,
    )
    input_grad, gain_one, out_low, cross_d, cross_d_other, diag = tick(
        (input_grad.T, gain_one, out_low, cross_d, cross_d_other, diag), self_g
    )
    out_other = other_core(out_low)
    kv_own = lax.dynamic_slice_in_dim(cross_d[1:], mem_index * enc, enc, 2)
    kv_other = lax.dynamic_slice_in_dim(cross_d_other[1:], mem_index * enc, enc, 2)
    kv_all = jnp.concatenate(
        [jnp.where(mem_index == 0, kv_own, kv_other), jnp.where(mem_index == 0, kv_other, kv_own)], axis=1
    )
    memory_grad = memory_gradient(cross_full, kv_all, block, pad).T.reshape(1, enc, D)
    memory_grad, out_low, out_other, diag = tick((memory_grad, out_low, out_other, diag), cross_g, self_g)
    layer_out = layer_output(resid_two, out_low, out_other, block, pad).T
    rel_grad = jnp.dot(diag.reshape(heads, -1), diag_hot, precision=lax.Precision.HIGHEST)
    layer_out, rel_grad = tick((layer_out, rel_grad), self_g, cross_g)
    ffn_sum = jnp.concatenate([t.finish() for t in ffn_g], axis=2)
    cross_sum = cross_g.finish()[0, :, :share]
    self_sum = self_g.finish()[0, :block]

    self_grads = self_sum.reshape(block, 4, own).transpose(1, 2, 0)
    ffn_grads = ffn_sum[:, :block].transpose(0, 2, 1)
    cross_grads = narrow(cross_sum, 2)
    local_squares = (
        jnp.sum(jnp.square(self_sum), keepdims=True)
        + jnp.sum(jnp.square(ffn_sum), keepdims=True)[0]
        + jnp.sum(jnp.square(cross_sum), keepdims=True)[0]
    )
    self_grads, ffn_grads, cross_grads, local_squares = lax.optimization_barrier(
        (self_grads, ffn_grads, cross_grads, local_squares)
    )
    gain_lines = 3 * rows // 128
    gain_grad = jnp.where(mem_index == 0, jnp.concatenate([gain_one, gain_two, gain_three], axis=1).T, 0.0)
    rel_padded = lax.dynamic_update_slice_in_dim(
        jnp.zeros((8, 128), F32), jnp.pad(rel_grad, ((0, 0), (0, 128 - NB))), mem_index * heads, 0
    )
    totals = sum_all(
        jnp.concatenate([gain_grad.reshape(gain_lines, 128), rel_padded.at[H : H + 1, :1].set(local_squares)])
    )
    gains_total, rel_total = totals[:gain_lines].reshape(3, rows), totals[gain_lines : gain_lines + H, :NB]
    gains_sum = lax.dynamic_slice_in_dim(gains_total, lax.axis_index("tok") * pad, pad, 1)[:, :block]
    total_squares = totals[gain_lines + H : gain_lines + H + 1, :1] + jnp.sum(gains_total * gains_total, keepdims=True)
    grad_norm = jnp.sqrt(total_squares + jnp.sum(rel_total * rel_total, keepdims=True))
    rel_g = lax.dynamic_slice_in_dim(rel_total, mem_index * heads, heads, 0)
    clip_scale = CLIP_NORM / jnp.maximum(grad_norm, CLIP_NORM)
    self_new = adam_step(self_weights, self_first, self_second, self_grads, clip_scale, RATE_MATRIX, DECAY_MATRIX)
    cross_new = adam_step(cross_weights, cross_first, cross_second, cross_grads, clip_scale, RATE_MATRIX, DECAY_MATRIX)
    ffn_new = adam_step(ffn_weights, ffn_first, ffn_second, ffn_grads, clip_scale, RATE_MATRIX, DECAY_MATRIX)
    gains_new = adam_step(norm_gains, gains_first, gains_second, gains_sum, clip_scale, RATE_SMALL, 0.0)
    rel_new = adam_step(rel_bias, rel_first, rel_second, rel_g, clip_scale, RATE_SMALL, 0.0)
    return (
        layer_out,
        input_grad,
        memory_grad,
        grad_norm.reshape(()),
        *self_new,
        *cross_new,
        *ffn_new,
        *gains_new,
        *rel_new,
    )


def solution(mesh):
    placed = (
        P("tok", None),
        P("tok", "mem", None),
        P("tok", "mem"),
        P("tok"),
        P(),
        P("tok", None),
        P(None, "mem", "tok"),
        P(None, "mem", "tok"),
        P(None, "mem", "tok"),
        P(None, ("tok", "mem"), None),
        P(None, ("tok", "mem"), None),
        P(None, ("tok", "mem"), None),
        P(None, "mem", "tok"),
        P(None, "mem", "tok"),
        P(None, "mem", "tok"),
        P(None, "tok"),
        P(None, "tok"),
        P(None, "tok"),
        P("mem", None),
        P("mem", None),
        P("mem", None),
    )
    return jax.shard_map(
        shards,
        mesh=mesh,
        in_specs=placed,
        out_specs=(
            P("tok", None),
            P("tok", None),
            P("tok", "mem", None),
            P(),
            P(None, "mem", "tok"),
            P(None, "mem", "tok"),
            P(None, "mem", "tok"),
            P(None, ("tok", "mem"), None),
            P(None, ("tok", "mem"), None),
            P(None, ("tok", "mem"), None),
            P(None, "mem", "tok"),
            P(None, "mem", "tok"),
            P(None, "mem", "tok"),
            P(None, "tok"),
            P(None, "tok"),
            P(None, "tok"),
            P("mem", None),
            P("mem", None),
            P("mem", None),
        ),
        check_vma=False,
    )
```

```python
import functools

import jax
import jax.numpy as jnp
from jax import lax
from jax.experimental import pallas as pl
from jax.experimental.pallas import tpu as pltpu
from jax.sharding import PartitionSpec as P

H = 6
DK = 64
NB = 32
LEN = 1024
STEP = 10
INNER = 384
D = 1472

EPS_NORM = 1e-06
NEG_FILL = -1e30
BETA_FIRST = 0.9
BETA_SECOND = 0.95
ADAM_EPS = 1e-08
RATE_MATRIX = 0.05
RATE_SMALL = 1.0
DECAY_MATRIX = 0.1
CLIP_NORM = 1.0

QB = 256
FC = 256
VMEM = 60 * 1024 * 1024
BF = jnp.bfloat16
F32 = jnp.float32


def dot_nn(a, b):
    return lax.dot_general(a, b, (((1,), (0,)), ((), ())), preferred_element_type=F32)


def dot_tn(a, b):
    return lax.dot_general(a, b, (((0,), (0,)), ((), ())), preferred_element_type=F32)


def dot_nt(a, b):
    return lax.dot_general(a, b, (((1,), (1,)), ((), ())), preferred_element_type=F32)


def bias_tile(vec, delta):
    row = vec[:, delta * QB : delta * QB + 2 * QB]
    wide = pltpu.roll(jnp.broadcast_to(row, (QB, 2 * QB)), 0, 1, stride=1, stride_axis=0)
    return wide[:, QB:]


def band(block):
    return max(0, block - LEN // 2 // QB)


def self_scores(q_ref, k_ref, segr_ref, segc_ref, tiles, block):
    low, high = band(block) * QB, (block + 1) * QB
    cols = slice(block * QB, high)
    scores = dot_tn(k_ref[:, low:high], q_ref[:, cols])
    scores = scores + jnp.concatenate([tiles[block - b] for b in range(band(block), block + 1)], axis=0)
    keys = lax.broadcasted_iota(jnp.int32, scores.shape, 0) + low
    queries = lax.broadcasted_iota(jnp.int32, scores.shape, 1) + block * QB
    allowed = (segc_ref[low:high, :] == segr_ref[:, cols]) & (keys <= queries)
    return jnp.where(allowed, scores, NEG_FILL)


def softmax_store(scores, v_block, o_ref, lse_ref, cols):
    top = jnp.max(scores, axis=0, keepdims=True)
    exps = jnp.exp(scores - top)
    total = jnp.sum(exps, axis=0, keepdims=True)
    probs = (exps * (1.0 / total)).astype(BF)
    o_ref[:, cols] = dot_nn(v_block, probs).astype(BF)
    lse_ref[0, :, cols] = top + jnp.log(total)


def self_fwd_kernel(q_ref, k_ref, v_ref, segr_ref, segc_ref, vec_ref, o_ref, lse_ref):
    tiles = [bias_tile(vec_ref[0], d) for d in range(LEN // 2 // QB + 1)]
    for block in range(LEN // QB):
        scores = self_scores(q_ref, k_ref, segr_ref, segc_ref, tiles, block)
        low, high = band(block) * QB, (block + 1) * QB
        softmax_store(scores, v_ref[:, low:high], o_ref, lse_ref, slice(block * QB, high))


def cross_fwd_kernel(q_ref, k_ref, v_ref, keep_ref, o_ref, lse_ref):
    for block in range(LEN // QB):
        cols = slice(block * QB, (block + 1) * QB)
        scores = jnp.where(keep_ref[...] > 0.0, dot_tn(k_ref[...], q_ref[:, cols]), NEG_FILL)
        softmax_store(scores, v_ref[...], o_ref, lse_ref, cols)


def score_grads(scores, lse, k_block, v_block, q_block, do_block):
    probs = jnp.exp(scores - lse)
    grad_probs = dot_tn(v_block, do_block)
    delta = jnp.sum(probs * grad_probs, axis=0, keepdims=True)
    grads = (probs * (grad_probs - delta)).astype(BF)
    grad_q = dot_nn(k_block, grads)
    grad_k = dot_nt(q_block, grads)
    grad_v = dot_nt(do_block, probs.astype(BF))
    return grads, grad_q, grad_k, grad_v


def self_bwd_kernel(
    q_ref, k_ref, v_ref, do_ref, lse_ref, segr_ref, segc_ref, vec_ref,
    grad_ref, diag_ref, dk_acc, dv_acc, tile_acc,
):
    count = LEN // 2 // QB + 1
    tiles = [bias_tile(vec_ref[0], d) for d in range(count)]
    dk_acc[...] = jnp.zeros_like(dk_acc)
    dv_acc[...] = jnp.zeros_like(dv_acc)
    tile_acc[...] = jnp.zeros_like(tile_acc)
    for block in range(LEN // QB):
        low, high = band(block) * QB, (block + 1) * QB
        cols = slice(block * QB, high)
        scores = self_scores(q_ref, k_ref, segr_ref, segc_ref, tiles, block)
        grads, grad_q, grad_k, grad_v = score_grads(
            scores, lse_ref[0, :, cols], k_ref[:, low:high], v_ref[:, low:high], q_ref[:, cols], do_ref[:, cols]
        )
        grad_ref[0, :, cols] = grad_q.astype(BF)
        dk_acc[:, low:high] += grad_k
        dv_acc[:, low:high] += grad_v
        for b in range(band(block), block + 1):
            start = b * QB - low
            tile_acc[block - b] += grads[start : start + QB].astype(F32)
    grad_ref[1] = dk_acc[...].astype(BF)
    grad_ref[2] = dv_acc[...].astype(BF)
    spots = lax.broadcasted_iota(jnp.int32, (QB, QB), 0) + lax.broadcasted_iota(jnp.int32, (QB, QB), 1)
    mirror = (spots == QB - 1).astype(F32)
    for d in range(count):
        mirrored = lax.dot_general(
            tile_acc[d], mirror, (((1,), (0,)), ((), ())),
            precision=lax.Precision.HIGHEST, preferred_element_type=F32,
        )
        padded = jnp.concatenate([mirrored, jnp.zeros((QB, QB), F32)], axis=1)
        skewed = pltpu.roll(padded, 0, 1, stride=1, stride_axis=0)
        diag_ref[0, d : d + 1, :] = jnp.sum(skewed, axis=0, keepdims=True)


def cross_bwd_kernel(q_ref, k_ref, v_ref, do_ref, lse_ref, keep_ref, grad_ref, dk_acc, dv_acc):
    dk_acc[...] = jnp.zeros_like(dk_acc)
    dv_acc[...] = jnp.zeros_like(dv_acc)
    for block in range(LEN // QB):
        cols = slice(block * QB, (block + 1) * QB)
        scores = jnp.where(keep_ref[...] > 0.0, dot_tn(k_ref[...], q_ref[:, cols]), NEG_FILL)
        grads, grad_q, grad_k, grad_v = score_grads(
            scores, lse_ref[0, :, cols], k_ref[...], v_ref[...], q_ref[:, cols], do_ref[:, cols]
        )
        grad_ref[0, :, cols] = grad_q.astype(BF)
        dk_acc[...] += grad_k
        dv_acc[...] += grad_v
    grad_ref[1] = dk_acc[...].astype(BF)
    grad_ref[2] = dv_acc[...].astype(BF)


def head_spec(first):
    return pl.BlockSpec((DK, LEN), lambda h: (first + h, 0))


def whole_spec(shape):
    return pl.BlockSpec(shape, lambda h: (0,) * len(shape))


def attn_call(kernel, heads, in_specs, out_specs, out_shape, operands, scratch, flops):
    return pl.pallas_call(
        kernel,
        grid=(heads,),
        in_specs=in_specs,
        out_specs=out_specs,
        out_shape=out_shape,
        scratch_shapes=scratch,
        compiler_params=pltpu.CompilerParams(vmem_limit_bytes=VMEM),
        cost_estimate=pl.CostEstimate(flops=flops, bytes_accessed=4 << 20, transcendentals=heads << 20),
    )(*operands)


def shape_of(*dims, dtype=BF):
    return jax.ShapeDtypeStruct(dims, dtype)


GRAD_SPEC = pl.BlockSpec((3, DK, LEN), lambda h: (0, h, 0))
LSE_SPEC = pl.BlockSpec((1, 1, LEN), lambda h: (h, 0, 0))


def self_forward(qkv, seg_row, seg_col, vec, heads):
    vec_spec = pl.BlockSpec((1, 1, vec.shape[2]), lambda h: (h, 0, 0))
    return attn_call(
        self_fwd_kernel, heads,
        [head_spec(0), head_spec(heads), head_spec(2 * heads), whole_spec((1, LEN)), whole_spec((LEN, 1)), vec_spec],
        [head_spec(0), LSE_SPEC],
        [shape_of(heads * DK, LEN), shape_of(heads, 1, LEN, dtype=F32)],
        (qkv, qkv, qkv, seg_row, seg_col, vec), [], heads * 2 * 2 * DK * LEN * LEN,
    )


def cross_forward(query, keyval, keep, heads):
    return attn_call(
        cross_fwd_kernel, heads,
        [head_spec(0), head_spec(0), head_spec(heads), whole_spec((LEN, 1))],
        [head_spec(0), LSE_SPEC],
        [shape_of(heads * DK, LEN), shape_of(heads, 1, LEN, dtype=F32)],
        (query, keyval, keyval, keep), [], heads * 2 * 2 * DK * LEN * LEN,
    )


def self_backward(qkv, grad_attn, lse, seg_row, seg_col, vec, heads):
    count = LEN // 2 // QB + 1
    vec_spec = pl.BlockSpec((1, 1, vec.shape[2]), lambda h: (h, 0, 0))
    out = shape_of(3, heads * DK, LEN)
    return attn_call(
        self_bwd_kernel, heads,
        [
            head_spec(0), head_spec(heads), head_spec(2 * heads), head_spec(0), LSE_SPEC,
            whole_spec((1, LEN)), whole_spec((LEN, 1)), vec_spec,
        ],
        [GRAD_SPEC, pl.BlockSpec((1, count, 2 * QB), lambda h: (h, 0, 0))],
        [out, shape_of(heads, count, 2 * QB, dtype=F32)],
        (qkv, qkv, qkv, grad_attn, lse, seg_row, seg_col, vec),
        [pltpu.VMEM((DK, LEN), F32), pltpu.VMEM((DK, LEN), F32), pltpu.VMEM((count, QB, QB), F32)],
        heads * 2 * 5 * DK * LEN * LEN,
    )


def cross_backward(query, keyval, grad_attn, lse, keep, heads):
    out = shape_of(3, heads * DK, LEN)
    return attn_call(
        cross_bwd_kernel, heads,
        [head_spec(0), head_spec(0), head_spec(heads), head_spec(0), LSE_SPEC, whole_spec((LEN, 1))],
        [GRAD_SPEC],
        [out],
        (query, keyval, keyval, grad_attn, lse, keep),
        [pltpu.VMEM((DK, LEN), F32), pltpu.VMEM((DK, LEN), F32)],
        heads * 2 * 5 * DK * LEN * LEN,
    )


def owner_copies(refs, owners_ref, target, sems, inward):
    copies = []
    slot = 0
    for ref in refs:
        for j in range(ref.shape[0]):
            owner = owners_ref[slot]
            here = target.at[:, owner]
            pair = (ref.at[j], here) if inward else (here, ref.at[j])
            copies.append(pltpu.make_async_copy(*pair, sems.at[slot]))
            slot += 1
    return copies


def ffn_kernel(by_owner, first, last, *refs):
    owners_ref, x_hbm, og_hbm, weight_hbm = refs[:4]
    refs = refs[4:]
    acc_refs, refs = ((), refs) if first else (refs[:2], refs[2:])
    out_refs, refs = refs[:2], refs[2:]
    grad_refs, refs = refs[:by_owner], refs[by_owner:]
    x_ref, og_ref, out_acc, back_acc, weights, grads, x_sems, in_sems, out_sems, acc_sems = refs[:10]
    unused, count, block, width = weights.shape
    rows = count * block
    inputs = [
        pltpu.make_async_copy(src, dst, x_sems.at[i])
        for i, (src, dst) in enumerate(((x_hbm, x_ref), (og_hbm, og_ref)))
    ]
    loads = [pltpu.make_async_copy(weight_hbm.at[:, c], weights.at[c], in_sems.at[c]) for c in range(3)]
    accs = [
        pltpu.make_async_copy(src, dst, acc_sems.at[i])
        for i, (src, dst) in enumerate(zip(acc_refs, (out_acc, back_acc)))
    ]
    for copy in (inputs[0], *loads, inputs[1], *accs):
        copy.start()
    inputs[0].wait()
    loads[0].wait()
    normed = x_ref[...]
    slope = 0.7978845608028654
    stores = []
    for step in range(-(-width // FC)):
        cols = slice(step * FC, min((step + 1) * FC, width))
        units = cols.stop - cols.start
        w_gate = weights[0, :, :, cols].reshape(rows, units)
        gate = dot_tn(w_gate, normed)
        square = gate * gate
        tanh = jnp.tanh(slope * gate * (1.0 + 0.044715 * square))
        half = 0.5 * (1.0 + tanh)
        act = gate * half
        act_grad = half + 0.5 * gate * (1.0 - tanh * tanh) * (slope * (1.0 + 0.134145 * square))
        if step == 0:
            loads[1].wait()
        w_up = weights[1, :, :, cols].reshape(rows, units)
        upward = dot_tn(w_up, normed)
        hidden = (act * upward).astype(BF)
        if step == 0:
            loads[2].wait()
            inputs[1].wait()
        w_down = weights[2, :, :, cols].reshape(rows, units)
        out_grad = og_ref[...]
        grad_hidden = dot_tn(w_down, out_grad)
        grad_gate = (grad_hidden * upward * act_grad).astype(BF)
        grad_up = (grad_hidden * act).astype(BF)
        if step == 0:
            for copy in accs:
                copy.wait()
        back = dot_nn(w_gate, grad_gate) + dot_nn(w_up, grad_up)
        out = dot_nn(w_down, hidden)
        if step > 0 or not first:
            back = back_acc[...] + back
            out = out_acc[...] + out
        final = cols.stop == width
        if final and last:
            out_low, back_low = refs[10:]
            back_low[...] = back.astype(BF)
            out_low[...] = out.astype(BF)
            sources = (out_low, back_low)
        else:
            back_acc[...] = back
            out_acc[...] = out
            sources = (out_acc, back_acc)
        if final:
            stores = [pltpu.make_async_copy(src, dst, acc_sems.at[i]) for i, (src, dst) in enumerate(zip(sources, out_refs))]
            for copy in stores:
                copy.start()
        shape = (count, block, units)
        grads[0, :, :, cols] = dot_nt(normed, grad_gate).astype(BF).reshape(shape)
        grads[1, :, :, cols] = dot_nt(normed, grad_up).astype(BF).reshape(shape)
        grads[2, :, :, cols] = dot_nt(out_grad, hidden).astype(BF).reshape(shape)
    if by_owner == 1:
        sends = [pltpu.make_async_copy(grads.at[c], grad_refs[0].at[:, c], out_sems.at[c]) for c in range(3)]
    else:
        sends = owner_copies(grad_refs, owners_ref, grads, out_sems, False)
    for copy in sends:
        copy.start()
    for copy in stores + sends:
        copy.wait()


SMEM_SPEC = pl.BlockSpec(memory_space=pltpu.SMEM)
VMEM_SPEC = pl.BlockSpec(memory_space=pltpu.VMEM)
ANY_SPEC = pl.BlockSpec(memory_space=pl.ANY)


def feed_forward(owners, normed, out_grad, weights, sums, by_owner, last):
    count, unused, block, width = weights.shape
    rows, tokens = normed.shape
    first = sums is None
    kind = BF if last else F32
    total = shape_of(rows, tokens, dtype=kind)
    sizes = block_sizes(count) if by_owner else [count]
    results = pl.pallas_call(
        functools.partial(ffn_kernel, len(sizes), first, last),
        in_specs=[SMEM_SPEC] + [ANY_SPEC] * (3 if first else 5),
        out_specs=[ANY_SPEC] * (2 + len(sizes)),
        out_shape=[total, total] + [shape_of(size, 3, block, width) for size in sizes],
        input_output_aliases={} if first or last else {4: 0, 5: 1},
        scratch_shapes=[
            pltpu.VMEM((rows, tokens), BF),
            pltpu.VMEM((rows, tokens), BF),
            pltpu.VMEM((rows, tokens), F32),
            pltpu.VMEM((rows, tokens), F32),
            pltpu.VMEM((3, count, block, width), BF),
            pltpu.VMEM((3, count, block, width), BF),
            pltpu.SemaphoreType.DMA((2,)),
            pltpu.SemaphoreType.DMA((3,)),
            pltpu.SemaphoreType.DMA((count,)),
            pltpu.SemaphoreType.DMA((2,)),
        ]
        + [pltpu.VMEM((rows, tokens), BF)] * (2 if last else 0),
        compiler_params=pltpu.CompilerParams(vmem_limit_bytes=VMEM),
        cost_estimate=pl.CostEstimate(
            flops=9 * 2 * rows * width * tokens, bytes_accessed=32 << 20, transcendentals=width * tokens
        ),
    )(owners, normed, out_grad, weights, *(() if first else sums))
    return results[:2], list(results[2:])


def block_sizes(count):
    return [2] * 8 if count == 16 else [count]


def place_kernel(parts, inward, owners_ref, *refs):
    sems = refs[-1]
    if inward:
        copies = owner_copies(refs[:parts], owners_ref, refs[parts], sems, True)
    else:
        copies = owner_copies(refs[1 : 1 + parts], owners_ref, refs[0], sems, False)
    for copy in copies:
        copy.start()
    for copy in copies:
        copy.wait()


def place_blocks(owners, blocks):
    count = owners.shape[0]
    return pl.pallas_call(
        functools.partial(place_kernel, len(blocks), True),
        in_specs=[SMEM_SPEC] + [ANY_SPEC] * len(blocks),
        out_specs=VMEM_SPEC,
        out_shape=shape_of(1, count, *blocks[0].shape[2:]),
        scratch_shapes=[pltpu.SemaphoreType.DMA((count,))],
        compiler_params=pltpu.CompilerParams(vmem_limit_bytes=VMEM),
    )(owners, *blocks)[0]


def split_blocks(owners, value):
    count = owners.shape[0]
    sizes = block_sizes(count)
    return list(
        pl.pallas_call(
            functools.partial(place_kernel, len(sizes), False),
            in_specs=[SMEM_SPEC, VMEM_SPEC],
            out_specs=[ANY_SPEC] * len(sizes),
            out_shape=[shape_of(size, 1, *value.shape[1:]) for size in sizes],
            scratch_shapes=[pltpu.SemaphoreType.DMA((count,))],
            compiler_params=pltpu.CompilerParams(vmem_limit_bytes=VMEM),
        )(owners, value[None])
    )


def merge_kernel(own_map, other_map, own_ref, other_ref, out_ref):
    rows = own_ref.shape[-1]
    here = dot_nn(own_map[...], own_ref[...].reshape(-1, rows))
    there = dot_nn(other_map[...], other_ref[...].reshape(-1, rows))
    out_ref[0] = (here + there).astype(BF)


def merge_cores(own_map, other_map, own, other):
    count, maps, share, rows = own.shape
    height = own_map.shape[0]
    whole = pl.BlockSpec(own_map.shape, lambda c: (0, 0))
    part = pl.BlockSpec((count, 1, share, rows), lambda c: (0, c, 0, 0))
    return pl.pallas_call(
        merge_kernel,
        grid=(maps,),
        in_specs=[whole, whole, part, part],
        out_specs=pl.BlockSpec((1, height, rows), lambda c: (c, 0, 0)),
        out_shape=shape_of(maps, height, rows),
        compiler_params=pltpu.CompilerParams(vmem_limit_bytes=VMEM),
        cost_estimate=pl.CostEstimate(flops=4 * maps * height * count * share * rows, bytes_accessed=12 << 20, transcendentals=0),
    )(own_map, other_map, own, other)


def cross_grad_kernel(parts, owners_ref, own_map, other_map, own_ref, other_ref, attn_own, attn_other, x_ref, mem_ref, g_ref, *refs):
    grads, sems = refs[parts:]
    unused, count, maps, share, rows = grads.shape
    pairs = [(own_ref[c], other_ref[c]) for c in range(3)] + [(attn_own[...], attn_other[...])]
    for c, (own, other) in enumerate(pairs):
        picked = (dot_tn(own_map[...], own) + dot_tn(other_map[...], other)).astype(BF)
        wide = (x_ref, mem_ref, mem_ref, g_ref)[c][...]
        grads[0, :, c] = dot_nt(picked, wide).astype(BF).reshape(count, share, rows)
    copies = owner_copies(refs[:parts], owners_ref, grads, sems, False)
    for copy in copies:
        copy.start()
    for copy in copies:
        copy.wait()


def cross_weight_grads(owners, own_map, other_map, own, other, attn_own, attn_other, normed, memory, grad, share):
    count = owners.shape[0]
    sizes = block_sizes(count)
    rows, tokens = normed.shape
    return list(
        pl.pallas_call(
            functools.partial(cross_grad_kernel, len(sizes)),
            in_specs=[SMEM_SPEC] + [VMEM_SPEC] * 9,
            out_specs=[ANY_SPEC] * len(sizes),
            out_shape=[shape_of(size, 1, 4, share, rows) for size in sizes],
            scratch_shapes=[pltpu.VMEM((1, count, 4, share, rows), BF), pltpu.SemaphoreType.DMA((count,))],
            compiler_params=pltpu.CompilerParams(vmem_limit_bytes=VMEM),
            cost_estimate=pl.CostEstimate(flops=8 * count * share * rows * tokens, bytes_accessed=16 << 20, transcendentals=0),
        )(owners, own_map, other_map, own, other, attn_own, attn_other, normed, memory, grad)
    )


def self_grad_kernel(parts, owners_ref, x_ref, qkv_ref, g_ref, attn_ref, *refs):
    grads, sems = refs[parts:]
    unused, count, block, width = grads.shape
    first = dot_nt(x_ref[...], qkv_ref[...].reshape(-1, x_ref.shape[1]))
    second = dot_nt(g_ref[...], attn_ref[...])
    grads[0] = jnp.concatenate([first, second], axis=1).astype(BF).reshape(count, block, width)
    copies = owner_copies(refs[:parts], owners_ref, grads, sems, False)
    for copy in copies:
        copy.start()
    for copy in copies:
        copy.wait()


def self_weight_grads(owners, normed, grad_qkv, grad, attn):
    count = owners.shape[0]
    sizes = block_sizes(count)
    rows, tokens = normed.shape
    width = 4 * attn.shape[0]
    return list(
        pl.pallas_call(
            functools.partial(self_grad_kernel, len(sizes)),
            in_specs=[SMEM_SPEC] + [VMEM_SPEC] * 4,
            out_specs=[ANY_SPEC] * len(sizes),
            out_shape=[shape_of(size, 1, rows // count, width) for size in sizes],
            scratch_shapes=[pltpu.VMEM((1, count, rows // count, width), BF), pltpu.SemaphoreType.DMA((count,))],
            compiler_params=pltpu.CompilerParams(vmem_limit_bytes=VMEM),
            cost_estimate=pl.CostEstimate(flops=2 * rows * width * tokens, bytes_accessed=12 << 20, transcendentals=0),
        )(owners, normed, grad_qkv, grad, attn)
    )


def squeeze_rows(value, block, pad):
    return jnp.concatenate([value[i : i + block] for i in range(0, value.shape[0], pad)], axis=0)


def spread_kernel(block, pad, in_ref, out_ref):
    value = in_ref[...].astype(F32)
    gap = jnp.zeros((pad - block, value.shape[1]), F32)
    parts = []
    for i in range(0, value.shape[0], block):
        parts += [value[i : i + block], gap]
    out_ref[...] = jnp.concatenate(parts, axis=0).astype(BF)


def spread_rows(value, block, pad):
    height, tokens = value.shape
    rows = height // block * pad
    return pl.pallas_call(
        functools.partial(spread_kernel, block, pad),
        grid=(tokens // QB,),
        in_specs=[pl.BlockSpec((height, QB), lambda j: (0, j))],
        out_specs=pl.BlockSpec((rows, QB), lambda j: (0, j)),
        out_shape=shape_of(rows, tokens),
        compiler_params=pltpu.CompilerParams(vmem_limit_bytes=VMEM),
        cost_estimate=pl.CostEstimate(flops=rows * tokens, bytes_accessed=4 * rows * tokens, transcendentals=0),
    )(value)


def out_kernel(block, pad, resid_ref, own_ref, other_ref, out_ref):
    total = resid_ref[...] + (own_ref[...].astype(F32) + other_ref[...].astype(F32))
    out_ref[...] = squeeze_rows(total, block, pad).astype(BF)


def layer_output(resid, own, other, block, pad):
    rows, tokens = resid.shape
    part = pl.BlockSpec((rows, QB), lambda j: (0, j))
    return pl.pallas_call(
        functools.partial(out_kernel, block, pad),
        grid=(tokens // QB,),
        in_specs=[part, part, part],
        out_specs=pl.BlockSpec((rows // pad * block, QB), lambda j: (0, j)),
        out_shape=shape_of(rows // pad * block, tokens),
        compiler_params=pltpu.CompilerParams(vmem_limit_bytes=VMEM),
        cost_estimate=pl.CostEstimate(flops=4 * rows * tokens, bytes_accessed=10 * rows * tokens, transcendentals=0),
    )(resid, own, other)


def memory_kernel(block, pad, key_map, value_map, kv_ref, out_ref):
    total = dot_tn(key_map[0], kv_ref[0]) + dot_tn(value_map[0], kv_ref[1])
    out_ref[...] = squeeze_rows(total, block, pad)


def memory_gradient(maps, grad_kv, block, pad):
    unused, inner, rows = maps.shape
    enc = grad_kv.shape[2]
    return pl.pallas_call(
        functools.partial(memory_kernel, block, pad),
        grid=(enc // QB,),
        in_specs=[
            pl.BlockSpec((1, inner, rows), lambda j: (1, 0, 0)),
            pl.BlockSpec((1, inner, rows), lambda j: (2, 0, 0)),
            pl.BlockSpec((2, inner, QB), lambda j: (0, 0, j)),
        ],
        out_specs=pl.BlockSpec((rows // pad * block, QB), lambda j: (0, j)),
        out_shape=shape_of(rows // pad * block, enc, dtype=F32),
        compiler_params=pltpu.CompilerParams(vmem_limit_bytes=VMEM),
        cost_estimate=pl.CostEstimate(flops=4 * inner * rows * enc, bytes_accessed=8 << 20, transcendentals=0),
    )(maps, maps, grad_kv)


def norm_back_kernel(upstream, squeeze, n_ups, *refs):
    values_ref, inv_ref, gain_ref, base_ref = refs[:4]
    outs = refs[4 + n_ups :]
    up = upstream(*refs[4 : 4 + n_ups])
    values = values_ref[...].astype(F32)
    inv_root = inv_ref[...]
    scaled = up * gain_ref[...]
    along = jnp.sum(values * scaled, axis=0, keepdims=True) * (inv_root * inv_root * (1.0 / D))
    total = base_ref[...].astype(F32) + inv_root * (scaled - values * along)
    outs[0][...] = squeeze_rows(total, *squeeze) if squeeze else total.astype(BF)
    gain_part = jnp.sum(up * (values * inv_root), axis=1, keepdims=True)

    @pl.when(pl.program_id(0) == 0)
    def start():
        outs[1][...] = gain_part

    @pl.when(pl.program_id(0) > 0)
    def add():
        outs[1][...] += gain_part


def norm_back(values, inv_root, gain, base, upstream, ups, fixed, squeeze=None, flops=0):
    rows, tokens = values.shape
    part = pl.BlockSpec((rows, QB), lambda j: (0, j))

    def spec(array, whole):
        if whole is None:
            return pl.BlockSpec((1,) + array.shape[1:], lambda j: (0,) * array.ndim)
        if whole:
            return pl.BlockSpec(array.shape, lambda j: (0,) * array.ndim)
        return pl.BlockSpec(array.shape[:-1] + (QB,), lambda j: (0,) * (array.ndim - 1) + (j,))

    column = pl.BlockSpec((rows, 1), lambda j: (0, 0))
    height = rows // squeeze[1] * squeeze[0] if squeeze else rows
    return pl.pallas_call(
        functools.partial(norm_back_kernel, upstream, squeeze, len(ups)),
        grid=(tokens // QB,),
        in_specs=[part, pl.BlockSpec((1, QB), lambda j: (0, j)), column, part]
        + [spec(a, w) for a, w in zip(ups, fixed)],
        out_specs=[pl.BlockSpec((height, QB), lambda j: (0, j)), column],
        out_shape=[shape_of(height, tokens, dtype=F32 if squeeze else BF), shape_of(rows, 1, dtype=F32)],
        compiler_params=pltpu.CompilerParams(vmem_limit_bytes=VMEM),
        cost_estimate=pl.CostEstimate(flops=flops + 12 * rows * tokens, bytes_accessed=20 * rows * tokens, transcendentals=0),
    )(values, inv_root, gain, base, *ups)


def rotated(value, step):
    return lax.ppermute(value, "tok", [(t, (t // 4 + step) % 4 * 4 + t % 4) for t in range(16)])


def flipped(value, bits):
    return lax.ppermute(value, "tok", [(t, t ^ bits) for t in range(16)])


def block_owners():
    count = lax.axis_size("tok")
    index = lax.axis_index("tok")
    if count != 16:
        return jnp.arange(count, dtype=jnp.int32)
    owners = [(index // 4 + 4 - k) % 4 * 4 + (index % 4 ^ bits) for bits in range(4) for k in range(4)]
    return jnp.stack(owners).astype(jnp.int32)


class Transfer:
    def __init__(self, steps):
        self.steps = steps
        self.value = None
        self.flying = None

    @property
    def done(self):
        return self.value is not None

    def resume(self, arrived):
        try:
            return next(self.steps) if self.flying is None else self.steps.send(arrived)
        except StopIteration as stop:
            self.value = stop.value
            return []

    def launch(self, sends):
        self.flying = [move(operand, *way) for operand, move, way in sends]

    def finish(self):
        while not self.done:
            self.launch(self.resume(self.flying))
        return self.value


def tick(state, *transfers):
    moving = [t for t in transfers if not t.done]
    state, arrived = lax.optimization_barrier((state, [t.flying or [] for t in moving]))
    sends = [t.resume(a) for t, a in zip(moving, arrived)]
    operands = [[send[0] for send in group] for group in sends]
    state, operands = lax.optimization_barrier((state, operands))
    for t, group, ready in zip(moving, sends, operands):
        t.launch([(value, *send[1:]) for value, send in zip(ready, group)])
    return state


def gather_steps(value):
    if lax.axis_size("tok") != 16:
        return [lax.all_gather(value, "tok", axis=0, tiled=False)]
    far = yield [(value, rotated, (k,)) for k in (1, 2, 3)]
    low, high = jnp.stack([value, far[0]]), jnp.stack(far[1:])
    x_low, x_high, y_low, y_high = yield [
        (low, flipped, (1,)), (high, flipped, (1,)), (low, flipped, (2,)), (high, flipped, (2,))
    ]
    d_low, d_high = yield [(y_low, flipped, (1,)), (x_high, flipped, (2,))]
    return [low, high, x_low, x_high, y_low, y_high, d_low, d_high]


def low_sum(*terms):
    return sum(term.astype(F32) for term in terms).astype(BF)


def scatter_steps(blocks, wide=False):
    if len(blocks) == 1:
        return lax.psum_scatter(blocks[0], "tok", scatter_dimension=0, tiled=False).astype(F32)
    m_low, m_high, x_low, x_high, y_low, y_high, d_low, d_high = blocks
    if wide:
        to_y, to_x = yield [(d_low, flipped, (1,)), (d_high, flipped, (2,))]
        x_first, y_second = yield [(x_low, flipped, (1,)), (y_high, flipped, (2,))]
    else:
        to_y, to_x, x_first, y_second = yield [
            (d_low, flipped, (1,)), (d_high, flipped, (2,)), (x_low, flipped, (1,)), (y_high, flipped, (2,))
        ]
    x_second, y_first = yield [
        (low_sum(x_high, to_x), flipped, (1,)), (low_sum(y_low, to_y), flipped, (2,))
    ]
    held = [
        low_sum(mine[k], gx[k], gy[k])
        for mine, gx, gy in ((m_low, x_first, y_first), (m_high, x_second, y_second))
        for k in range(2)
    ]
    far = yield [(held[k], rotated, (4 - k,)) for k in (1, 2, 3)]
    return sum(term.astype(F32) for term in (held[0], *far))


def sum_all(value):
    if lax.axis_size("tok") != 16:
        return lax.psum(value, ("tok", "mem"))
    value = value + other_core(value)
    value = (value + flipped(value, 1)) + (flipped(value, 2) + flipped(value, 3))
    return (value + rotated(value, 2)) + (rotated(value, 1) + rotated(value, 3))


def norm_stats(values):
    return lax.rsqrt(jnp.sum(values * values, axis=0, keepdims=True) * (1.0 / D) + EPS_NORM)


def adam_step(weight, first_mom, second_mom, gradient, clip_scale, step_rate, decay_rate):
    clipped = gradient * clip_scale
    first_new = BETA_FIRST * first_mom + (1.0 - BETA_FIRST) * clipped
    second_new = BETA_SECOND * second_mom + (1.0 - BETA_SECOND) * clipped * clipped
    first_hat = first_new / (1.0 - BETA_FIRST**STEP)
    second_hat = second_new / (1.0 - BETA_SECOND**STEP)
    weight_new = weight - step_rate * (
        first_hat / (jnp.sqrt(second_hat) + ADAM_EPS) + decay_rate * weight
    )
    return (weight_new, first_new, second_new)


def other_core(value):
    return lax.ppermute(value, "mem", [(0, 1), (1, 0)])


def core_pair(value, mem_index):
    other = other_core(value)
    return jnp.where(mem_index == 0, value, other), jnp.where(mem_index == 0, other, value)


def chunk_sizes(width):
    if lax.axis_size("tok") != 16:
        return [FC] * (width // FC)
    return [5 * FC + FC // 2, width - 5 * FC - FC // 2]


def shards(
    inputs,
    memory,
    kept_mask,
    segment_ids,
    bucket_ids,
    out_grad,
    self_weights,
    self_first,
    self_second,
    cross_weights,
    cross_first,
    cross_second,
    ffn_weights,
    ffn_first,
    ffn_second,
    norm_gains,
    gains_first,
    gains_second,
    rel_bias,
    rel_first,
    rel_second,
):
    count = lax.axis_size("tok")
    mem_index = lax.axis_index("mem")
    heads = rel_bias.shape[0]
    own = heads * DK
    block = norm_gains.shape[1]
    pad = -(-block // 16) * 16
    rows = count * pad
    share = cross_weights.shape[1]
    enc = memory.shape[1]

    def widen(value, axis):
        shape = value.shape
        split = value.reshape(shape[:axis] + (shape[axis] // block, block) + shape[axis + 1 :])
        pads = [(0, 0)] * split.ndim
        pads[axis + 1] = (0, pad - block)
        return jnp.pad(split, pads).reshape(shape[:axis] + (-1,) + shape[axis + 1 :])

    def narrow(value, axis):
        shape = value.shape
        split = value.reshape(shape[:axis] + (shape[axis] // pad, pad) + shape[axis + 1 :])
        kept = lax.slice_in_dim(split, 0, block, axis=axis + 1)
        return kept.reshape(shape[:axis] + (-1,) + shape[axis + 1 :])

    owners = block_owners()
    self_wire = widen(jnp.transpose(self_weights, (2, 0, 1)).astype(BF).reshape(block, 4 * own), 0)
    share_pad = -(-share // 16) * 16
    self_wire = self_wire.at[block : block + 3, :block].set(norm_gains.astype(BF))
    self_w = Transfer(gather_steps(self_wire[None]))
    tick((), self_w)
    ffn_wire = widen(jnp.transpose(ffn_weights, (0, 2, 1)).astype(BF), 1)
    ffn_w = []
    start = 0
    for size in chunk_sizes(ffn_wire.shape[2]):
        ffn_w.append(lax.all_gather(ffn_wire[:, :, start : start + size], "tok", axis=0, tiled=False))
        start += size
    cross_wire = jnp.pad(widen(cross_weights.astype(BF), 2), ((0, 0), (0, share_pad - share), (0, 0)))[None]
    cross_w = Transfer(gather_steps(cross_wire))

    x_low = spread_rows(inputs.T, block, pad)
    x_low = tick(x_low, self_w, cross_w)
    resid_zero = x_low.astype(F32)
    inv_one = norm_stats(resid_zero)
    og_low = spread_rows(out_grad.T, block, pad)
    og_low, inv_one = tick((og_low, inv_one), self_w, cross_w)
    mem_own = spread_rows(memory.reshape(enc, D).T, block, pad)
    mem_parts = core_pair(mem_own, mem_index)
    mem_full = jnp.concatenate(mem_parts, axis=1)
    kept_parts = core_pair(kept_mask.reshape(enc), mem_index)
    keep = (jnp.concatenate(kept_parts) > 0).astype(F32).reshape(LEN, 1)
    seg_row = segment_ids.reshape(1, LEN)
    seg_col = segment_ids.reshape(LEN, 1)
    bucket_hot = (bucket_ids[None, :] == jnp.arange(NB, dtype=jnp.int32)[:, None]).astype(F32)
    bias_vec = jnp.dot(rel_bias, bucket_hot, precision=lax.Precision.HIGHEST)
    vec = jnp.pad(bias_vec, ((0, 0), (QB, 0))).reshape(heads, 1, QB + LEN)
    far_ids = jnp.pad(bucket_ids, (QB, 0), constant_values=-1)
    diag_ids = jnp.concatenate([far_ids[d * QB : (d + 2) * QB][::-1] for d in range(LEN // 2 // QB + 1)])
    diag_hot = (diag_ids[:, None] == jnp.arange(NB, dtype=jnp.int32)[None, :]).astype(F32)
    mem_full, inv_one, vec, keep, diag_hot = tick((mem_full, inv_one, vec, keep, diag_hot), self_w)

    self_blocks = place_blocks(owners, self_w.finish())
    gain_blocks = self_blocks[:, block : block + 3, :block]
    gain_rows = widen(jnp.transpose(gain_blocks, (1, 0, 2)).reshape(3, -1), 1).astype(F32)
    gains = lax.optimization_barrier([gain_rows[c].reshape(rows, 1) for c in range(3)])
    self_own = self_blocks.reshape(rows, 4 * own)
    self_low, self_high = core_pair(self_own, mem_index)
    normed_one = (resid_zero * inv_one * gains[0]).astype(BF)
    qkv = dot_tn(self_own[:, : 3 * own], normed_one).astype(BF)
    qkv = tick(qkv, cross_w)
    attn_self, lse_self = self_forward(qkv, seg_row, seg_col, vec, heads)
    attn_self = tick(attn_self, cross_w)
    attn_low, attn_high = core_pair(attn_self, mem_index)
    resid_one = resid_zero + (
        dot_nn(self_low[:, 3 * own :], attn_low) + dot_nn(self_high[:, 3 * own :], attn_high)
    )

    inv_two = norm_stats(resid_one)
    normed_two = (resid_one * inv_two * gains[1]).astype(BF)
    cross_blocks = place_blocks(owners, cross_w.finish())
    place = jnp.arange(INNER, dtype=jnp.int32)[:, None]
    spot = jnp.arange(count * share_pad, dtype=jnp.int32)[None, :]
    match = (place // (2 * share) == spot // share_pad) & (place % share == spot % share_pad)
    core_of = place // share % 2
    own_map = (match & (core_of == mem_index)).astype(BF)
    other_map = (match & (core_of != mem_index)).astype(BF)
    cross_full = merge_cores(own_map, other_map, cross_blocks, other_core(cross_blocks))
    cross_own = lax.dynamic_slice_in_dim(cross_full, mem_index * own, own, 1)
    keyval = dot_nn(cross_own[1:3].reshape(2 * own, rows), mem_full).astype(BF)
    query = dot_nn(cross_own[0], normed_two).astype(BF)
    attn_cross, lse_cross = cross_forward(query, keyval, keep, heads)
    attn_cross_other = other_core(attn_cross)
    attn_cross_full = jnp.concatenate(
        [jnp.where(mem_index == 0, attn_cross, attn_cross_other), jnp.where(mem_index == 0, attn_cross_other, attn_cross)]
    )
    resid_two = resid_one + dot_tn(cross_full[3], attn_cross_full)

    inv_three = norm_stats(resid_two)
    normed_three = (resid_two * inv_three * gains[2]).astype(BF)
    sums = None
    ffn_g = []
    for i, weights in enumerate(ffn_w):
        last = i == len(ffn_w) - 1
        sums, grads = feed_forward(owners, normed_three, og_low, weights, sums, last and count == 16, last)
        ffn_g.append(Transfer(scatter_steps(grads, True)))
        if not last:
            sums = tick(sums, ffn_g[i])
    out_low, back_low = sums
    back_other = other_core(back_low)
    back_low, back_other = tick((back_low, back_other), ffn_g[-1])
    grad_two_low, gain_three = norm_back(
        resid_two, inv_three, gains[2], og_low,
        lambda own, other: own[...].astype(F32) + other[...].astype(F32), (back_low, back_other), (False, False),
    )

    grad_two_low = tick(grad_two_low, ffn_g[-1])
    grad_cattn = dot_nn(cross_own[3], grad_two_low).astype(BF)
    (cross_d,) = cross_backward(query, keyval, grad_cattn, lse_cross, keep, heads)
    cross_d = tick(cross_d, ffn_g[-1])
    cross_d_other = other_core(cross_d)
    grad_q_full = jnp.concatenate(
        [jnp.where(mem_index == 0, cross_d[0], cross_d_other[0]), jnp.where(mem_index == 0, cross_d_other[0], cross_d[0])]
    )
    grad_one_low, gain_two = norm_back(
        resid_one, inv_two, gains[1], grad_two_low,
        lambda w, g: dot_tn(w[0], g[...]), (cross_full, grad_q_full), (None, False), flops=2 * INNER * rows * LEN,
    )

    grad_one_low, cross_d, cross_d_other = tick((grad_one_low, cross_d, cross_d_other), ffn_g[-1])
    other_half = lax.dynamic_slice_in_dim(own_map, (1 - mem_index) * own, own, 0)
    own_half = lax.dynamic_slice_in_dim(own_map, mem_index * own, own, 0)
    cross_g = Transfer(
        scatter_steps(
            cross_weight_grads(
                owners, own_half, other_half, cross_d, cross_d_other, attn_cross, attn_cross_other,
                normed_two, mem_full, grad_two_low, share_pad,
            )
        )
    )
    grad_sattn = dot_tn(self_own[:, 3 * own :], grad_one_low).astype(BF)
    grad_sattn = tick(grad_sattn, ffn_g[-1], cross_g)

    grad_qkv, diag = self_backward(qkv, grad_sattn, lse_self, seg_row, seg_col, vec, heads)
    grad_qkv = tick(grad_qkv, cross_g)
    self_g = Transfer(scatter_steps(self_weight_grads(owners, normed_one, grad_qkv, grad_one_low, attn_self)))
    grad_qkv, grad_other, out_low = tick((grad_qkv, other_core(grad_qkv), out_low), cross_g, self_g)

    qkv_low = jnp.where(mem_index == 0, grad_qkv, grad_other).reshape(3 * own, LEN)
    qkv_high = jnp.where(mem_index == 0, grad_other, grad_qkv).reshape(3 * own, LEN)
    input_grad, gain_one = norm_back(
        x_low, inv_one, gains[0], grad_one_low,
        lambda a, b, c, d: dot_nn(a[:, : 3 * own], c[...]) + dot_nn(b[:, : 3 * own], d[...]),
        (self_low, self_high, qkv_low, qkv_high), (True, True, False, False), (block, pad), 12 * own * rows * LEN,
    )
    input_grad, gain_one, out_low, cross_d, cross_d_other, diag = tick(
        (input_grad.T, gain_one, out_low, cross_d, cross_d_other, diag), self_g
    )
    out_other = other_core(out_low)
    kv_own = lax.dynamic_slice_in_dim(cross_d[1:], mem_index * enc, enc, 2)
    kv_other = lax.dynamic_slice_in_dim(cross_d_other[1:], mem_index * enc, enc, 2)
    kv_all = jnp.concatenate(
        [jnp.where(mem_index == 0, kv_own, kv_other), jnp.where(mem_index == 0, kv_other, kv_own)], axis=1
    )
    memory_grad = memory_gradient(cross_full, kv_all, block, pad).T.reshape(1, enc, D)
    memory_grad, out_low, out_other, diag = tick((memory_grad, out_low, out_other, diag), cross_g, self_g)
    layer_out = layer_output(resid_two, out_low, out_other, block, pad).T
    rel_grad = jnp.dot(diag.reshape(heads, -1), diag_hot, precision=lax.Precision.HIGHEST)
    layer_out, rel_grad = tick((layer_out, rel_grad), self_g, cross_g)
    ffn_sums = [t.finish() for t in ffn_g]
    cross_sum = cross_g.finish()[0, :, :share]
    self_sum = self_g.finish()[0, :block]

    self_grads = self_sum.reshape(block, 4, own).transpose(1, 2, 0)
    ffn_grads = jnp.concatenate(ffn_sums, axis=2)[:, :block].transpose(0, 2, 1)
    cross_grads = narrow(cross_sum, 2)
    local_squares = (
        jnp.sum(jnp.square(self_sum), keepdims=True)
        + sum(jnp.sum(jnp.square(part), keepdims=True)[0] for part in ffn_sums[::-1])
        + jnp.sum(jnp.square(cross_sum), keepdims=True)[0]
    )
    self_grads, cross_grads, local_squares = lax.optimization_barrier((self_grads, cross_grads, local_squares))
    gain_lines = 3 * rows // 128
    gain_grad = jnp.where(mem_index == 0, jnp.concatenate([gain_one, gain_two, gain_three], axis=1).T, 0.0)
    rel_padded = lax.dynamic_update_slice_in_dim(
        jnp.zeros((8, 128), F32), jnp.pad(rel_grad, ((0, 0), (0, 128 - NB))), mem_index * heads, 0
    )
    totals = sum_all(
        jnp.concatenate([gain_grad.reshape(gain_lines, 128), rel_padded.at[H : H + 1, :1].set(local_squares)])
    )
    gains_total, rel_total = totals[:gain_lines].reshape(3, rows), totals[gain_lines : gain_lines + H, :NB]
    gains_sum = lax.dynamic_slice_in_dim(gains_total, lax.axis_index("tok") * pad, pad, 1)[:, :block]
    total_squares = totals[gain_lines + H : gain_lines + H + 1, :1] + jnp.sum(gains_total * gains_total, keepdims=True)
    grad_norm = jnp.sqrt(total_squares + jnp.sum(rel_total * rel_total, keepdims=True))
    rel_g = lax.dynamic_slice_in_dim(rel_total, mem_index * heads, heads, 0)
    clip_scale = CLIP_NORM / jnp.maximum(grad_norm, CLIP_NORM)
    self_new = adam_step(self_weights, self_first, self_second, self_grads, clip_scale, RATE_MATRIX, DECAY_MATRIX)
    cross_new = adam_step(cross_weights, cross_first, cross_second, cross_grads, clip_scale, RATE_MATRIX, DECAY_MATRIX)
    ffn_new = adam_step(ffn_weights, ffn_first, ffn_second, ffn_grads, clip_scale, RATE_MATRIX, DECAY_MATRIX)
    gains_new = adam_step(norm_gains, gains_first, gains_second, gains_sum, clip_scale, RATE_SMALL, 0.0)
    rel_new = adam_step(rel_bias, rel_first, rel_second, rel_g, clip_scale, RATE_SMALL, 0.0)
    return (
        layer_out,
        input_grad,
        memory_grad,
        grad_norm.reshape(()),
        *self_new,
        *cross_new,
        *ffn_new,
        *gains_new,
        *rel_new,
    )


def solution(mesh):
    placed = (
        P("tok", None),
        P("tok", "mem", None),
        P("tok", "mem"),
        P("tok"),
        P(),
        P("tok", None),
        P(None, "mem", "tok"),
        P(None, "mem", "tok"),
        P(None, "mem", "tok"),
        P(None, ("tok", "mem"), None),
        P(None, ("tok", "mem"), None),
        P(None, ("tok", "mem"), None),
        P(None, "mem", "tok"),
        P(None, "mem", "tok"),
        P(None, "mem", "tok"),
        P(None, "tok"),
        P(None, "tok"),
        P(None, "tok"),
        P("mem", None),
        P("mem", None),
        P("mem", None),
    )
    return jax.shard_map(
        shards,
        mesh=mesh,
        in_specs=placed,
        out_specs=(
            P("tok", None),
            P("tok", None),
            P("tok", "mem", None),
            P(),
            P(None, "mem", "tok"),
            P(None, "mem", "tok"),
            P(None, "mem", "tok"),
            P(None, ("tok", "mem"), None),
            P(None, ("tok", "mem"), None),
            P(None, ("tok", "mem"), None),
            P(None, "mem", "tok"),
            P(None, "mem", "tok"),
            P(None, "mem", "tok"),
            P(None, "tok"),
            P(None, "tok"),
            P(None, "tok"),
            P("mem", None),
            P("mem", None),
            P("mem", None),
        ),
        check_vma=False,
    )
```
